128 devices in a mesh: region: 16 (over x, y_lo, core), patch: 8 (over z, y_hi).
Axes of the slice: x: 4, y: 4 (y_hi: 2, y_lo: 2; y = y_hi * 2 + y_lo), z: 4, core: 2. Of those that a mesh axis runs over, the one named last changes fastest.
Arguments:
- coarse_state: float32 [12, 256, 256], P(None, ('region', 'patch')), may hold values from -6 to 6
- anchors: int32 [256, 2], P('region'), may hold values from 0 to 1920, as said below
- region_count: int32 [16], P('region'), may hold values from 8 to 16, as said below
- blend: int32 [256], P('region'), may hold values from 1 to 4
- w_in: bfloat16 [3, 3, 16, 128], replicated, may hold values from -0.5 to 0.5
- b_in: float32 [128], replicated, may hold values from -4 to 4
- gamma: float32 [128], replicated, may hold values from 0.1 to 1.9
- beta: float32 [128], replicated, may hold values from -3 to 3
- w_mid: bfloat16 [3, 3, 128, 128], replicated, may hold values from -0.1875 to 0.1875
- w_out: bfloat16 [3, 3, 128, 12], replicated, may hold values from -0.1875 to 0.1875
Outputs:
- downscaled: float32 [12, 2048, 2048], P(None, 'region', 'patch')
The draws below stay inside these ranges and needn't reach their ends.
Inputs may be any that keep to these rules, and one draw needn't show every extreme that they name: `anchors`: rows r * 16 to r * 16 + 15 belong to region r. The first entry is the patch's top row: at least r * 128 and at most r * 128 + 128 / 2; the second is its left column; every patch of 128 x 128 cells lies inside the grid. The first region_count[r] slots of region r are live; some region has all 16 slots live.
All inputs are finite; a program needn't handle non-finite values.
Results may differ from the reference program's by a relative error of at most 0.006.
Values may be sent and summed in bfloat16 or wider, within the bound.
A program may use at most 192 MiB of HBM per device.

```python
import math
import jax
import jax.numpy as jnp
from jax import lax

VARS = 12
CHAN = 128
GROUPS = 32
PS = 128
F = 8
TH = 128
SLOTS_REG = 16
PATCHES = 256
H = 2048
W = 2048
CH = 256
CW = 256
CIN = 16
N_REGION = 16


def draw_anchors(key, part):
    key = jax.random.fold_in(key, 11)
    key_rows, key_cols = jax.random.split(key)
    slot_ident = jnp.arange(PATCHES)
    region = slot_ident // SLOTS_REG
    offset = jax.random.randint(key_rows, (PATCHES,), 0, TH // 2 + 1)
    top_rows = jnp.minimum(region * TH + offset, H - PS)
    left_cols = jax.random.randint(key_cols, (PATCHES,), 0, W - PS + 1)
    left_cols = left_cols.at[0].set(0).at[1].set(W - PS)
    return jnp.stack([top_rows, left_cols], axis=1).astype(jnp.int32)


def draw_region_count(key, part):
    key = jax.random.fold_in(key, 23)
    key_counts, key_full = jax.random.split(key)
    counts = jax.random.randint(key_counts, (N_REGION,), SLOTS_REG // 2, SLOTS_REG + 1)
    full_region = jax.random.randint(key_full, (), 0, N_REGION)
    counts = jnp.where(jnp.arange(N_REGION) == full_region, SLOTS_REG, counts)
    return counts.astype(jnp.int32)


def set_ends(array, own_key, low, top_value):
    longest = array.shape.index(max(array.shape))
    spots = []
    for shift in (0, 1):
        where = [jax.random.randint(jax.random.fold_in(own_key, axis), (), 0, length) for axis, length in enumerate(array.shape)]
        where[longest] = (where[longest] + shift) % array.shape[longest]
        spots.append(tuple(where))
    return array.at[spots[0]].set(low).at[spots[1]].set(top_value)


def block_scale(own_key, dims, cuts, low, high):
    loudness, own = 1.0, jax.random.fold_in(own_key, 6)
    for dim, parts in cuts:
        steps = jnp.exp(jax.random.uniform(jax.random.fold_in(own, dim), (parts,), jnp.float32, low / len(cuts), high / len(cuts)))
        loudness = loudness * jnp.repeat(steps, dims[dim] // parts).reshape([-1 if axis == dim else 1 for axis in range(len(dims))])
    return loudness


def noise(key, extent, width, reach, pieces=(), held_as=jnp.bfloat16):
    values = width * jax.random.normal(key, extent, jnp.float32)
    if pieces:
        values = values * block_scale(key, extent, pieces, -0.22, 0.18)
    return jnp.clip(values, -reach, reach).astype(held_as)


def setup_inputs(seed: int = 0) -> dict:
    seeds = jax.random.split(jax.random.key(seed), 11)
    coarse_state = noise(seeds[0], (VARS, CH, CW), 1.0, 6.0, ((1, 128),), jnp.float32)
    anchors = draw_anchors(jax.random.fold_in(seeds[10], 71), 0)
    region_count = draw_region_count(jax.random.fold_in(seeds[10], 71), 0)
    blend = set_ends(jax.random.randint(seeds[3], (PATCHES,), 1, 5), jax.random.fold_in(seeds[3], 1), 1, 4).astype(jnp.int32)
    w_in = noise(seeds[4], (3, 3, CIN, CHAN), (9 * CIN) ** -0.5, 0.5)
    b_in = noise(seeds[5], (CHAN,), 1.0, 4.0, (), jnp.float32)
    gamma = jnp.clip(1.0 + 0.18 * jax.random.normal(seeds[6], (CHAN,), jnp.float32), 0.1, 1.9)
    beta = noise(seeds[7], (CHAN,), 0.5, 3.0, (), jnp.float32)
    w_mid = noise(seeds[8], (3, 3, CHAN, CHAN), (9 * CHAN) ** -0.5, 0.1875)
    w_out = noise(seeds[9], (3, 3, CHAN, VARS), (9 * CHAN) ** -0.5, 0.1875)
    return {"coarse_state": coarse_state, "anchors": anchors, "region_count": region_count, "blend": blend, "w_in": w_in, "b_in": b_in, "gamma": gamma, "beta": beta, "w_mid": w_mid, "w_out": w_out}


def hat_table(start_cell, length, coarse_limit, start_coarse, table_width):
    fine_index = start_cell.astype(jnp.float32) + jnp.arange(length).astype(jnp.float32)
    location = jnp.clip((fine_index + 0.5) / F - 0.5, 0.0, coarse_limit - 1.0)
    coarse_index = start_coarse.astype(jnp.float32) + jnp.arange(table_width).astype(jnp.float32)
    return jnp.maximum(0.0, 1.0 - jnp.abs(location[:, None] - coarse_index[None, :]))

def conv_same(inputs, kernel):
    return lax.conv_general_dilated(inputs, kernel, (1, 1), 'SAME', dimension_numbers=('NHWC', 'HWIO', 'NHWC'), preferred_element_type=jnp.float32)

def group_act(first_act, gamma, beta):
    channels = first_act.shape[3]
    values = first_act.astype(jnp.float32).reshape(first_act.shape[1] * first_act.shape[2], GROUPS, channels // GROUPS)
    group_mean = lax.optimization_barrier(jnp.mean(values, axis=(0, 2), keepdims=True))
    centred = values - group_mean
    group_var = lax.optimization_barrier(jnp.mean(centred * centred, axis=(0, 2), keepdims=True))
    normed = (centred / jnp.sqrt(group_var + 1e-05)).reshape(first_act.shape)
    return jax.nn.silu(normed * gamma + beta).astype(jnp.bfloat16)

def unet_patch(coarse_rows, row_base, coarse_limit, height, breadth, anchor_y, anchor_x, weights):
    w_in, b_in, gamma, beta, w_mid, w_out = weights
    window = PS // F + 3
    column_limit = coarse_rows.shape[2]
    row_start = jnp.clip(anchor_y // F - 1, 0, coarse_limit - window).astype(jnp.int32)
    col_start = jnp.clip(anchor_x // F - 1, 0, column_limit - window).astype(jnp.int32)
    local_row = (row_start - row_base).astype(jnp.int32)
    patch_coarse = lax.dynamic_slice(coarse_rows, (jnp.int32(0), local_row, col_start), (coarse_rows.shape[0], window, window))
    table_y = hat_table(anchor_y, PS, coarse_limit, row_start, window)
    table_x = hat_table(anchor_x, PS, column_limit, col_start, window)
    half_done = jnp.einsum('ic,vcd->ivd', table_y, patch_coarse, precision=lax.Precision.HIGHEST)
    interp = jnp.einsum('ivd,jd->ijv', half_done, table_x, precision=lax.Precision.HIGHEST)
    angle_y = (anchor_y.astype(jnp.float32) + jnp.arange(PS).astype(jnp.float32)) * (2.0 * math.pi / height)
    angle_x = (anchor_x.astype(jnp.float32) + jnp.arange(PS).astype(jnp.float32)) * (2.0 * math.pi / breadth)
    patch_shape = (PS, PS)
    position = jnp.stack([jnp.broadcast_to(jnp.sin(angle_y)[:, None], patch_shape), jnp.broadcast_to(jnp.cos(angle_y)[:, None], patch_shape), jnp.broadcast_to(jnp.sin(angle_x)[None, :], patch_shape), jnp.broadcast_to(jnp.cos(angle_x)[None, :], patch_shape)], axis=2)
    inputs = jnp.concatenate([interp, position], axis=2).astype(jnp.bfloat16)[None]
    first_act = (conv_same(inputs, w_in) + b_in).astype(jnp.bfloat16)
    norm_act = group_act(first_act, gamma, beta)
    second = (first_act.astype(jnp.float32) + conv_same(norm_act, w_mid)).astype(jnp.bfloat16)
    result = (conv_same(second, w_out)[0] + interp).astype(jnp.bfloat16)
    return jnp.transpose(result, (2, 0, 1))

def reference(coarse_state, anchors, region_count, blend, w_in, b_in, gamma, beta, w_mid, w_out):
    weights = (w_in, b_in, gamma, beta, w_mid, w_out)

    def patch_step(sums_so_far, slot_ident):
        numerator, cover = sums_so_far
        region = slot_ident // SLOTS_REG
        is_live = slot_ident % SLOTS_REG < region_count[region]
        anchor_y = anchors[slot_ident, 0]
        anchor_x = anchors[slot_ident, 1]
        produced = lax.cond(is_live, lambda: unet_patch(coarse_state, jnp.int32(0), CH, H, W, anchor_y, anchor_x, weights), lambda: jnp.zeros((VARS, PS, PS), jnp.bfloat16))
        blend_scale = jnp.where(is_live, blend[slot_ident], 0).astype(jnp.float32)
        current = lax.dynamic_slice(numerator, (jnp.int32(0), anchor_y, anchor_x), (VARS, PS, PS))
        numerator = lax.dynamic_update_slice(numerator, current + blend_scale * produced.astype(jnp.float32), (jnp.int32(0), anchor_y, anchor_x))
        covered = lax.dynamic_slice(cover, (anchor_y, anchor_x), (PS, PS))
        cover = lax.dynamic_update_slice(cover, covered + blend_scale, (anchor_y, anchor_x))
        return ((numerator, cover), None)
    start_sums = (jnp.zeros((VARS, H, W), jnp.float32), jnp.zeros((H, W), jnp.float32))
    (numerator, cover), _ = lax.scan(patch_step, start_sums, jnp.arange(PATCHES).astype(jnp.int32))
    return numerator / jnp.maximum(cover, 1.0)[None]
```

```python
import math

import jax
import jax.numpy as jnp
from jax import lax
from jax.experimental import pallas as pl
from jax.experimental.pallas import tpu as pltpu
from jax.sharding import PartitionSpec as P

VARS = 12
CHAN = 128
PS = 128
F = 8
TH = 128
TW = 256
BF = jnp.bfloat16
F32 = jnp.float32
NT, NS = 8, 16
XR = (NT + 2) * NS
KC = 512
GROUP = PS * VARS


def dot(a, b):
    return jnp.dot(a, b, preferred_element_type=F32)


def dot_nt(a, b):
    return lax.dot_general(a, b, (((1,), (1,)), ((), ())), preferred_element_type=F32)


def split(x):
    hi = x.astype(BF)
    return hi, (x - hi.astype(F32)).astype(BF)


def row_halo(x):
    rows = x.shape[0]
    s = lax.broadcasted_iota(jnp.int32, (rows, NS, CHAN), 1)
    before = jnp.where(s == 0, 0.0, pltpu.roll(x[:, NT - 1], 1, 1))
    after = jnp.where(s == NS - 1, 0.0, pltpu.roll(x[:, 0], NS - 1, 1))
    return before, after


def interp_stage(hx, xpos, coarse, loc_ref, extra_ref, slot, xh, xl):
    chi, clo = split(coarse)
    t1 = dot_nt(hx, chi) + dot_nt(hx, clo) + xpos
    hi, lo = split(t1)
    lhs = jnp.concatenate([hi, lo], axis=0)
    v_at = lax.broadcasted_iota(jnp.int32, (16, 256), 0)
    ch_at = lax.broadcasted_iota(jnp.int32, (16, 256), 1) % 16
    diag = jnp.where((v_at == ch_at) & (v_at < VARS), 1.0, 0.0)

    def step(g, _):
        loc = jnp.broadcast_to(loc_ref[slot, g], (16, 256))
        blocks = []
        for c in range(28):
            hat = jnp.maximum(0.0, 1.0 - jnp.abs(loc - float(c))) * diag
            if c == 0:
                hat = hat + extra_ref[slot, g]
            blocks.append(hat.astype(BF))
        blocks.append(jnp.zeros((64, 256), BF))
        res = dot(lhs, jnp.concatenate(blocks, axis=0))
        x = res[:XR] + res[XR:]
        for h in range(2):
            xa, xb = split(x[:, h * 128 : h * 128 + 128])
            xh[2 * g + h] = xa.reshape(NT + 2, NS, 128)
            xl[2 * g + h] = xb.reshape(NT + 2, NS, 128)
        return 0

    lax.fori_loop(0, 16, step, 0)


def first_stage(win, b_in, xh, fa, shift, sums):
    bias = b_in[...]
    sums[...] = jnp.zeros_like(sums)

    def step(it, _):
        lhs = jnp.concatenate(
            [xh[pl.ds(4 * it, 4), dx : dx + 8].reshape(512, 128) for dx in range(3)], axis=1
        )
        acc = dot(lhs, win[...])
        parts = []
        for r in range(4):
            x = (acc[:, r * 128 : r * 128 + 128] + bias).astype(BF)
            for b in range(4):
                fa[8 * it + 2 * b + r // 2, r % 2] = x[b * 128 : b * 128 + 128]
            parts.append(x.astype(F32))

        @pl.when(it == 0)
        def _():
            shift[...] = jnp.mean(parts[0], axis=0, keepdims=True)

        base = shift[...]
        one = jnp.zeros((8, CHAN), F32)
        two = jnp.zeros((8, CHAN), F32)
        for x in parts:
            d = (x - base).reshape(64, 8, CHAN)
            one = one + jnp.sum(d, axis=0)
            two = two + jnp.sum(d * d, axis=0)
        sums[0] += one
        sums[1] += two
        return 0

    lax.fori_loop(0, 8, step, 0)


def group_mean(x):
    lane = lax.broadcasted_iota(jnp.int32, x.shape, 1)
    total = x
    for k in (1, 2):
        low = (lane // k) % 2 == 0
        total = total + jnp.where(low, pltpu.roll(total, CHAN - k, 1), pltpu.roll(total, k, 1))
    return total * 0.25


def scale_shift(sums, shift, gamma, beta):
    n = float(PS * PS)
    one = jnp.broadcast_to(jnp.sum(sums[0], axis=0, keepdims=True), (8, CHAN)) / n
    two = jnp.broadcast_to(jnp.sum(sums[1], axis=0, keepdims=True), (8, CHAN)) / n
    own_var = jnp.maximum(two - one * one, 0.0)
    mean = one + shift[...]
    g_mean = group_mean(mean)
    off = mean - g_mean
    g_var = group_mean(own_var + off * off)
    scale = gamma[...] / jnp.sqrt(g_var + 1e-05)
    return scale[0:1], (beta[...] - g_mean * scale)[0:1]


def norm_stage(scale, offset, fa, nb):
    half_scale = 0.5 * scale
    half_offset = 0.5 * offset

    def step(p, _):
        x = fa[p].astype(F32).reshape(2, NT, NS, CHAN)
        h = x * half_scale + half_offset
        y = h + h * jnp.tanh(h)
        before, after = row_halo(y)
        for r in range(2):
            at, k = (p, 1) if r == 0 else (p + 1, 0)
            nb[at, k, 1 : NT + 1] = y[r].astype(BF)
            nb[at, k, 0] = before[r].astype(BF)
            nb[at, k, NT + 1] = after[r].astype(BF)
        return 0

    lax.fori_loop(0, 64, step, 0, unroll=2)


def mid_stage(wmid, nb, fa, sb):
    def step(it, _):
        p0 = 4 * it
        lhs = []
        for k in range(4):
            for dx in range(3):
                lhs.append(nb[pl.ds(p0 + k // 2, 4), k % 2, dx : dx + 8].reshape(512, CHAN))
        acc = dot(jnp.concatenate(lhs, axis=1), wmid[...])
        for r in range(2):
            x = acc[:, r * 128 : r * 128 + 128] + fa[pl.ds(p0, 4), r].astype(F32).reshape(512, CHAN)
            x = x.reshape(4, NT, NS, CHAN)
            before, after = row_halo(x)
            for b in range(4):
                at = 2 * b + r + 1
                q, k = 2 * it + at // 4, at % 4
                sb[q, k, 1 : NT + 1] = x[b].astype(BF)
                sb[q, k, 0] = before[b].astype(BF)
                sb[q, k, NT + 1] = after[b].astype(BF)
        return 0

    lax.fori_loop(0, 16, step, 0)


def out_step(it, wout, sb, xh, xl):
    g0 = 4 * it
    lhs = [sb[pl.ds(g0 + k // 4, 4), k % 4].reshape(4 * XR, CHAN) for k in range(6)]
    lhs.append(xh[pl.ds(g0, 4)].reshape(4 * XR, CHAN))
    lhs.append(xl[pl.ds(g0, 4)].reshape(4 * XR, CHAN))
    acc = dot(jnp.concatenate(lhs, axis=1), wout[...])
    y0 = acc[:, :128].reshape(4, NT + 2, NS, 128)
    y1 = acc[:, 128:].reshape(4, NT + 2, NS, 128)
    centre = pltpu.roll(y0[:, 1 : NT + 1].reshape(512, 128), 64, 1).reshape(4, NT, NS, 128)
    res = y0[:, 0:NT] + centre + y1[:, 2 : NT + 2]
    res = res.reshape(4, 128, 128)
    lane = lax.broadcasted_iota(jnp.int32, (128, 128), 1)
    parts = []
    for h in range(2):
        both = jnp.where(lane < 48, res[2 * h], pltpu.roll(res[2 * h + 1], 48, 1))
        parts.append(jnp.transpose(both)[:96])
    return jnp.concatenate(parts, axis=0).astype(BF)


def patch_kernel(
    hx, xpos, loc, extra, coarse, win, b_in, gamma, beta, wmid, wout, out, xh, xl, fa, nb, sb, shift, sums
):
    zero = jnp.zeros((NT + 2, NS, CHAN), BF)
    nb[0, 0] = zero
    nb[64, 1] = zero
    sb[0, 0] = zero
    sb[32, 1] = zero

    def one_slot(slot, _):
        interp_stage(hx[slot], xpos[slot], coarse[...], loc, extra, slot, xh, xl)
        first_stage(win, b_in, xh, fa, shift, sums)
        scale, offset = scale_shift(sums, shift, gamma, beta)
        norm_stage(scale, offset, fa, nb)
        mid_stage(wmid, nb, fa, sb)

        def out_loop(it, _):
            at = pl.multiple_of(slot * GROUP + it * 192, 192)
            out[pl.ds(at, 192)] = out_step(it, wout, sb, xh, xl)
            return 0

        lax.fori_loop(0, 8, out_loop, 0)
        return 0

    lax.fori_loop(0, 2, one_slot, 0)


VM = pl.BlockSpec(memory_space=pltpu.VMEM)
SM = pl.BlockSpec(memory_space=pltpu.SMEM)


def run_patches(tables, coarse, weights):
    return pl.pallas_call(
        patch_kernel,
        out_shape=jax.ShapeDtypeStruct((2 * GROUP, 128), BF),
        in_specs=[VM] * 11,
        out_specs=VM,
        scratch_shapes=[
            pltpu.VMEM((32, NT + 2, NS, 128), BF),
            pltpu.VMEM((32, NT + 2, NS, 128), BF),
            pltpu.VMEM((64, 2, 128, CHAN), BF),
            pltpu.VMEM((65, 2, NT + 2, NS, CHAN), BF),
            pltpu.VMEM((33, 4, NT + 2, NS, CHAN), BF),
            pltpu.VMEM((1, CHAN), F32),
            pltpu.VMEM((2, 8, CHAN), F32),
        ],
        compiler_params=pltpu.CompilerParams(vmem_limit_bytes=56 * 2**20),
        name="patch_net",
    )(*tables, coarse, *weights)


def patch_tables(anchor_y, anchor_x, c0, height, breadth, limit_y, limit_x):
    rows = jnp.arange(XR)
    j = (rows % NS) * NT + rows // NS - 1
    good_x = (j >= 0) & (j < PS)
    x = (anchor_x[:, None] + j).astype(F32)
    at = jnp.clip((x + 0.5) / F - 0.5, 0.0, limit_x - 1.0)
    d = jnp.arange(limit_x).astype(F32)
    hx = jnp.maximum(0.0, 1.0 - jnp.abs(at[:, :, None] - d))
    hx = jnp.where(good_x[None, :, None], hx, 0.0).astype(BF)
    angle_x = x * (2.0 * math.pi / breadth)
    col = jnp.arange(KC)
    xpos = jnp.where(
        col == 12,
        1.0,
        jnp.where(
            col == 13,
            jnp.sin(angle_x)[:, :, None],
            jnp.where(col == 14, jnp.cos(angle_x)[:, :, None], 0.0),
        ),
    )
    xpos = jnp.where(good_x[None, :, None], xpos, 0.0).astype(F32)
    lane = jnp.arange(4096)
    b, k, ch = lane // 128, (lane % 128) // 16, lane % 16
    i = 4 * b - 1 + k
    good_y = (i >= 0) & (i < PS) & (k < 6)
    y = (anchor_y[:, None] + i).astype(F32)
    loc = jnp.clip((y + 0.5) / F - 0.5, 0.0, limit_y - 1.0) - c0.astype(F32)
    loc = jnp.where(good_y, loc, -1000.0).reshape(2, 16, 1, 256)
    angle_y = y * (2.0 * math.pi / height)
    ypos = jnp.where(ch == 12, jnp.sin(angle_y), jnp.where(ch == 13, jnp.cos(angle_y), 0.0))
    v = jnp.arange(16)[:, None]
    extra = jnp.where(v == 12, ypos[:, None], 0.0)
    extra = extra + jnp.where((v == 13) & (ch == 14) | (v == 14) & (ch == 15), 1.0, 0.0)
    extra = jnp.where(good_y, extra, 0.0).astype(F32)
    extra = extra.reshape(2, 16, 16, 256).transpose(0, 2, 1, 3)
    return hx, xpos, loc, extra


def packed_weights(w_in, b_in, gamma, beta, w_mid, w_out):
    w = w_in.transpose(1, 0, 2, 3)
    win = jnp.stack([jnp.pad(w, ((0, 0), (r, 5 - r), (0, 0), (0, 0))) for r in range(4)], axis=3)
    win = win.reshape(3 * 128, 4 * CHAN)
    wmid = jnp.stack([jnp.pad(w_mid, ((r, 1 - r), (0, 0), (0, 0), (0, 0))) for r in range(2)], axis=3)
    wmid = wmid.reshape(4 * 3 * CHAN, 2 * CHAN)
    wo = w_out.transpose(0, 2, 1, 3)
    wout = jnp.stack([jnp.pad(wo, ((r, 3 - r), (0, 0), (0, 0), (0, 0))) for r in range(4)], axis=3)
    wout = wout.reshape(6 * CHAN, 3, 48)
    wout = jnp.pad(wout, ((0, 0), (0, 1), (0, 16))).reshape(6 * CHAN, 256)
    row = jnp.arange(128)[:, None]
    colm = jnp.arange(256)[None]
    keep = (colm >= 64) & (colm < 112) & (row % 16 == (colm - 64) % 12) & (row // 16 == (colm - 64) // 12 + 1)
    ident = keep.astype(BF)
    wout = jnp.concatenate([wout, ident, ident], axis=0)
    return (
        win,
        b_in.reshape(1, CHAN),
        gamma.reshape(1, CHAN),
        beta.reshape(1, CHAN),
        wmid,
        wout,
    )


ACC_ROWS = (3 * TH // 2) * VARS


def place_kernel(info, gathered, num, over, acc, buf, sem):
    acc[...] = jnp.zeros_like(acc)
    lane = lax.broadcasted_iota(jnp.int32, (128, TW), 0)
    x_at = lax.broadcasted_iota(jnp.int32, (128, TW), 1)
    j_at = (lane % NS) * NT + lane // NS

    def fetch(s, k):
        return pltpu.make_async_copy(gathered.at[pl.ds(s * GROUP, GROUP)], buf.at[k], sem.at[k])

    fetch(0, 0).start()

    def slot(s, _):
        k = s % 2

        @pl.when(s < 15)
        def _():
            fetch(s + 1, 1 - k).start()

        fetch(s, k).wait()
        dy, dx, weight = info[0, s], info[1, s], info[2, s]

        @pl.when((weight > 0) & (dx > -PS) & (dx < TW))
        def _():
            onehot = jnp.where(x_at - j_at == dx, weight, 0).astype(F32).astype(BF)
            par = dy % 2
            base = ((dy - par) // 2) * 24

            def part(n, _):
                y = dot(buf[k, pl.ds(pl.multiple_of(n * 384, 384), 384)], onehot)
                at = pl.multiple_of(base + n * 384, 8)
                for h in range(2):
                    acc[par, h, pl.ds(at, 384)] += y[:, h * 128 : h * 128 + 128]
                return 0

            lax.fori_loop(0, 4, part, 0)

        return 0

    lax.fori_loop(0, 16, slot, 0)
    for v in range(VARS):
        for h in range(2):
            cols = slice(h * 128, h * 128 + 128)
            num[v, :, cols] = acc[0, h, pl.ds(v, TH, VARS)]
            num[v, 1:, cols] += acc[1, h, pl.ds(v, TH - 1, VARS)]
            low = acc[0, h, pl.ds(TH * VARS + v, TH // 2, VARS)]
            low = low + acc[1, h, pl.ds((TH - 1) * VARS + v, TH // 2, VARS)]
            over[v, :, cols] = low.astype(BF)


def run_place(info, gathered):
    return pl.pallas_call(
        place_kernel,
        out_shape=(
            jax.ShapeDtypeStruct((VARS, TH, TW), F32),
            jax.ShapeDtypeStruct((VARS, TH // 2, TW), BF),
        ),
        in_specs=[SM, pl.BlockSpec(memory_space=pl.ANY)],
        out_specs=(VM, VM),
        scratch_shapes=[
            pltpu.VMEM((2, 2, ACC_ROWS, 128), F32),
            pltpu.VMEM((2, GROUP, 128), BF),
            pltpu.SemaphoreType.DMA((2,)),
        ],
        compiler_params=pltpu.CompilerParams(vmem_limit_bytes=40 * 2**20),
        name="place",
    )(info, gathered)


def covered(dy, dx, weight, rows):
    r = jnp.arange(rows)
    c = jnp.arange(TW)
    in_r = (r >= dy[:, None]) & (r < dy[:, None] + PS)
    in_c = (c >= dx[:, None]) & (c < dx[:, None] + PS)
    left = jnp.where(in_r, weight[:, None], 0).astype(F32)
    return lax.dot_general(left, in_c.astype(F32), (((0,), (0,)), ((), ())), preferred_element_type=F32)


def per_device(coarse_state, anchors, region_count, blend, w_in, b_in, gamma, beta, w_mid, w_out):
    n_region = lax.axis_size("region")
    n_patch = lax.axis_size("patch")
    region = lax.axis_index("region")
    column = lax.axis_index("patch")
    limit = coarse_state.shape[1] * n_region * n_patch
    band = limit // n_region
    up = [(i, i + 1) for i in range(n_region - 1)]
    down = [(j, i) for i, j in up]

    slots = anchors.shape[0]
    weight = jnp.where(jnp.arange(slots) < region_count[0], blend, 0).astype(jnp.int32)
    dy = anchors[:, 0] - region * TH
    dx = anchors[:, 1] - column * TW
    info = jnp.stack([dy, dx, weight])
    above = lax.ppermute(jnp.stack([dy - TH, anchors[:, 1], weight]), "region", up)

    within = lax.all_gather(coarse_state.transpose(1, 0, 2), "patch", axis=0, tiled=True)
    before = lax.ppermute(within[band - 2 :], "region", up)
    after = lax.ppermute(within[:10], "region", down)
    coarse = jnp.concatenate([before, within, after], axis=0)
    coarse = jnp.pad(coarse, ((0, 4), (0, 4), (0, 0))).reshape(KC, limit)

    mine = lax.dynamic_slice(anchors, (column * 2, jnp.int32(0)), (2, 2))
    tables = patch_tables(
        mine[:, 0], mine[:, 1], region * band - 2, TH * n_region, TW * n_patch, limit, limit
    )
    weights = packed_weights(w_in, b_in, gamma, beta, w_mid, w_out)
    produced = run_patches(tables, coarse, weights)
    gathered = lax.all_gather(produced, "patch", axis=0, tiled=True)
    num, over = run_place(info, gathered)
    cover = covered(dy, dx, weight, TH) + covered(above[0], above[1] - column * TW, above[2], TH)
    low = lax.ppermute(over, "region", up).astype(F32)
    num = num + jnp.pad(low, ((0, 0), (0, TH // 2), (0, 0)))
    return num / jnp.maximum(cover, 1.0)


def solution(mesh):
    return jax.shard_map(
        per_device,
        mesh=mesh,
        in_specs=(
            P(None, ("region", "patch"), None),
            P("region", None),
            P("region"),
            P("region"),
            P(),
            P(),
            P(),
            P(),
            P(),
            P(),
        ),
        out_specs=P(None, "region", "patch"),
        check_vma=False,
    )
```

```python
import math

import jax
import jax.numpy as jnp
from jax import lax
from jax.experimental import pallas as pl
from jax.experimental.pallas import tpu as pltpu
from jax.sharding import PartitionSpec as P

VARS = 12
CHAN = 128
PS = 128
F = 8
TH = 128
TW = 256
BF = jnp.bfloat16
F32 = jnp.float32
NT, NS = 8, 16
XR = (NT + 2) * NS
KC = 512
GROUP = PS * VARS
MESH = pl.DeviceIdType.MESH


def dot(a, b):
    return jnp.dot(a, b, preferred_element_type=F32)


def dot_nt(a, b):
    return lax.dot_general(a, b, (((1,), (1,)), ((), ())), preferred_element_type=F32)


def split(x):
    hi = x.astype(BF)
    return hi, (x - hi.astype(F32)).astype(BF)


def row_halo(x):
    rows = x.shape[0]
    s = lax.broadcasted_iota(jnp.int32, (rows, NS, CHAN), 1)
    before = jnp.where(s == 0, 0.0, pltpu.roll(x[:, NT - 1], 1, 1))
    after = jnp.where(s == NS - 1, 0.0, pltpu.roll(x[:, 0], NS - 1, 1))
    return before, after


def interp_stage(hx, xpos, coarse, loc_ref, extra_ref, slot, xh, xl):
    chi, clo = split(coarse)
    t1 = dot_nt(hx, chi) + dot_nt(hx, clo) + xpos
    hi, lo = split(t1)
    lhs = jnp.concatenate([hi, lo], axis=0)
    v_at = lax.broadcasted_iota(jnp.int32, (16, 256), 0)
    ch_at = lax.broadcasted_iota(jnp.int32, (16, 256), 1) % 16
    diag = jnp.where((v_at == ch_at) & (v_at < VARS), 1.0, 0.0)

    def step(g, _):
        loc = jnp.broadcast_to(loc_ref[slot, g], (16, 256))
        blocks = []
        for c in range(28):
            hat = jnp.maximum(0.0, 1.0 - jnp.abs(loc - float(c))) * diag
            if c == 0:
                hat = hat + extra_ref[slot, g]
            blocks.append(hat.astype(BF))
        blocks.append(jnp.zeros((64, 256), BF))
        res = dot(lhs, jnp.concatenate(blocks, axis=0))
        x = res[:XR] + res[XR:]
        for h in range(2):
            xa, xb = split(x[:, h * 128 : h * 128 + 128])
            xh[2 * g + h] = xa.reshape(NT + 2, NS, 128)
            xl[2 * g + h] = xb.reshape(NT + 2, NS, 128)
        return 0

    lax.fori_loop(0, 16, step, 0)


def first_stage(win, b_in, xh, fa, shift, sums, also):
    bias = b_in[...]
    sums[...] = jnp.zeros_like(sums)

    def step(it, _):
        lhs = jnp.concatenate(
            [xh[pl.ds(4 * it, 4), dx : dx + 8].reshape(512, 128) for dx in range(3)], axis=1
        )
        acc = dot(lhs, win[...])
        parts = []
        for r in range(4):
            x = (acc[:, r * 128 : r * 128 + 128] + bias).astype(BF)
            for b in range(4):
                fa[8 * it + 2 * b + r // 2, r % 2] = x[b * 128 : b * 128 + 128]
            parts.append(x.astype(F32))

        @pl.when(it == 0)
        def _():
            shift[...] = jnp.mean(parts[0], axis=0, keepdims=True)

        base = shift[...]
        one = jnp.zeros((8, CHAN), F32)
        two = jnp.zeros((8, CHAN), F32)
        for x in parts:
            d = (x - base).reshape(64, 8, CHAN)
            one = one + jnp.sum(d, axis=0)
            two = two + jnp.sum(d * d, axis=0)
        sums[0] += one
        sums[1] += two
        also(it)
        return 0

    lax.fori_loop(0, 8, step, 0)


def group_mean(x):
    lane = lax.broadcasted_iota(jnp.int32, x.shape, 1)
    total = x
    for k in (1, 2):
        low = (lane // k) % 2 == 0
        total = total + jnp.where(low, pltpu.roll(total, CHAN - k, 1), pltpu.roll(total, k, 1))
    return total * 0.25


def scale_shift(sums, shift, gamma, beta):
    n = float(PS * PS)
    one = jnp.broadcast_to(jnp.sum(sums[0], axis=0, keepdims=True), (8, CHAN)) / n
    two = jnp.broadcast_to(jnp.sum(sums[1], axis=0, keepdims=True), (8, CHAN)) / n
    own_var = jnp.maximum(two - one * one, 0.0)
    mean = one + shift[...]
    g_mean = group_mean(mean)
    off = mean - g_mean
    g_var = group_mean(own_var + off * off)
    scale = gamma[...] / jnp.sqrt(g_var + 1e-05)
    return scale[0:1], (beta[...] - g_mean * scale)[0:1]


def norm_stage(scale, offset, fa, nb):
    half_scale = 0.5 * scale
    half_offset = 0.5 * offset

    def step(p, _):
        x = fa[p].astype(F32).reshape(2, NT, NS, CHAN)
        h = x * half_scale + half_offset
        y = h + h * jnp.tanh(h)
        before, after = row_halo(y)
        for r in range(2):
            at, k = (p, 1) if r == 0 else (p + 1, 0)
            nb[at, k, 1 : NT + 1] = y[r].astype(BF)
            nb[at, k, 0] = before[r].astype(BF)
            nb[at, k, NT + 1] = after[r].astype(BF)
        return 0

    lax.fori_loop(0, 64, step, 0, unroll=2)


def mid_step(it, wmid, nb, fa, sb):
    p0 = 4 * it
    lhs = []
    for k in range(4):
        for dx in range(3):
            lhs.append(nb[pl.ds(p0 + k // 2, 4), k % 2, dx : dx + 8].reshape(512, CHAN))
    acc = dot(jnp.concatenate(lhs, axis=1), wmid[...])
    for r in range(2):
        x = acc[:, r * 128 : r * 128 + 128] + fa[pl.ds(p0, 4), r].astype(F32).reshape(512, CHAN)
        x = x.reshape(4, NT, NS, CHAN)
        before, after = row_halo(x)
        for b in range(4):
            at = 2 * b + r + 1
            q, k = 2 * it + at // 4, at % 4
            sb[q, k, 1 : NT + 1] = x[b].astype(BF)
            sb[q, k, 0] = before[b].astype(BF)
            sb[q, k, NT + 1] = after[b].astype(BF)


def out_step(it, wout, sb, xh, xl):
    g0 = 4 * it
    lhs = [sb[pl.ds(g0 + k // 4, 4), k % 4].reshape(4 * XR, CHAN) for k in range(6)]
    lhs.append(xh[pl.ds(g0, 4)].reshape(4 * XR, CHAN))
    lhs.append(xl[pl.ds(g0, 4)].reshape(4 * XR, CHAN))
    acc = dot(jnp.concatenate(lhs, axis=1), wout[...])
    y0 = acc[:, :128].reshape(4, NT + 2, NS, 128)
    y1 = acc[:, 128:].reshape(4, NT + 2, NS, 128)
    centre = pltpu.roll(y0[:, 1 : NT + 1].reshape(512, 128), 64, 1).reshape(4, NT, NS, 128)
    res = y0[:, 0:NT] + centre + y1[:, 2 : NT + 2]
    res = res.reshape(4, 128, 128)
    lane = lax.broadcasted_iota(jnp.int32, (128, 128), 1)
    parts = []
    for h in range(2):
        both = jnp.where(lane < 48, res[2 * h], pltpu.roll(res[2 * h + 1], 48, 1))
        parts.append(jnp.transpose(both)[:96])
    return jnp.concatenate(parts, axis=0).astype(BF)


def exchange_kernel(shard, out, send_sem, recv_sem):
    r, p = lax.axis_index("region"), lax.axis_index("patch")
    n_r, n_p = lax.axis_size("region"), lax.axis_size("patch")
    has_up, has_down = r > 0, r < n_r - 1
    barrier = pltpu.get_barrier_semaphore()

    out[28:32] = jnp.zeros((4, 16, 256), F32)

    @pl.when(r == 0)
    def _():
        out[0:2] = jnp.zeros((2, 16, 256), F32)

    @pl.when(r == n_r - 1)
    def _():
        out[18:28] = jnp.zeros((10, 16, 256), F32)

    out[pl.ds(2 + 2 * p, 2)] = shard[...]

    def greet(to):
        pl.semaphore_signal(barrier, inc=1, device_id=to, device_id_type=MESH)

    for d in range(1, n_p):
        greet((r, (p + d) % n_p))

    @pl.when(has_up)
    def _():
        greet((r - 1, n_p - 1))

    @pl.when(has_down)
    def _():
        for k in range(5):
            greet((r + 1, k))

    feeds_down = (p == n_p - 1) & has_down
    feeds_up = (p < 5) & has_up
    count = n_p - 1 + jnp.where(feeds_down, n_p, 0) + jnp.where(feeds_up, n_p, 0)
    pl.semaphore_wait(barrier, count)

    def copy(row, key, k, to):
        return pltpu.make_async_remote_copy(
            src_ref=shard,
            dst_ref=out.at[pl.ds(row, 2)],
            send_sem=send_sem.at[k],
            recv_sem=recv_sem.at[key],
            device_id=to,
            device_id_type=MESH,
        )

    def to_down(k):
        return copy(0, 0, 7 + k, (r + 1, k))

    def to_up(k):
        return copy(18 + 2 * p, 9 + p, 15 + k, (r - 1, k))

    def to_peer(d):
        return copy(2 + 2 * p, 1 + p, d - 1, (r, (p + d) % n_p))

    def each(act):
        @pl.when(feeds_down)
        def _():
            for k in range(n_p):
                act(to_down(k))

        @pl.when(feeds_up)
        def _():
            for k in range(n_p):
                act(to_up(k))

        for d in range(1, n_p):
            act(to_peer(d))

    each(lambda c: c.start())

    for d in range(1, n_p):
        q = (p + d) % n_p
        copy(2 + 2 * q, 1 + q, 0, (r, q)).wait_recv()

    @pl.when(has_up)
    def _():
        copy(0, 0, 0, (r - 1, 7)).wait_recv()

    @pl.when(has_down)
    def _():
        for k in range(5):
            copy(18 + 2 * k, 9 + k, 0, (r + 1, k)).wait_recv()

    each(lambda c: c.wait_send())


def run_exchange(shard):
    return pl.pallas_call(
        exchange_kernel,
        out_shape=jax.ShapeDtypeStruct((32, 16, 256), F32),
        in_specs=[VM],
        out_specs=VM,
        scratch_shapes=[pltpu.SemaphoreType.DMA((23,)), pltpu.SemaphoreType.DMA((14,))],
        compiler_params=pltpu.CompilerParams(collective_id=0, has_side_effects=True),
        name="coarse_rows",
    )(shard)


CHUNK = 16 * VARS
HALF = CHUNK // 2


class Sharer:
    def __init__(self, out, g, send_sem, recv_sem, tail_sem, own_sem):
        self.out, self.g = out, g
        self.send_sem, self.recv_sem = send_sem, recv_sem
        self.tail_sem, self.own_sem = tail_sem, own_sem
        p = lax.axis_index("patch")
        z, y = p // 2, p % 2
        self.me = p
        self.fore = ((z + 1) % 4) * 2 + y
        self.back = ((z + 3) % 4) * 2 + y
        self.pair = z * 2 + 1 - y
        self.fore_pair = ((z + 1) % 4) * 2 + 1 - y
        self.back_pair = ((z + 3) % 4) * 2 + 1 - y

    def at(self, owner, q, half=None):
        start = (owner * 16 + q) * CHUNK
        if half is None:
            return self.g.at[pl.ds(pl.multiple_of(start, CHUNK), CHUNK)]
        return self.g.at[pl.ds(pl.multiple_of(start + half * HALF, HALF), HALF)]

    def remote(self, src, dst, stream, sem, to):
        return pltpu.make_async_remote_copy(
            src_ref=src,
            dst_ref=dst,
            send_sem=self.send_sem.at[stream],
            recv_sem=sem,
            device_id={"patch": to},
            device_id_type=MESH,
        )

    def greet(self):
        barrier = pltpu.get_barrier_semaphore()
        for to in (self.fore, self.back, self.pair):
            pl.semaphore_signal(barrier, inc=1, device_id={"patch": to}, device_id_type=MESH)
        pl.semaphore_wait(barrier, 3)

    def arrived(self, owner, q, stream):
        there = self.at(owner, q)
        self.remote(there, there, stream, self.recv_sem.at[stream, q], self.fore).wait_recv()

    def own(self, q):
        src = self.out.at[pl.ds(pl.multiple_of(q * CHUNK, CHUNK), CHUNK)]
        dst = self.at(self.me, q)
        self.remote(src, dst, 2, self.recv_sem.at[2, q], self.pair).start()
        self.remote(src, dst, 0, self.recv_sem.at[0, q], self.fore).start()
        self.remote(src, dst, 1, self.recv_sem.at[1, q], self.back).start()
        pltpu.make_async_copy(src, dst, self.own_sem).start()

    def first(self, q):
        self.arrived(self.pair, q, 2)
        there = self.at(self.pair, q)
        self.remote(there, there, 3, self.recv_sem.at[3, q], self.fore).start()
        self.remote(there, there, 4, self.recv_sem.at[4, q], self.back).start()
        self.arrived(self.back, q, 0)
        there = self.at(self.back, q, 0)
        self.remote(there, there, 5, self.tail_sem.at[0], self.fore).start()
        self.arrived(self.fore, q, 1)
        there = self.at(self.fore, q, 1)
        self.remote(there, there, 6, self.tail_sem.at[1], self.back).start()

    def second(self, q):
        self.arrived(self.back_pair, q, 3)
        there = self.at(self.back_pair, q, 0)
        self.remote(there, there, 7, self.tail_sem.at[2], self.fore).start()
        self.arrived(self.fore_pair, q, 4)
        there = self.at(self.fore_pair, q, 1)
        self.remote(there, there, 8, self.tail_sem.at[3], self.back).start()

    def finish(self):
        whole = self.g.at[pl.ds(0, 2 * GROUP)]
        part = self.g.at[pl.ds(0, GROUP)]
        for k in range(4):
            self.remote(part, part, 5 + k, self.tail_sem.at[k], self.fore).wait()
        for k in range(5):
            self.remote(whole, whole, k, self.tail_sem.at[0], self.fore).wait_send()
        pltpu.make_async_copy(whole, whole, self.own_sem).wait()


def patch_kernel(
    hx, xpos, loc, extra, coarse, win, b_in, gamma, beta, wmid, wout, g,
    out, xh, xl, fa, nb, sb, shift, sums, send_sem, recv_sem, tail_sem, own_sem,
):
    share = Sharer(out, g, send_sem, recv_sem, tail_sem, own_sem)
    share.greet()
    zero = jnp.zeros((NT + 2, NS, CHAN), BF)
    nb[0, 0] = zero
    nb[64, 1] = zero
    sb[0, 0] = zero
    sb[32, 1] = zero

    def one_slot(slot, _):
        interp_stage(hx[slot], xpos[slot], coarse[...], loc, extra, slot, xh, xl)

        def forward(it):
            @pl.when(slot == 1)
            def _():
                share.first(it)

        first_stage(win, b_in, xh, fa, shift, sums, forward)
        scale, offset = scale_shift(sums, shift, gamma, beta)
        norm_stage(scale, offset, fa, nb)

        def out_chunk(it):
            q = slot * 8 + it
            at = pl.multiple_of(q * CHUNK, CHUNK)
            out[pl.ds(at, CHUNK)] = out_step(it, wout, sb, xh, xl)
            share.own(q)

        def rows(it, _):
            mid_step(2 * it, wmid, nb, fa, sb)
            mid_step(2 * it + 1, wmid, nb, fa, sb)

            @pl.when(it > 0)
            def _():
                out_chunk(it - 1)

            @pl.when(slot == 1)
            def _():
                share.second(it)

                @pl.when(it >= 3)
                def _():
                    share.first(8 + it - 3)

                @pl.when(it >= 5)
                def _():
                    share.second(8 + it - 5)

            return 0

        lax.fori_loop(0, 8, rows, 0)
        out_chunk(7)
        return 0

    lax.fori_loop(0, 2, one_slot, 0)

    def drain(n, _):
        share.first(13 + n)
        share.second(11 + n)
        return 0

    lax.fori_loop(0, 3, drain, 0)
    share.second(14)
    share.second(15)
    share.finish()


VM = pl.BlockSpec(memory_space=pltpu.VMEM)
SM = pl.BlockSpec(memory_space=pltpu.SMEM)


def run_patches(tables, coarse, weights):
    return pl.pallas_call(
        patch_kernel,
        out_shape=jax.ShapeDtypeStruct((16 * GROUP, 128), BF),
        in_specs=[VM] * 11,
        out_specs=pl.BlockSpec(memory_space=pltpu.HBM),
        scratch_shapes=[
            pltpu.VMEM((2 * GROUP, 128), BF),
            pltpu.VMEM((32, NT + 2, NS, 128), BF),
            pltpu.VMEM((32, NT + 2, NS, 128), BF),
            pltpu.VMEM((64, 2, 128, CHAN), BF),
            pltpu.VMEM((65, 2, NT + 2, NS, CHAN), BF),
            pltpu.VMEM((33, 4, NT + 2, NS, CHAN), BF),
            pltpu.VMEM((1, CHAN), F32),
            pltpu.VMEM((2, 8, CHAN), F32),
            pltpu.SemaphoreType.DMA((9,)),
            pltpu.SemaphoreType.DMA((5, 16)),
            pltpu.SemaphoreType.DMA((4,)),
            pltpu.SemaphoreType.DMA,
        ],
        compiler_params=pltpu.CompilerParams(
            vmem_limit_bytes=56 * 2**20, collective_id=1, has_side_effects=True
        ),
        name="patch_net",
    )(*tables, coarse, *weights)


def patch_tables(anchor_y, anchor_x, c0, height, breadth, limit_y, limit_x):
    rows = jnp.arange(XR)
    j = (rows % NS) * NT + rows // NS - 1
    good_x = (j >= 0) & (j < PS)
    x = (anchor_x[:, None] + j).astype(F32)
    at = jnp.clip((x + 0.5) / F - 0.5, 0.0, limit_x - 1.0)
    d = jnp.arange(limit_x).astype(F32)
    hx = jnp.maximum(0.0, 1.0 - jnp.abs(at[:, :, None] - d))
    hx = jnp.where(good_x[None, :, None], hx, 0.0).astype(BF)
    angle_x = x * (2.0 * math.pi / breadth)
    col = jnp.arange(KC)
    xpos = jnp.where(
        col == 12,
        1.0,
        jnp.where(
            col == 13,
            jnp.sin(angle_x)[:, :, None],
            jnp.where(col == 14, jnp.cos(angle_x)[:, :, None], 0.0),
        ),
    )
    xpos = jnp.where(good_x[None, :, None], xpos, 0.0).astype(F32)
    lane = jnp.arange(4096)
    b, k, ch = lane // 128, (lane % 128) // 16, lane % 16
    i = 4 * b - 1 + k
    good_y = (i >= 0) & (i < PS) & (k < 6)
    y = (anchor_y[:, None] + i).astype(F32)
    loc = jnp.clip((y + 0.5) / F - 0.5, 0.0, limit_y - 1.0) - c0.astype(F32)
    loc = jnp.where(good_y, loc, -1000.0).reshape(2, 16, 1, 256)
    angle_y = y * (2.0 * math.pi / height)
    ypos = jnp.where(ch == 12, jnp.sin(angle_y), jnp.where(ch == 13, jnp.cos(angle_y), 0.0))
    v = jnp.arange(16)[:, None]
    extra = jnp.where(v == 12, ypos[:, None], 0.0)
    extra = extra + jnp.where((v == 13) & (ch == 14) | (v == 14) & (ch == 15), 1.0, 0.0)
    extra = jnp.where(good_y, extra, 0.0).astype(F32)
    extra = extra.reshape(2, 16, 16, 256).transpose(0, 2, 1, 3)
    return hx, xpos, loc, extra


def packed_weights(w_in, b_in, gamma, beta, w_mid, w_out):
    w = w_in.transpose(1, 0, 2, 3)
    win = jnp.stack([jnp.pad(w, ((0, 0), (r, 5 - r), (0, 0), (0, 0))) for r in range(4)], axis=3)
    win = win.reshape(3 * 128, 4 * CHAN)
    wmid = jnp.stack([jnp.pad(w_mid, ((r, 1 - r), (0, 0), (0, 0), (0, 0))) for r in range(2)], axis=3)
    wmid = wmid.reshape(4 * 3 * CHAN, 2 * CHAN)
    wo = w_out.transpose(0, 2, 1, 3)
    wout = jnp.stack([jnp.pad(wo, ((r, 3 - r), (0, 0), (0, 0), (0, 0))) for r in range(4)], axis=3)
    wout = wout.reshape(6 * CHAN, 3, 48)
    wout = jnp.pad(wout, ((0, 0), (0, 1), (0, 16))).reshape(6 * CHAN, 256)
    row = jnp.arange(128)[:, None]
    colm = jnp.arange(256)[None]
    keep = (colm >= 64) & (colm < 112) & (row % 16 == (colm - 64) % 12) & (row // 16 == (colm - 64) // 12 + 1)
    ident = keep.astype(BF)
    wout = jnp.concatenate([wout, ident, ident], axis=0)
    return (
        win,
        b_in.reshape(1, CHAN),
        gamma.reshape(1, CHAN),
        beta.reshape(1, CHAN),
        wmid,
        wout,
    )


ACC_ROWS = (3 * TH // 2) * VARS


def place_kernel(info, gathered, num, over, acc, buf, sem):
    acc[...] = jnp.zeros_like(acc)
    lane = lax.broadcasted_iota(jnp.int32, (128, TW), 0)
    x_at = lax.broadcasted_iota(jnp.int32, (128, TW), 1)
    j_at = (lane % NS) * NT + lane // NS

    def fetch(s, k):
        return pltpu.make_async_copy(gathered.at[pl.ds(s * GROUP, GROUP)], buf.at[k], sem.at[k])

    fetch(0, 0).start()

    def slot(s, _):
        k = s % 2

        @pl.when(s < 15)
        def _():
            fetch(s + 1, 1 - k).start()

        fetch(s, k).wait()
        dy, dx, weight = info[0, s], info[1, s], info[2, s]

        @pl.when((weight > 0) & (dx > -PS) & (dx < TW))
        def _():
            onehot = jnp.where(x_at - j_at == dx, weight, 0).astype(F32).astype(BF)
            par = dy % 2
            base = ((dy - par) // 2) * 24

            def part(n, _):
                y = dot(buf[k, pl.ds(pl.multiple_of(n * 384, 384), 384)], onehot)
                at = pl.multiple_of(base + n * 384, 8)
                for h in range(2):
                    acc[par, h, pl.ds(at, 384)] += y[:, h * 128 : h * 128 + 128]
                return 0

            lax.fori_loop(0, 4, part, 0)

        return 0

    lax.fori_loop(0, 16, slot, 0)
    for v in range(VARS):
        for h in range(2):
            cols = slice(h * 128, h * 128 + 128)
            num[v, :, cols] = acc[0, h, pl.ds(v, TH, VARS)]
            num[v, 1:, cols] += acc[1, h, pl.ds(v, TH - 1, VARS)]
            low = acc[0, h, pl.ds(TH * VARS + v, TH // 2, VARS)]
            low = low + acc[1, h, pl.ds((TH - 1) * VARS + v, TH // 2, VARS)]
            over[v, :, cols] = low.astype(BF)


def run_place(info, gathered):
    return pl.pallas_call(
        place_kernel,
        out_shape=(
            jax.ShapeDtypeStruct((VARS, TH, TW), F32),
            jax.ShapeDtypeStruct((VARS, TH // 2, TW), BF),
        ),
        in_specs=[SM, pl.BlockSpec(memory_space=pltpu.HBM)],
        out_specs=(VM, VM),
        scratch_shapes=[
            pltpu.VMEM((2, 2, ACC_ROWS, 128), F32),
            pltpu.VMEM((2, GROUP, 128), BF),
            pltpu.SemaphoreType.DMA((2,)),
        ],
        compiler_params=pltpu.CompilerParams(vmem_limit_bytes=40 * 2**20),
        name="place",
    )(info, gathered)


def covered(dy, dx, weight, rows):
    r = jnp.arange(rows)
    c = jnp.arange(TW)
    in_r = (r >= dy[:, None]) & (r < dy[:, None] + PS)
    in_c = (c >= dx[:, None]) & (c < dx[:, None] + PS)
    left = jnp.where(in_r, weight[:, None], 0).astype(F32)
    return lax.dot_general(left, in_c.astype(F32), (((0,), (0,)), ((), ())), preferred_element_type=F32)


def per_device(coarse_state, anchors, region_count, blend, w_in, b_in, gamma, beta, w_mid, w_out):
    n_region = lax.axis_size("region")
    n_patch = lax.axis_size("patch")
    region = lax.axis_index("region")
    column = lax.axis_index("patch")
    limit = coarse_state.shape[1] * n_region * n_patch
    band = limit // n_region
    up = [(i, i + 1) for i in range(n_region - 1)]

    slots = anchors.shape[0]
    weight = jnp.where(jnp.arange(slots) < region_count[0], blend, 0).astype(jnp.int32)
    dy = anchors[:, 0] - region * TH
    dx = anchors[:, 1] - column * TW
    info = jnp.stack([dy, dx, weight])
    above = lax.ppermute(jnp.stack([dy - TH, anchors[:, 1], weight]), "region", up)

    shard = jnp.pad(coarse_state.transpose(1, 0, 2), ((0, 0), (0, 4), (0, 0)))
    coarse = run_exchange(shard).reshape(KC, limit)

    mine = lax.dynamic_slice(anchors, (column * 2, jnp.int32(0)), (2, 2))
    tables = patch_tables(
        mine[:, 0], mine[:, 1], region * band - 2, TH * n_region, TW * n_patch, limit, limit
    )
    weights = packed_weights(w_in, b_in, gamma, beta, w_mid, w_out)
    gathered = run_patches(tables, coarse, weights)
    num, over = run_place(info, gathered)
    cover = covered(dy, dx, weight, TH) + covered(above[0], above[1] - column * TW, above[2], TH)
    low = lax.ppermute(over, "region", up).astype(F32)
    num = num + jnp.pad(low, ((0, 0), (0, TH // 2), (0, 0)))
    return num / jnp.maximum(cover, 1.0)


def solution(mesh):
    return jax.shard_map(
        per_device,
        mesh=mesh,
        in_specs=(
            P(None, ("region", "patch"), None),
            P("region", None),
            P("region"),
            P("region"),
            P(),
            P(),
            P(),
            P(),
            P(),
            P(),
        ),
        out_specs=P(None, "region", "patch"),
        check_vma=False,
    )
```

```python
import math
from functools import partial

import jax
import jax.numpy as jnp
from jax import lax
from jax.experimental import pallas as pl
from jax.experimental.pallas import tpu as pltpu
from jax.sharding import PartitionSpec as P

VARS = 12
CHAN = 128
PS = 128
F = 8
TH = 128
TW = 256
BF = jnp.bfloat16
F32 = jnp.float32
NT, NS = 8, 16
XR = (NT + 2) * NS
KC = 512
GROUP = PS * VARS
UI, UF, UN = 4, 4, 8
MESH = pl.DeviceIdType.MESH


def dot(a, b):
    return jnp.dot(a, b, preferred_element_type=F32)


def dot_nt(a, b):
    return lax.dot_general(a, b, (((1,), (1,)), ((), ())), preferred_element_type=F32)


def split(x):
    hi = x.astype(BF)
    return hi, (x - hi.astype(F32)).astype(BF)


def row_halo(x):
    rows = x.shape[0]
    s = lax.broadcasted_iota(jnp.int32, (rows, NS, CHAN), 1)
    before = jnp.where(s == 0, 0.0, pltpu.roll(x[:, NT - 1], 1, 1))
    after = jnp.where(s == NS - 1, 0.0, pltpu.roll(x[:, 0], NS - 1, 1))
    return before, after


def column_tables(anchor_x, breadth, limit):
    row = lax.broadcasted_iota(jnp.int32, (XR, 256), 0)
    d = lax.broadcasted_iota(jnp.int32, (XR, 256), 1)
    j = (row % NS) * NT + row // NS - 1
    good = (j >= 0) & (j < PS)
    x = (anchor_x + j).astype(F32)
    at = jnp.clip((x + 0.5) * (1.0 / F) - 0.5, 0.0, limit - 1.0)
    hat = jnp.maximum(0.0, 1.0 - jnp.abs(at - d.astype(F32)))
    hat = jnp.where(good, hat, 0.0).astype(BF)
    lane = d[:, :128]
    angle = x[:, :128] * (2.0 * math.pi / breadth)
    pos = jnp.where(lane == 13, jnp.sin(angle), jnp.where(lane == 14, jnp.cos(angle), 0.0))
    pos = jnp.where(lane == 12, 1.0, pos)
    pos = jnp.where(good[:, :128], pos, 0.0)
    return hat, jnp.concatenate([pos, jnp.zeros((XR, KC - 128), F32)], axis=1)


def row_tables(anchor_y, c0, height, limit, loc_ref, pos_ref):
    g = lax.broadcasted_iota(jnp.int32, (16, 256), 0)
    lane = lax.broadcasted_iota(jnp.int32, (16, 256), 1)
    k, ch = (lane % 128) // 16, lane % 16
    i = 8 * g + 4 * (lane // 128) - 1 + k
    good = (i >= 0) & (i < PS) & (k < 6)
    y = (anchor_y + i).astype(F32)
    loc = jnp.clip((y + 0.5) * (1.0 / F) - 0.5, 0.0, limit - 1.0) - c0.astype(F32)
    loc_ref[...] = jnp.where(good, loc - 14.0, -1000.0)
    angle = y * (2.0 * math.pi / height)
    pos = jnp.where(ch == 12, jnp.sin(angle), jnp.where(ch == 13, jnp.cos(angle), 0.0))
    pos_ref[0] = jnp.where(good, pos, 0.0)
    pos_ref[1] = jnp.where(good, 1.0, 0.0)


def interp_stage(hx, xpos, coarse, loc_ref, pos_ref, xh, xl):
    chi, clo = split(coarse)
    t1 = dot_nt(hx, chi) + dot_nt(hx, clo) + xpos
    hi, lo = split(t1)
    lhs = jnp.concatenate([hi, lo], axis=0)
    v_at = lax.broadcasted_iota(jnp.int32, (16, 256), 0)
    ch_at = lax.broadcasted_iota(jnp.int32, (16, 256), 1) % 16
    diag = jnp.where((v_at == ch_at) & (v_at < VARS), 1.0, 0.0).astype(BF)
    pick_y = jnp.where(v_at == 12, 1.0, 0.0)
    pick_x = jnp.where((v_at == 13) & (ch_at == 14) | (v_at == 14) & (ch_at == 15), 1.0, 0.0)
    one = jnp.ones((16, 256), BF)
    none = jnp.zeros((16, 256), BF)

    def step(g, _):
        loc = jnp.broadcast_to(loc_ref[pl.ds(g, 1)], (16, 256)).astype(BF)
        extra = pick_y * pos_ref[0, pl.ds(g, 1)] + pick_x * pos_ref[1, pl.ds(g, 1)]
        blocks = []
        for c in range(28):
            hat = jnp.maximum(none, one - jnp.abs(loc - BF(c - 14))) * diag
            if c == 0:
                hat = hat + extra.astype(BF)
            blocks.append(hat)
        blocks.append(jnp.zeros((64, 256), BF))
        res = dot(lhs, jnp.concatenate(blocks, axis=0))
        x = res[:XR] + res[XR:]
        for h in range(2):
            xa, xb = split(x[:, h * 128 : h * 128 + 128])
            xh[2 * g + h] = xa.reshape(NT + 2, NS, 128)
            xl[2 * g + h] = xb.reshape(NT + 2, NS, 128)
        return 0

    lax.fori_loop(0, 16, step, 0, unroll=UI)


def first_stage(win, b_in, xh, fa, shift, sums):
    bias = b_in[...]
    sums[...] = jnp.zeros_like(sums)

    def rows(at, n):
        lhs = jnp.concatenate(
            [xh[pl.ds(at, n), dx : dx + 8].reshape(n * 128, 128) for dx in range(3)], axis=1
        )
        return dot(lhs, win[...])

    sample = jnp.mean(rows(16, 1)[:, :128] + bias, axis=0, keepdims=True)
    shift[...] = sample

    def step(it, _):
        acc = rows(4 * it, 4)
        base = shift[...]
        one = jnp.zeros((8, CHAN), F32)
        two = jnp.zeros((8, CHAN), F32)
        for r in range(4):
            x = (acc[:, r * 128 : r * 128 + 128] + bias).astype(BF)
            for b in range(4):
                fa[8 * it + 2 * b + r // 2, r % 2] = x[b * 128 : b * 128 + 128]
            d = (x.astype(F32) - base).reshape(64, 8, CHAN)
            one = one + jnp.sum(d, axis=0)
            two = two + jnp.sum(d * d, axis=0)
        sums[0] += one
        sums[1] += two
        return 0

    lax.fori_loop(0, 8, step, 0, unroll=UF)


def group_mean(x):
    lane = lax.broadcasted_iota(jnp.int32, x.shape, 1)
    total = x
    for k in (1, 2):
        low = (lane // k) % 2 == 0
        total = total + jnp.where(low, pltpu.roll(total, CHAN - k, 1), pltpu.roll(total, k, 1))
    return total * 0.25


def scale_shift(sums, shift, gamma, beta):
    n = float(PS * PS)
    one = jnp.broadcast_to(jnp.sum(sums[0], axis=0, keepdims=True), (8, CHAN)) / n
    two = jnp.broadcast_to(jnp.sum(sums[1], axis=0, keepdims=True), (8, CHAN)) / n
    own_var = jnp.maximum(two - one * one, 0.0)
    mean = one + shift[...]
    g_mean = group_mean(mean)
    off = mean - g_mean
    g_var = group_mean(own_var + off * off)
    scale = gamma[...] / jnp.sqrt(g_var + 1e-05)
    return scale[0:1], (beta[...] - g_mean * scale)[0:1]


def norm_stage(scale, offset, fa, nb):
    half_scale = 0.5 * scale
    half_offset = 0.5 * offset

    def step(p, _):
        x = fa[p].astype(F32).reshape(2, NT, NS, CHAN)
        h = x * half_scale + half_offset
        y = h + h * jnp.tanh(h)
        before, after = row_halo(y)
        for r in range(2):
            at, k = (p, 1) if r == 0 else (p + 1, 0)
            nb[at, k, 1 : NT + 1] = y[r].astype(BF)
            nb[at, k, 0] = before[r].astype(BF)
            nb[at, k, NT + 1] = after[r].astype(BF)
        return 0

    lax.fori_loop(0, 64, step, 0, unroll=UN)


def mid_step(it, wmid, nb, fa, sb):
    p0 = 8 * it
    lhs = []
    for k in range(4):
        for dx in range(3):
            lhs.append(nb[pl.ds(p0 + k // 2, 8), k % 2, dx : dx + 8].reshape(1024, CHAN))
    acc = dot(jnp.concatenate(lhs, axis=1), wmid[...])
    for r in range(2):
        x = acc[:, r * 128 : r * 128 + 128] + fa[pl.ds(p0, 8), r].astype(F32).reshape(1024, CHAN)
        x = x.reshape(8, NT, NS, CHAN)
        before, after = row_halo(x)
        for b in range(8):
            at = 2 * b + r + 1
            q, k = 4 * it + at // 4, at % 4
            sb[q, k, 1 : NT + 1] = x[b].astype(BF)
            sb[q, k, 0] = before[b].astype(BF)
            sb[q, k, NT + 1] = after[b].astype(BF)


def out_step(it, wout, sb, xh, xl):
    g0 = 4 * it
    lhs = [sb[pl.ds(g0 + k // 4, 4), k % 4].reshape(4 * XR, CHAN) for k in range(6)]
    lhs.append(xh[pl.ds(g0, 4)].reshape(4 * XR, CHAN))
    lhs.append(xl[pl.ds(g0, 4)].reshape(4 * XR, CHAN))
    acc = dot(jnp.concatenate(lhs, axis=1), wout[...])
    y0 = acc[:, :128].reshape(4, NT + 2, NS, 128)
    y1 = acc[:, 128:].reshape(4, NT + 2, NS, 128)
    centre = pltpu.roll(y0[:, 1 : NT + 1].reshape(512, 128), 64, 1).reshape(4, NT, NS, 128)
    res = y0[:, 0:NT] + centre + y1[:, 2 : NT + 2]
    res = res.reshape(4, 128, 128)
    lane = lax.broadcasted_iota(jnp.int32, (128, 128), 1)
    parts = []
    for h in range(2):
        both = jnp.where(lane < 48, res[2 * h], pltpu.roll(res[2 * h + 1], 48, 1))
        parts.append(jnp.transpose(both)[:96])
    return jnp.concatenate(parts, axis=0).astype(BF)


class CoarseRows:
    def __init__(self, shard, rows, send_sem, recv_sem):
        self.shard, self.rows = shard, rows
        self.send_sem, self.recv_sem = send_sem, recv_sem
        self.r, self.p = lax.axis_index("region"), lax.axis_index("patch")
        self.n_r, self.n_p = lax.axis_size("region"), lax.axis_size("patch")
        self.has_up, self.has_down = self.r > 0, self.r < self.n_r - 1
        self.feeds_down = (self.p == self.n_p - 1) & self.has_down
        self.feeds_up = (self.p < 5) & self.has_up

    def prepare(self, coarse_state):
        r, n_r, rows = self.r, self.n_r, self.rows
        rows[28:32] = jnp.zeros((4, 16, 256), F32)

        @pl.when(r == 0)
        def _():
            rows[0:2] = jnp.zeros((2, 16, 256), F32)

        @pl.when(r == n_r - 1)
        def _():
            rows[18:28] = jnp.zeros((10, 16, 256), F32)

        for c in range(2):
            self.shard[c, 0:VARS] = coarse_state[:, c, :]
            self.shard[c, VARS:16] = jnp.zeros((16 - VARS, 256), F32)
        rows[pl.ds(2 + 2 * self.p, 2)] = self.shard[...]

    def greet(self):
        r, p, n_p = self.r, self.p, self.n_p
        barrier = pltpu.get_barrier_semaphore()

        def hello(to):
            pl.semaphore_signal(barrier, inc=1, device_id=to, device_id_type=MESH)

        for d in range(1, n_p):
            hello((r, (p + d) % n_p))

        @pl.when(self.has_up)
        def _():
            hello((r - 1, n_p - 1))

        @pl.when(self.has_down)
        def _():
            for k in range(5):
                hello((r + 1, k))

        count = n_p - 1 + jnp.where(self.feeds_down, n_p, 0) + jnp.where(self.feeds_up, n_p, 0)
        pl.semaphore_wait(barrier, count)

    def copy(self, row, key, k, to):
        return pltpu.make_async_remote_copy(
            src_ref=self.shard,
            dst_ref=self.rows.at[pl.ds(row, 2)],
            send_sem=self.send_sem.at[k],
            recv_sem=self.recv_sem.at[key],
            device_id=to,
            device_id_type=MESH,
        )

    def each(self, act):
        r, p, n_p = self.r, self.p, self.n_p

        @pl.when(self.feeds_down)
        def _():
            for k in range(n_p):
                act(self.copy(0, 0, 7 + k, (r + 1, k)))

        @pl.when(self.feeds_up)
        def _():
            for k in range(n_p):
                act(self.copy(18 + 2 * p, 9 + p, 15 + k, (r - 1, k)))

        for d in range(1, n_p):
            act(self.copy(2 + 2 * p, 1 + p, d - 1, (r, (p + d) % n_p)))

    def start(self):
        self.each(lambda c: c.start())

    def finish(self):
        r, p, n_p = self.r, self.p, self.n_p
        for d in range(1, n_p):
            q = (p + d) % n_p
            self.copy(2 + 2 * q, 1 + q, 0, (r, q)).wait_recv()

        @pl.when(self.has_up)
        def _():
            self.copy(0, 0, 0, (r - 1, n_p - 1)).wait_recv()

        @pl.when(self.has_down)
        def _():
            for k in range(5):
                self.copy(18 + 2 * k, 9 + k, 0, (r + 1, k)).wait_recv()

        self.each(lambda c: c.wait_send())


CHUNK = 16 * VARS
HALF = CHUNK // 2


class Sharer:
    def __init__(self, out, g, send_sem, recv_sem, tail_sem, own_sem):
        self.out, self.g = out, g
        self.send_sem, self.recv_sem = send_sem, recv_sem
        self.tail_sem, self.own_sem = tail_sem, own_sem
        p = lax.axis_index("patch")
        z, y = p // 2, p % 2
        self.me = p
        self.fore = ((z + 1) % 4) * 2 + y
        self.back = ((z + 3) % 4) * 2 + y
        self.pair = z * 2 + 1 - y
        self.fore_pair = ((z + 1) % 4) * 2 + 1 - y
        self.back_pair = ((z + 3) % 4) * 2 + 1 - y

    def at(self, owner, q, half=None):
        start = (owner * 16 + q) * CHUNK
        if half is None:
            return self.g.at[pl.ds(pl.multiple_of(start, CHUNK), CHUNK)]
        return self.g.at[pl.ds(pl.multiple_of(start + half * HALF, HALF), HALF)]

    def remote(self, src, dst, stream, sem, to):
        return pltpu.make_async_remote_copy(
            src_ref=src,
            dst_ref=dst,
            send_sem=self.send_sem.at[stream],
            recv_sem=sem,
            device_id={"patch": to},
            device_id_type=MESH,
        )

    def arrived(self, owner, q, stream):
        there = self.at(owner, q)
        self.remote(there, there, stream, self.recv_sem.at[stream, q], self.fore).wait_recv()

    def own(self, q):
        src = self.out.at[pl.ds(pl.multiple_of(q * CHUNK, CHUNK), CHUNK)]
        dst = self.at(self.me, q)
        self.remote(src, dst, 2, self.recv_sem.at[2, q], self.pair).start()
        self.remote(src, dst, 0, self.recv_sem.at[0, q], self.fore).start()
        self.remote(src, dst, 1, self.recv_sem.at[1, q], self.back).start()
        pltpu.make_async_copy(src, dst, self.own_sem).start()

    def first(self, q):
        self.arrived(self.pair, q, 2)
        there = self.at(self.pair, q)
        self.remote(there, there, 3, self.recv_sem.at[3, q], self.fore).start()
        self.remote(there, there, 4, self.recv_sem.at[4, q], self.back).start()
        self.arrived(self.back, q, 0)
        there = self.at(self.back, q, 0)
        self.remote(there, there, 5, self.tail_sem.at[0], self.fore).start()
        self.arrived(self.fore, q, 1)
        there = self.at(self.fore, q, 1)
        self.remote(there, there, 6, self.tail_sem.at[1], self.back).start()

    def second(self, q):
        self.arrived(self.back_pair, q, 3)
        there = self.at(self.back_pair, q, 0)
        self.remote(there, there, 7, self.tail_sem.at[2], self.fore).start()
        self.arrived(self.fore_pair, q, 4)
        there = self.at(self.fore_pair, q, 1)
        self.remote(there, there, 8, self.tail_sem.at[3], self.back).start()

    def finish(self):
        whole = self.g.at[pl.ds(0, 2 * GROUP)]
        part = self.g.at[pl.ds(0, GROUP)]
        for k in range(4):
            self.remote(part, part, 5 + k, self.tail_sem.at[k], self.fore).wait()
        for k in range(5):
            self.remote(whole, whole, k, self.tail_sem.at[0], self.fore).wait_send()
        pltpu.make_async_copy(whole, whole, self.own_sem).wait()


def pack_weights(w_in, w_mid, win, wmid):
    zero = jnp.zeros((CHAN, CHAN), BF)
    for dx in range(3):
        for r in range(4):
            cols = slice(r * CHAN, r * CHAN + CHAN)
            parts = [w_in[k - r, dx] if 0 <= k - r < 3 else zero[:16] for k in range(8)]
            win[dx * 128 : dx * 128 + 128, cols] = jnp.concatenate(parts, axis=0)
        for r in range(2):
            cols = slice(r * CHAN, r * CHAN + CHAN)
            for k in range(4):
                at = (k * 3 + dx) * CHAN
                wmid[at : at + CHAN, cols] = w_mid[k - r, dx] if 0 <= k - r < 3 else zero


def patch_kernel(
    grid_size, anchors, coarse_state, w_in, b_in, gamma, beta, w_mid, wout, g,
    shard, rows, loc, pos, win, wmid, out, xh, xl, fa, nb, sb, shift, sums,
    csend_sem, crecv_sem, send_sem, recv_sem, tail_sem, own_sem,
):
    height, breadth, limit_y, limit_x = grid_size
    coarse = CoarseRows(shard, rows, csend_sem, crecv_sem)
    share = Sharer(out, g, send_sem, recv_sem, tail_sem, own_sem)
    coarse.prepare(coarse_state)
    coarse.greet()
    coarse.start()
    pack_weights(w_in, w_mid, win, wmid)
    zero = jnp.zeros((NT + 2, NS, CHAN), BF)
    nb[0, 0] = zero
    nb[64, 1] = zero
    sb[0, 0] = zero
    sb[32, 1] = zero
    c0 = coarse.r * 16 - 2
    coarse.finish()

    def one_slot(slot, _):
        here = share.me * 2 + slot
        row_tables(anchors[here, 0], c0, height, limit_y, loc, pos)
        hx, xpos = column_tables(anchors[here, 1], breadth, limit_x)
        interp_stage(hx, xpos, rows[...].reshape(KC, 256), loc, pos, xh, xl)

        @pl.when(slot == 1)
        def _():
            share.first(6)
            share.first(7)

        first_stage(win, b_in, xh, fa, shift, sums)
        scale, offset = scale_shift(sums, shift, gamma, beta)
        norm_stage(scale, offset, fa, nb)

        def out_chunk(it):
            at = pl.multiple_of((slot * 8 + it) * CHUNK, CHUNK)
            out[pl.ds(at, CHUNK)] = out_step(it, wout, sb, xh, xl)

        mid_step(0, wmid, nb, fa, sb)
        mid_step(1, wmid, nb, fa, sb)

        def step(it, _):
            out_chunk(it - 2)
            mid_step(it, wmid, nb, fa, sb)
            q = slot * 8 + it - 2
            share.own(q)

            @pl.when(it >= 4)
            def _():
                share.first(q - 2)

            @pl.when(slot == 1)
            def _():
                share.second(it - 2)

            return 0

        lax.fori_loop(2, 8, step, 0)
        out_chunk(6)
        out_chunk(7)
        q = slot * 8 + 6
        share.own(q)
        share.own(q + 1)
        share.first(q - 2)
        share.first(q - 1)
        return 0

    lax.fori_loop(0, 2, one_slot, 0)
    share.second(6)
    share.second(7)
    share.first(14)
    share.first(15)

    def drain(q, _):
        share.second(q)
        return 0

    lax.fori_loop(8, 16, drain, 0)
    share.finish()


VM = pl.BlockSpec(memory_space=pltpu.VMEM)
SM = pl.BlockSpec(memory_space=pltpu.SMEM)


def run_patches(grid_size, anchors, coarse_state, weights):
    return pl.pallas_call(
        partial(patch_kernel, grid_size),
        out_shape=jax.ShapeDtypeStruct((16 * GROUP, 128), BF),
        in_specs=[SM] + [VM] * 7,
        out_specs=pl.BlockSpec(memory_space=pltpu.HBM),
        scratch_shapes=[
            pltpu.VMEM((2, 16, 256), F32),
            pltpu.VMEM((32, 16, 256), F32),
            pltpu.VMEM((16, 256), F32),
            pltpu.VMEM((2, 16, 256), F32),
            pltpu.VMEM((3 * 128, 4 * CHAN), BF),
            pltpu.VMEM((12 * CHAN, 2 * CHAN), BF),
            pltpu.VMEM((2 * GROUP, 128), BF),
            pltpu.VMEM((32, NT + 2, NS, 128), BF),
            pltpu.VMEM((32, NT + 2, NS, 128), BF),
            pltpu.VMEM((64, 2, 128, CHAN), BF),
            pltpu.VMEM((65, 2, NT + 2, NS, CHAN), BF),
            pltpu.VMEM((33, 4, NT + 2, NS, CHAN), BF),
            pltpu.VMEM((1, CHAN), F32),
            pltpu.VMEM((2, 8, CHAN), F32),
            pltpu.SemaphoreType.DMA((23,)),
            pltpu.SemaphoreType.DMA((14,)),
            pltpu.SemaphoreType.DMA((9,)),
            pltpu.SemaphoreType.DMA((5, 16)),
            pltpu.SemaphoreType.DMA((4,)),
            pltpu.SemaphoreType.DMA,
        ],
        compiler_params=pltpu.CompilerParams(
            vmem_limit_bytes=56 * 2**20, collective_id=0, has_side_effects=True
        ),
        name="patch_net",
    )(anchors, coarse_state, *weights)


def packed_out(w_out):
    wo = w_out.transpose(0, 2, 1, 3)
    wout = jnp.stack([jnp.pad(wo, ((r, 3 - r), (0, 0), (0, 0), (0, 0))) for r in range(4)], axis=3)
    wout = wout.reshape(6 * CHAN, 3, 48)
    wout = jnp.pad(wout, ((0, 0), (0, 1), (0, 16))).reshape(6 * CHAN, 256)
    row = jnp.arange(128)[:, None]
    col = jnp.arange(256)[None] - 64
    keep = (col >= 0) & (col < 48) & (row % 16 == col % 12) & (row // 16 == col // 12 + 1)
    ident = keep.astype(BF)
    return jnp.concatenate([wout, ident, ident], axis=0)


ACC_ROWS = (3 * TH // 2) * VARS


def place_kernel(anchors, count, blend, gathered, num, cover, over, acc, cov, buf, sem):
    top = lax.axis_index("region") * TH
    left = lax.axis_index("patch") * TW
    acc[...] = jnp.zeros_like(acc)
    cov[...] = jnp.zeros_like(cov)
    lane = lax.broadcasted_iota(jnp.int32, (128, TW), 0)
    x_at = lax.broadcasted_iota(jnp.int32, (128, TW), 1)
    j_at = (lane % NS) * NT + lane // NS
    cov_y = lax.broadcasted_iota(jnp.int32, cov.shape, 0)
    cov_x = lax.broadcasted_iota(jnp.int32, cov.shape, 1)

    def fetch(s, k):
        return pltpu.make_async_copy(gathered.at[pl.ds(s * GROUP, GROUP)], buf.at[k], sem.at[k])

    fetch(0, 0).start()

    def slot(s, _):
        k = s % 2

        @pl.when(s < 15)
        def _():
            fetch(s + 1, 1 - k).start()

        fetch(s, k).wait()
        dy, dx = anchors[s, 0] - top, anchors[s, 1] - left

        @pl.when((s < count[0]) & (dx > -PS) & (dx < TW))
        def _():
            weight = blend[s].astype(F32)
            onehot = jnp.where(x_at - j_at == dx, weight, 0.0).astype(BF)
            par = dy % 2
            base = ((dy - par) // 2) * 24

            def part(n, _):
                y = dot(buf[k, pl.ds(pl.multiple_of(n * 384, 384), 384)], onehot)
                at = pl.multiple_of(base + n * 384, 8)
                for h in range(2):
                    acc[par, h, pl.ds(at, 384)] += y[:, h * 128 : h * 128 + 128]
                return 0

            lax.fori_loop(0, 4, part, 0, unroll=True)
            inside = (cov_y >= dy) & (cov_y < dy + PS) & (cov_x >= dx) & (cov_x < dx + PS)
            cov[...] += jnp.where(inside, weight, 0.0)

        return 0

    lax.fori_loop(0, 16, slot, 0)
    cover[...] = cov[:TH]
    over[VARS] = cov[TH:].astype(BF)
    for v in range(VARS):
        for h in range(2):
            cols = slice(h * 128, h * 128 + 128)
            num[v, :, cols] = acc[0, h, pl.ds(v, TH, VARS)]
            num[v, 1:, cols] += acc[1, h, pl.ds(v, TH - 1, VARS)]
            low = acc[0, h, pl.ds(TH * VARS + v, TH // 2, VARS)]
            low = low + acc[1, h, pl.ds((TH - 1) * VARS + v, TH // 2, VARS)]
            over[v, :, cols] = low.astype(BF)


def run_place(anchors, count, blend, gathered):
    return pl.pallas_call(
        place_kernel,
        out_shape=(
            jax.ShapeDtypeStruct((VARS, TH, TW), F32),
            jax.ShapeDtypeStruct((TH, TW), F32),
            jax.ShapeDtypeStruct((VARS + 1, TH // 2, TW), BF),
        ),
        in_specs=[SM, SM, SM, pl.BlockSpec(memory_space=pltpu.HBM)],
        out_specs=(VM, VM, VM),
        scratch_shapes=[
            pltpu.VMEM((2, 2, ACC_ROWS, 128), F32),
            pltpu.VMEM((3 * TH // 2, TW), F32),
            pltpu.VMEM((2, GROUP, 128), BF),
            pltpu.SemaphoreType.DMA((2,)),
        ],
        compiler_params=pltpu.CompilerParams(vmem_limit_bytes=60 * 2**20),
        name="place",
    )(anchors, count, blend, gathered)


def per_device(coarse_state, anchors, region_count, blend, w_in, b_in, gamma, beta, w_mid, w_out):
    n_region = lax.axis_size("region")
    n_patch = lax.axis_size("patch")
    limit_y = coarse_state.shape[1] * n_region * n_patch
    limit_x = coarse_state.shape[2]
    grid_size = (TH * n_region, TW * n_patch, limit_y, limit_x)
    up = [(i, i + 1) for i in range(n_region - 1)]
    weights = (
        w_in,
        b_in.reshape(1, CHAN),
        gamma.reshape(1, CHAN),
        beta.reshape(1, CHAN),
        w_mid,
        packed_out(w_out),
    )
    gathered = run_patches(grid_size, anchors, coarse_state, weights)
    num, cover, over = run_place(anchors, region_count, blend, gathered)
    low = lax.ppermute(over, "region", up).astype(F32)
    low = jnp.pad(low, ((0, 0), (0, TH // 2), (0, 0)))
    return (num + low[:VARS]) / jnp.maximum(cover + low[VARS], 1.0)


def solution(mesh):
    return jax.shard_map(
        per_device,
        mesh=mesh,
        in_specs=(
            P(None, ("region", "patch"), None),
            P("region", None),
            P("region"),
            P("region"),
            P(),
            P(),
            P(),
            P(),
            P(),
            P(),
        ),
        out_specs=P(None, "region", "patch"),
        check_vma=False,
    )
```

```python
import math
from functools import partial

import jax
import jax.numpy as jnp
from jax import lax
from jax.experimental import pallas as pl
from jax.experimental.pallas import tpu as pltpu
from jax.sharding import PartitionSpec as P

VARS = 12
CHAN = 128
PS = 128
F = 8
TH = 128
TW = 256
BF = jnp.bfloat16
F32 = jnp.float32
NT, NS = 8, 16
XR = (NT + 2) * NS
KC = 512
GROUP = PS * VARS
UI, UF, UN = 4, 4, 8
MESH = pl.DeviceIdType.MESH


def dot(a, b):
    return jnp.dot(a, b, preferred_element_type=F32)


def dot_nt(a, b):
    return lax.dot_general(a, b, (((1,), (1,)), ((), ())), preferred_element_type=F32)


def split(x):
    hi = x.astype(BF)
    return hi, (x - hi.astype(F32)).astype(BF)


def row_halo(x):
    rows = x.shape[0]
    s = lax.broadcasted_iota(jnp.int32, (rows, NS, CHAN), 1)
    before = jnp.where(s == 0, 0.0, pltpu.roll(x[:, NT - 1], 1, 1))
    after = jnp.where(s == NS - 1, 0.0, pltpu.roll(x[:, 0], NS - 1, 1))
    return before, after


def column_tables(anchor_x, breadth, limit):
    row = lax.broadcasted_iota(jnp.int32, (XR, 256), 0)
    d = lax.broadcasted_iota(jnp.int32, (XR, 256), 1)
    j = (row % NS) * NT + row // NS - 1
    good = (j >= 0) & (j < PS)
    x = (anchor_x + j).astype(F32)
    at = jnp.clip((x + 0.5) * (1.0 / F) - 0.5, 0.0, limit - 1.0)
    hat = jnp.maximum(0.0, 1.0 - jnp.abs(at - d.astype(F32)))
    hat = jnp.where(good, hat, 0.0).astype(BF)
    lane = d[:, :128]
    angle = x[:, :128] * (2.0 * math.pi / breadth)
    pos = jnp.where(lane == 13, jnp.sin(angle), jnp.where(lane == 14, jnp.cos(angle), 0.0))
    pos = jnp.where(lane == 12, 1.0, pos)
    pos = jnp.where(good[:, :128], pos, 0.0)
    return hat, jnp.concatenate([pos, jnp.zeros((XR, KC - 128), F32)], axis=1)


def row_tables(anchor_y, c0, height, limit, loc_ref, pos_ref):
    g = lax.broadcasted_iota(jnp.int32, (16, 256), 0)
    lane = lax.broadcasted_iota(jnp.int32, (16, 256), 1)
    k, ch = (lane % 128) // 16, lane % 16
    i = 8 * g + 4 * (lane // 128) - 1 + k
    good = (i >= 0) & (i < PS) & (k < 6)
    y = (anchor_y + i).astype(F32)
    loc = jnp.clip((y + 0.5) * (1.0 / F) - 0.5, 0.0, limit - 1.0) - c0.astype(F32)
    loc_ref[...] = jnp.where(good, loc - 14.0, -1000.0)
    angle = y * (2.0 * math.pi / height)
    pos = jnp.where(ch == 12, jnp.sin(angle), jnp.where(ch == 13, jnp.cos(angle), 0.0))
    pos_ref[0] = jnp.where(good, pos, 0.0)
    pos_ref[1] = jnp.where(good, 1.0, 0.0)


def interp_stage(hx, xpos, coarse, loc_ref, pos_ref, xh, xl):
    t1 = dot_nt(hx, coarse) + xpos
    hi, lo = split(t1)
    lhs = jnp.concatenate([hi, lo], axis=0)
    v_at = lax.broadcasted_iota(jnp.int32, (16, 256), 0)
    ch_at = lax.broadcasted_iota(jnp.int32, (16, 256), 1) % 16
    diag = jnp.where((v_at == ch_at) & (v_at < VARS), 1.0, 0.0).astype(BF)
    pick_y = jnp.where(v_at == 12, 1.0, 0.0)
    pick_x = jnp.where((v_at == 13) & (ch_at == 14) | (v_at == 14) & (ch_at == 15), 1.0, 0.0)
    one = jnp.ones((16, 256), BF)
    none = jnp.zeros((16, 256), BF)

    def step(g, _):
        loc = jnp.broadcast_to(loc_ref[pl.ds(g, 1)], (16, 256)).astype(BF)
        extra = pick_y * pos_ref[0, pl.ds(g, 1)] + pick_x * pos_ref[1, pl.ds(g, 1)]
        blocks = []
        for c in range(28):
            hat = jnp.maximum(none, one - jnp.abs(loc - BF(c - 14))) * diag
            if c == 0:
                hat = hat + extra.astype(BF)
            blocks.append(hat)
        blocks.append(jnp.zeros((64, 256), BF))
        res = dot(lhs, jnp.concatenate(blocks, axis=0))
        x = res[:XR] + res[XR:]
        for h in range(2):
            xa, xb = split(x[:, h * 128 : h * 128 + 128])
            xh[2 * g + h] = xa.reshape(NT + 2, NS, 128)
            xl[2 * g + h] = xb.reshape(NT + 2, NS, 128)
        return 0

    lax.fori_loop(0, 16, step, 0, unroll=UI)


def first_stage(win, b_in, xh, fa, shift, sums):
    bias = b_in[...]
    sums[...] = jnp.zeros_like(sums)

    def rows(at, n):
        lhs = jnp.concatenate(
            [xh[pl.ds(at, n), dx : dx + 8].reshape(n * 128, 128) for dx in range(3)], axis=1
        )
        return dot(lhs, win[...])

    sample = jnp.mean(rows(16, 1)[:, :128] + bias, axis=0, keepdims=True)
    shift[...] = sample

    def step(it, _):
        acc = rows(4 * it, 4)
        base = shift[...]
        one = jnp.zeros((8, CHAN), F32)
        two = jnp.zeros((8, CHAN), F32)
        for r in range(4):
            x = (acc[:, r * 128 : r * 128 + 128] + bias).astype(BF)
            for b in range(4):
                fa[8 * it + 2 * b + r // 2, r % 2] = x[b * 128 : b * 128 + 128]
            d = (x.astype(F32) - base).reshape(64, 8, CHAN)
            one = one + jnp.sum(d, axis=0)
            two = two + jnp.sum(d * d, axis=0)
        sums[0] += one
        sums[1] += two
        return 0

    lax.fori_loop(0, 8, step, 0, unroll=UF)


def group_mean(x):
    lane = lax.broadcasted_iota(jnp.int32, x.shape, 1)
    total = x
    for k in (1, 2):
        low = (lane // k) % 2 == 0
        total = total + jnp.where(low, pltpu.roll(total, CHAN - k, 1), pltpu.roll(total, k, 1))
    return total * 0.25


def scale_shift(sums, shift, gamma, beta):
    n = float(PS * PS)
    one = jnp.broadcast_to(jnp.sum(sums[0], axis=0, keepdims=True), (8, CHAN)) / n
    two = jnp.broadcast_to(jnp.sum(sums[1], axis=0, keepdims=True), (8, CHAN)) / n
    own_var = jnp.maximum(two - one * one, 0.0)
    mean = one + shift[...]
    g_mean = group_mean(mean)
    off = mean - g_mean
    g_var = group_mean(own_var + off * off)
    scale = gamma[...] / jnp.sqrt(g_var + 1e-05)
    return scale[0:1], (beta[...] - g_mean * scale)[0:1]


def norm_stage(scale, offset, fa, nb):
    half_scale = 0.5 * scale
    half_offset = 0.5 * offset

    def step(p, _):
        x = fa[p].astype(F32).reshape(2, NT, NS, CHAN)
        h = x * half_scale + half_offset
        y = h + h * jnp.tanh(h)
        before, after = row_halo(y)
        for r in range(2):
            at, k = (p, 1) if r == 0 else (p + 1, 0)
            nb[at, k, 1 : NT + 1] = y[r].astype(BF)
            nb[at, k, 0] = before[r].astype(BF)
            nb[at, k, NT + 1] = after[r].astype(BF)
        return 0

    lax.fori_loop(0, 64, step, 0, unroll=UN)


def mid_step(it, wmid, nb, fa, sb):
    p0 = 8 * it
    lhs = []
    for k in range(4):
        for dx in range(3):
            lhs.append(nb[pl.ds(p0 + k // 2, 8), k % 2, dx : dx + 8].reshape(1024, CHAN))
    acc = dot(jnp.concatenate(lhs, axis=1), wmid[...])
    for r in range(2):
        x = acc[:, r * 128 : r * 128 + 128] + fa[pl.ds(p0, 8), r].astype(F32).reshape(1024, CHAN)
        x = x.reshape(8, NT, NS, CHAN)
        before, after = row_halo(x)
        for b in range(8):
            at = 2 * b + r + 1
            q, k = 4 * it + at // 4, at % 4
            sb[q, k, 1 : NT + 1] = x[b].astype(BF)
            sb[q, k, 0] = before[b].astype(BF)
            sb[q, k, NT + 1] = after[b].astype(BF)


def out_step(it, wout, sb, xh, xl):
    g0 = 4 * it
    lhs = [sb[pl.ds(g0 + k // 4, 4), k % 4].reshape(4 * XR, CHAN) for k in range(6)]
    lhs.append(xh[pl.ds(g0, 4)].reshape(4 * XR, CHAN))
    lhs.append(xl[pl.ds(g0, 4)].reshape(4 * XR, CHAN))
    acc = dot(jnp.concatenate(lhs, axis=1), wout[...])
    y0 = acc[:, :128].reshape(4, NT + 2, NS, 128)
    y1 = acc[:, 128:].reshape(4, NT + 2, NS, 128)
    centre = pltpu.roll(y0[:, 1 : NT + 1].reshape(512, 128), 64, 1).reshape(4, NT, NS, 128)
    res = y0[:, 0:NT] + centre + y1[:, 2 : NT + 2]
    res = res.reshape(4, 128, 128)
    lane = lax.broadcasted_iota(jnp.int32, (128, 128), 1)
    parts = []
    for h in range(2):
        both = jnp.where(lane < 48, res[2 * h], pltpu.roll(res[2 * h + 1], 48, 1))
        parts.append(jnp.transpose(both)[:96])
    return jnp.concatenate(parts, axis=0).astype(BF)


class CoarseRows:
    def __init__(self, shard, rows, send_sem, recv_sem):
        self.shard, self.rows = shard, rows
        self.send_sem, self.recv_sem = send_sem, recv_sem
        self.r, self.p = lax.axis_index("region"), lax.axis_index("patch")
        self.n_r, self.n_p = lax.axis_size("region"), lax.axis_size("patch")
        self.has_up, self.has_down = self.r > 0, self.r < self.n_r - 1
        self.feeds_down = (self.p == self.n_p - 1) & self.has_down
        self.feeds_up = (self.p < 5) & self.has_up

    def prepare(self, coarse_state):
        r, n_r, rows = self.r, self.n_r, self.rows
        rows[28:32] = jnp.zeros((4, 16, 256), BF)

        @pl.when(r == 0)
        def _():
            rows[0:2] = jnp.zeros((2, 16, 256), BF)

        @pl.when(r == n_r - 1)
        def _():
            rows[18:28] = jnp.zeros((10, 16, 256), BF)

        pad = jnp.zeros((16 - VARS, 256), F32)
        for c in range(2):
            self.shard[c] = jnp.concatenate([coarse_state[:, c, :], pad], axis=0).astype(BF)
        rows[pl.ds(2 + 2 * self.p, 2)] = self.shard[...]

    def greet(self):
        r, p, n_p = self.r, self.p, self.n_p
        barrier = pltpu.get_barrier_semaphore()

        def hello(to):
            pl.semaphore_signal(barrier, inc=1, device_id=to, device_id_type=MESH)

        for d in range(1, n_p):
            hello((r, (p + d) % n_p))

        @pl.when(self.has_up)
        def _():
            hello((r - 1, n_p - 1))

        @pl.when(self.has_down)
        def _():
            for k in range(5):
                hello((r + 1, k))

        count = n_p - 1 + jnp.where(self.feeds_down, n_p, 0) + jnp.where(self.feeds_up, n_p, 0)
        pl.semaphore_wait(barrier, count)

    def copy(self, row, key, k, to):
        return pltpu.make_async_remote_copy(
            src_ref=self.shard,
            dst_ref=self.rows.at[pl.ds(row, 2)],
            send_sem=self.send_sem.at[k],
            recv_sem=self.recv_sem.at[key],
            device_id=to,
            device_id_type=MESH,
        )

    def each(self, act):
        r, p, n_p = self.r, self.p, self.n_p

        @pl.when(self.feeds_down)
        def _():
            for k in range(n_p):
                act(self.copy(0, 0, 7 + k, (r + 1, k)))

        @pl.when(self.feeds_up)
        def _():
            for k in range(n_p):
                act(self.copy(18 + 2 * p, 9 + p, 15 + k, (r - 1, k)))

        for d in range(1, n_p):
            act(self.copy(2 + 2 * p, 1 + p, d - 1, (r, (p + d) % n_p)))

    def start(self):
        self.each(lambda c: c.start())

    def finish(self):
        r, p, n_p = self.r, self.p, self.n_p
        for d in range(1, n_p):
            q = (p + d) % n_p
            self.copy(2 + 2 * q, 1 + q, 0, (r, q)).wait_recv()

        @pl.when(self.has_up)
        def _():
            self.copy(0, 0, 0, (r - 1, n_p - 1)).wait_recv()

        @pl.when(self.has_down)
        def _():
            for k in range(5):
                self.copy(18 + 2 * k, 9 + k, 0, (r + 1, k)).wait_recv()

        self.each(lambda c: c.wait_send())


CHUNK = 16 * VARS
HALF = CHUNK // 2


class Sharer:
    def __init__(self, out, g, send_sem, recv_sem, tail_sem, own_sem):
        self.out, self.g = out, g
        self.send_sem, self.recv_sem = send_sem, recv_sem
        self.tail_sem, self.own_sem = tail_sem, own_sem
        p = lax.axis_index("patch")
        z, y = p // 2, p % 2
        self.me = p
        self.fore = ((z + 1) % 4) * 2 + y
        self.back = ((z + 3) % 4) * 2 + y
        self.pair = z * 2 + 1 - y
        self.far = ((z + 2) % 4) * 2 + y

    def at(self, owner, q, half=None):
        start = (owner * 16 + q) * CHUNK
        if half is None:
            return self.g.at[pl.ds(pl.multiple_of(start, CHUNK), CHUNK)]
        return self.g.at[pl.ds(pl.multiple_of(start + half * HALF, HALF), HALF)]

    def remote(self, src, dst, stream, sem, to):
        return pltpu.make_async_remote_copy(
            src_ref=src,
            dst_ref=dst,
            send_sem=self.send_sem.at[stream],
            recv_sem=sem,
            device_id={"patch": to},
            device_id_type=MESH,
        )

    def arrived(self, owner, q, stream):
        there = self.at(owner, q)
        self.remote(there, there, stream, self.recv_sem.at[stream, q], self.fore).wait_recv()

    def own(self, q):
        src = self.out.at[pl.ds(pl.multiple_of(q * CHUNK, CHUNK), CHUNK)]
        dst = self.at(self.me, q)
        self.remote(src, dst, 2, self.recv_sem.at[2, q], self.pair).start()
        self.remote(src, dst, 0, self.recv_sem.at[0, q], self.fore).start()
        self.remote(src, dst, 1, self.recv_sem.at[1, q], self.back).start()
        pltpu.make_async_copy(src, dst, self.own_sem).start()

    def first(self, q):
        self.arrived(self.pair, q, 2)
        there = self.at(self.pair, q)
        self.remote(there, there, 3, self.tail_sem.at[0], self.fore).start()
        self.remote(there, there, 4, self.tail_sem.at[1], self.back).start()
        self.arrived(self.back, q, 0)
        there = self.at(self.back, q, 0)
        self.remote(there, there, 5, self.recv_sem.at[3, q], self.fore).start()
        self.arrived(self.fore, q, 1)
        there = self.at(self.fore, q, 1)
        self.remote(there, there, 6, self.recv_sem.at[4, q], self.back).start()

    def second(self, q):
        for half in range(2):
            there = self.at(self.far, q, half)
            self.remote(there, there, 5, self.recv_sem.at[3 + half, q], self.fore).wait_recv()
            self.remote(there, there, 7 + half, self.tail_sem.at[2 + half], self.pair).start()

    def finish(self):
        whole = self.g.at[pl.ds(0, 2 * GROUP)]
        part = self.g.at[pl.ds(0, GROUP)]
        for k in range(2):
            self.remote(whole, whole, 3 + k, self.tail_sem.at[k], self.fore).wait()
            self.remote(part, part, 7 + k, self.tail_sem.at[2 + k], self.fore).wait()
            self.remote(part, part, 5 + k, self.tail_sem.at[0], self.fore).wait_send()
        for k in range(3):
            self.remote(whole, whole, k, self.tail_sem.at[0], self.fore).wait_send()
        pltpu.make_async_copy(whole, whole, self.own_sem).wait()


def pack_weights(w_in, w_mid, w_out, win, wmid, wout):
    zero = jnp.zeros((CHAN, CHAN), BF)
    for dx in range(3):
        for r in range(4):
            cols = slice(r * CHAN, r * CHAN + CHAN)
            parts = [w_in[k - r, dx] if 0 <= k - r < 3 else zero[:16] for k in range(8)]
            win[dx * 128 : dx * 128 + 128, cols] = jnp.concatenate(parts, axis=0)
        for r in range(2):
            cols = slice(r * CHAN, r * CHAN + CHAN)
            for k in range(4):
                at = (k * 3 + dx) * CHAN
                wmid[at : at + CHAN, cols] = w_mid[k - r, dx] if 0 <= k - r < 3 else zero
    for k in range(6):
        halves = []
        for h in range(2):
            parts = []
            for dx in (2 * h, 2 * h + 1):
                for r in range(4):
                    used = dx < 3 and 0 <= k - r < 3
                    parts.append(w_out[k - r, dx].astype(F32) if used else jnp.zeros((VARS, CHAN), F32))
                parts.append(jnp.zeros((16, CHAN), F32))
            halves.append(jnp.transpose(jnp.concatenate(parts, axis=0)))
        wout[k * CHAN : k * CHAN + CHAN] = jnp.concatenate(halves, axis=1).astype(BF)
    row = lax.broadcasted_iota(jnp.int32, (CHAN, 256), 0)
    col = lax.broadcasted_iota(jnp.int32, (CHAN, 256), 1) - 64
    r, v = row // 16 - 1, row % 16
    keep = (r >= 0) & (r < 4) & (v < VARS) & (col == r * VARS + v)
    ident = jnp.where(keep, 1.0, 0.0).astype(BF)
    wout[6 * CHAN : 7 * CHAN] = ident
    wout[7 * CHAN :] = ident


def patch_kernel(
    grid_size, anchors, coarse_state, w_in, b_in, gamma, beta, w_mid, w_out, g,
    shard, rows, loc, pos, win, wmid, wout, out, xh, xl, fa, nb, sb, shift, sums,
    csend_sem, crecv_sem, send_sem, recv_sem, tail_sem, own_sem,
):
    height, breadth, limit_y, limit_x = grid_size
    coarse = CoarseRows(shard, rows, csend_sem, crecv_sem)
    share = Sharer(out, g, send_sem, recv_sem, tail_sem, own_sem)
    coarse.prepare(coarse_state)
    coarse.greet()
    coarse.start()
    pack_weights(w_in, w_mid, w_out, win, wmid, wout)
    zero = jnp.zeros((NT + 2, NS, CHAN), BF)
    nb[0, 0] = zero
    nb[64, 1] = zero
    sb[0, 0] = zero
    sb[32, 1] = zero
    c0 = coarse.r * 16 - 2
    coarse.finish()

    def one_slot(slot, _):
        here = share.me * 2 + slot
        row_tables(anchors[0, here], c0, height, limit_y, loc, pos)
        hx, xpos = column_tables(anchors[1, here], breadth, limit_x)
        interp_stage(hx, xpos, rows[...].reshape(KC, 256), loc, pos, xh, xl)

        @pl.when(slot == 1)
        def _():
            share.first(6)
            share.first(7)

        first_stage(win, b_in, xh, fa, shift, sums)
        scale, offset = scale_shift(sums, shift, gamma, beta)
        norm_stage(scale, offset, fa, nb)

        def out_chunk(it):
            at = pl.multiple_of((slot * 8 + it) * CHUNK, CHUNK)
            out[pl.ds(at, CHUNK)] = out_step(it, wout, sb, xh, xl)

        mid_step(0, wmid, nb, fa, sb)
        mid_step(1, wmid, nb, fa, sb)

        def step(it, _):
            out_chunk(it - 2)
            mid_step(it, wmid, nb, fa, sb)
            q = slot * 8 + it - 2
            share.own(q)

            @pl.when(it >= 4)
            def _():
                share.first(q - 2)

            @pl.when(slot == 1)
            def _():
                share.second(it - 2)

            return 0

        lax.fori_loop(2, 8, step, 0)
        out_chunk(6)
        out_chunk(7)
        q = slot * 8 + 6
        share.own(q)
        share.own(q + 1)
        share.first(q - 2)
        share.first(q - 1)
        return 0

    lax.fori_loop(0, 2, one_slot, 0)
    share.second(6)
    share.second(7)
    share.first(14)
    share.first(15)

    def drain(q, _):
        share.second(q)
        return 0

    lax.fori_loop(8, 16, drain, 0)
    share.finish()


VM = pl.BlockSpec(memory_space=pltpu.VMEM)
SM = pl.BlockSpec(memory_space=pltpu.SMEM)


def run_patches(grid_size, anchors, coarse_state, weights):
    return pl.pallas_call(
        partial(patch_kernel, grid_size),
        out_shape=jax.ShapeDtypeStruct((16 * GROUP, 128), BF),
        in_specs=[SM] + [VM] * 7,
        out_specs=pl.BlockSpec(memory_space=pltpu.HBM),
        scratch_shapes=[
            pltpu.VMEM((2, 16, 256), BF),
            pltpu.VMEM((32, 16, 256), BF),
            pltpu.VMEM((16, 256), F32),
            pltpu.VMEM((2, 16, 256), F32),
            pltpu.VMEM((3 * 128, 4 * CHAN), BF),
            pltpu.VMEM((12 * CHAN, 2 * CHAN), BF),
            pltpu.VMEM((8 * CHAN, 256), BF),
            pltpu.VMEM((2 * GROUP, 128), BF),
            pltpu.VMEM((32, NT + 2, NS, 128), BF),
            pltpu.VMEM((32, NT + 2, NS, 128), BF),
            pltpu.VMEM((64, 2, 128, CHAN), BF),
            pltpu.VMEM((65, 2, NT + 2, NS, CHAN), BF),
            pltpu.VMEM((33, 4, NT + 2, NS, CHAN), BF),
            pltpu.VMEM((1, CHAN), F32),
            pltpu.VMEM((2, 8, CHAN), F32),
            pltpu.SemaphoreType.DMA((23,)),
            pltpu.SemaphoreType.DMA((14,)),
            pltpu.SemaphoreType.DMA((9,)),
            pltpu.SemaphoreType.DMA((5, 16)),
            pltpu.SemaphoreType.DMA((4,)),
            pltpu.SemaphoreType.DMA,
        ],
        compiler_params=pltpu.CompilerParams(
            vmem_limit_bytes=56 * 2**20, collective_id=0, has_side_effects=True
        ),
        name="patch_net",
    )(anchors, coarse_state, *weights)


class Placer:
    def __init__(self, anchors, count, blend, gathered, first, acc, cov, buf, sem):
        self.anchors, self.count, self.blend = anchors, count, blend
        self.gathered, self.first, self.acc, self.cov = gathered, first, acc, cov
        self.buf, self.sem = buf, sem
        self.top = lax.axis_index("region") * TH
        self.left = lax.axis_index("patch") * TW
        self.size = (PS - first) * VARS

    def where(self, s):
        return self.anchors[0, s] - self.top, self.anchors[1, s] - self.left

    def meets(self, s):
        dy, dx = self.where(s)
        met = (s < self.count[0]) & (dx > -PS) & (dx < TW)
        return met & (dy > 0) if self.first else met

    def fetch(self, s):
        at = pl.multiple_of(s * GROUP + self.first * VARS, 96)
        return pltpu.make_async_copy(
            self.gathered.at[pl.ds(at, self.size)], self.buf.at[s], self.sem.at[s]
        )

    def run(self):
        def start(s, _):
            @pl.when(self.meets(s))
            def _():
                self.fetch(s).start()

            return 0

        lax.fori_loop(0, 16, start, 0)
        acc, cov = self.acc, self.cov
        acc[...] = jnp.zeros_like(acc)
        cov[...] = jnp.zeros_like(cov)
        lane = lax.broadcasted_iota(jnp.int32, (128, TW), 0)
        x_at = lax.broadcasted_iota(jnp.int32, (128, TW), 1)
        shift = x_at - (lane % NS) * NT - lane // NS
        cov_y = lax.broadcasted_iota(jnp.int32, cov.shape, 0) + self.first
        cov_x = lax.broadcasted_iota(jnp.int32, cov.shape, 1)
        step = min(self.size, 768)

        def add(s, _):
            @pl.when(self.meets(s))
            def _():
                dy, dx = self.where(s)
                weight = self.blend[s].astype(F32)
                onehot = jnp.where(shift == dx, weight, 0.0).astype(BF)
                par = dy % 2
                base = ((dy - par) // 2) * 24
                inside = (cov_y >= dy) & (cov_y < dy + PS) & (cov_x >= dx) & (cov_x < dx + PS)
                cov[...] += jnp.where(inside, weight, 0.0)
                self.fetch(s).wait()
                for n in range(self.size // step):
                    y = dot(self.buf[s, n * step : n * step + step], onehot)
                    at = pl.multiple_of(base + n * step, 8)
                    for h in range(2):
                        acc[par, h, pl.ds(at, step)] += y[:, h * 128 : h * 128 + 128]

            return 0

        lax.fori_loop(0, 16, add, 0)

    def rows(self, v, h, start, n):
        even = self.acc[0, h, pl.ds(start * VARS + v, n, VARS)]
        odd = self.acc[1, h, pl.ds((start - 1) * VARS + v, n, VARS)]
        return even + odd


def place_own_kernel(anchors, count, blend, gathered, num, cover, acc, cov, buf, sem):
    placer = Placer(anchors, count, blend, gathered, 0, acc, cov, buf, sem)
    placer.run()
    half = TH // 2
    cover[...] = cov[:half]
    inverse = 1.0 / jnp.maximum(cov[half:], 1.0)
    for v in range(VARS):
        for h in range(2):
            cols = slice(h * 128, h * 128 + 128)
            num[v, half:, cols] = placer.rows(v, h, half, half) * inverse[:, cols]
            num[v, 8:half, cols] = placer.rows(v, h, 8, half - 8)
            num[v, :8, cols] = acc[0, h, pl.ds(v, 8, VARS)]
            num[v, 1:8, cols] += acc[1, h, pl.ds(v, 7, VARS)]


def finish_kernel(num, cover, low, cover_low, out):
    inverse = 1.0 / jnp.maximum(cover[...] + cover_low[0].astype(F32), 1.0)
    out[...] = (num[...] + low[...].astype(F32)) * inverse


def run_finish(num, cover, low):
    half = TH // 2
    return pl.pallas_call(
        finish_kernel,
        grid=(2,),
        out_shape=jax.ShapeDtypeStruct(num.shape, F32),
        in_specs=[
            pl.BlockSpec((VARS // 2, half, TW), lambda i: (i, 0, 0)),
            pl.BlockSpec((half, TW), lambda i: (0, 0)),
            pl.BlockSpec((VARS // 2, half, TW), lambda i: (i, 0, 0)),
            pl.BlockSpec((1, half, TW), lambda i: (VARS, 0, 0)),
        ],
        out_specs=pl.BlockSpec((VARS // 2, half, TW), lambda i: (i, 0, 0)),
        input_output_aliases={0: 0},
        name="finish",
    )(num, cover, low, low)


def place_over_kernel(anchors, count, blend, gathered, over, acc, cov, buf, sem):
    half = PS // 2
    placer = Placer(anchors, count, blend, gathered, half, acc, cov, buf, sem)
    placer.run()
    over[VARS] = cov[half:].astype(BF)
    for v in range(VARS):
        for h in range(2):
            over[v, :, h * 128 : h * 128 + 128] = placer.rows(v, h, half, half).astype(BF)


def place_call(kernel, first, cov_rows, outs, args, name):
    lines = (PS - first + TH // 2) * VARS
    size = (PS - first) * VARS
    return pl.pallas_call(
        kernel,
        out_shape=outs,
        in_specs=[SM, SM, SM, pl.BlockSpec(memory_space=pltpu.HBM)],
        out_specs=jax.tree.map(lambda _: VM, outs),
        scratch_shapes=[
            pltpu.VMEM((2, 2, lines, 128), F32),
            pltpu.VMEM((cov_rows, TW), F32),
            pltpu.VMEM((16, size, 128), BF),
            pltpu.SemaphoreType.DMA((16,)),
        ],
        compiler_params=pltpu.CompilerParams(vmem_limit_bytes=60 * 2**20),
        cost_estimate=pl.CostEstimate(flops=2 * 8 * size * 128 * 256, bytes_accessed=16 * size * 256, transcendentals=0),
        name=name,
    )(*args)


def run_place(anchors, count, blend, gathered):
    args = (anchors, count, blend, gathered)
    over_shape = jax.ShapeDtypeStruct((VARS + 1, TH // 2, TW), BF)
    own_shape = (
        jax.ShapeDtypeStruct((VARS, TH, TW), F32),
        jax.ShapeDtypeStruct((TH // 2, TW), F32),
    )
    over = place_call(place_over_kernel, PS // 2, TH, over_shape, args, "place_over")
    n = lax.axis_size("region")
    low = lax.ppermute(over, "region", [(i, i + 1) for i in range(n - 1)])
    num, cover = place_call(place_own_kernel, 0, TH, own_shape, args, "place_own")
    return num, cover, low


def per_device(coarse_state, anchors, region_count, blend, w_in, b_in, gamma, beta, w_mid, w_out):
    n_region = lax.axis_size("region")
    n_patch = lax.axis_size("patch")
    limit_y = coarse_state.shape[1] * n_region * n_patch
    limit_x = coarse_state.shape[2]
    grid_size = (TH * n_region, TW * n_patch, limit_y, limit_x)
    weights = (
        w_in,
        b_in.reshape(1, CHAN),
        gamma.reshape(1, CHAN),
        beta.reshape(1, CHAN),
        w_mid,
        w_out.transpose(0, 1, 3, 2),
    )
    places = anchors.T
    gathered = run_patches(grid_size, places, coarse_state, weights)
    num, cover, low = run_place(places, region_count, blend, gathered)
    return run_finish(num, cover, low)


def solution(mesh):
    return jax.shard_map(
        per_device,
        mesh=mesh,
        in_specs=(
            P(None, ("region", "patch"), None),
            P("region", None),
            P("region"),
            P("region"),
            P(),
            P(),
            P(),
            P(),
            P(),
            P(),
        ),
        out_specs=P(None, "region", "patch"),
        check_vma=False,
    )
```

```python
import math
from functools import partial

import jax
import jax.numpy as jnp
from jax import lax
from jax.experimental import pallas as pl
from jax.experimental.pallas import tpu as pltpu
from jax.sharding import PartitionSpec as P

VARS = 12
CHAN = 128
PS = 128
F = 8
TH = 128
TW = 256
BF = jnp.bfloat16
F32 = jnp.float32
NT, NS = 8, 16
XR = (NT + 2) * NS
KC = 512
GROUP = PS * VARS
UI, UF, UN = 4, 4, 8
LAG, LAG2 = 4, 6
LATER = {
    "tables": (("pair_on", 0, 4),),
    "interp": (("far_on", 6, 8), ("pair_on", 4, 8)),
    "first": (("second", 0, 4),),
    "norm": (("second", 4, 6),),
}
START, COUNT = 2, 2
DRAIN = (("far_on", 6, 8), ("pair_on", 0, 4), ("second", 0, 4), ("pair_on", 4, 8), ("second", 4, 8))
MESH = pl.DeviceIdType.MESH


def dot(a, b):
    return jnp.dot(a, b, preferred_element_type=F32)


def dot_nt(a, b):
    return lax.dot_general(a, b, (((1,), (1,)), ((), ())), preferred_element_type=F32)


def split(x):
    hi = x.astype(BF)
    return hi, (x - hi.astype(F32)).astype(BF)


def row_halo(x):
    rows = x.shape[0]
    s = lax.broadcasted_iota(jnp.int32, (rows, NS, CHAN), 1)
    before = jnp.where(s == 0, 0.0, pltpu.roll(x[:, NT - 1], 1, 1))
    after = jnp.where(s == NS - 1, 0.0, pltpu.roll(x[:, 0], NS - 1, 1))
    return before, after


def column_tables(anchor_x, breadth, limit):
    row = lax.broadcasted_iota(jnp.int32, (XR, 256), 0)
    d = lax.broadcasted_iota(jnp.int32, (XR, 256), 1)
    j = (row % NS) * NT + row // NS - 1
    good = (j >= 0) & (j < PS)
    x = (anchor_x + j).astype(F32)
    at = jnp.clip((x + 0.5) * (1.0 / F) - 0.5, 0.0, limit - 1.0)
    hat = jnp.maximum(0.0, 1.0 - jnp.abs(at - d.astype(F32)))
    hat = jnp.where(good, hat, 0.0).astype(BF)
    lane = d[:, :128]
    angle = x[:, :128] * (2.0 * math.pi / breadth)
    pos = jnp.where(lane == 13, jnp.sin(angle), jnp.where(lane == 14, jnp.cos(angle), 0.0))
    pos = jnp.where(lane == 12, 1.0, pos)
    pos = jnp.where(good[:, :128], pos, 0.0)
    return hat, jnp.concatenate([pos, jnp.zeros((XR, KC - 128), F32)], axis=1)


def row_tables(anchor_y, c0, height, limit, loc_ref, pos_ref):
    g = lax.broadcasted_iota(jnp.int32, (16, 256), 0)
    lane = lax.broadcasted_iota(jnp.int32, (16, 256), 1)
    k, ch = (lane % 128) // 16, lane % 16
    i = 8 * g + 4 * (lane // 128) - 1 + k
    good = (i >= 0) & (i < PS) & (k < 6)
    y = (anchor_y + i).astype(F32)
    loc = jnp.clip((y + 0.5) * (1.0 / F) - 0.5, 0.0, limit - 1.0) - c0.astype(F32)
    loc_ref[...] = jnp.where(good, loc - 14.0, -1000.0)
    angle = y * (2.0 * math.pi / height)
    pos = jnp.where(ch == 12, jnp.sin(angle), jnp.where(ch == 13, jnp.cos(angle), 0.0))
    pos_ref[0] = jnp.where(good, pos, 0.0)
    pos_ref[1] = jnp.where(good, 1.0, 0.0)


def interp_stage(hx, xpos, chi, clo, loc_ref, pos_ref, xh, xl):
    t1 = dot_nt(hx, chi[...]) + dot_nt(hx, clo[...]) + xpos
    hi, lo = split(t1)
    lhs = jnp.concatenate([hi, lo], axis=0)
    v_at = lax.broadcasted_iota(jnp.int32, (16, 256), 0)
    ch_at = lax.broadcasted_iota(jnp.int32, (16, 256), 1) % 16
    diag = jnp.where((v_at == ch_at) & (v_at < VARS), 1.0, 0.0).astype(BF)
    pick_y = jnp.where(v_at == 12, 1.0, 0.0)
    pick_x = jnp.where((v_at == 13) & (ch_at == 14) | (v_at == 14) & (ch_at == 15), 1.0, 0.0)
    one = jnp.ones((16, 256), BF)
    none = jnp.zeros((16, 256), BF)

    def step(g, _):
        loc = jnp.broadcast_to(loc_ref[pl.ds(g, 1)], (16, 256)).astype(BF)
        extra = pick_y * pos_ref[0, pl.ds(g, 1)] + pick_x * pos_ref[1, pl.ds(g, 1)]
        blocks = []
        for c in range(28):
            hat = jnp.maximum(none, one - jnp.abs(loc - BF(c - 14))) * diag
            if c == 0:
                hat = hat + extra.astype(BF)
            blocks.append(hat)
        blocks.append(jnp.zeros((64, 256), BF))
        res = dot(lhs, jnp.concatenate(blocks, axis=0))
        x = res[:XR] + res[XR:]
        for h in range(2):
            xa, xb = split(x[:, h * 128 : h * 128 + 128])
            xh[2 * g + h] = xa.reshape(NT + 2, NS, 128)
            xl[2 * g + h] = xb.reshape(NT + 2, NS, 128)
        return 0

    lax.fori_loop(0, 16, step, 0, unroll=UI)


def first_stage(win, b_in, xh, fa, shift, sums):
    bias = b_in[...]
    sums[...] = jnp.zeros_like(sums)

    def rows(at, n):
        lhs = jnp.concatenate(
            [xh[pl.ds(at, n), dx : dx + 8].reshape(n * 128, 128) for dx in range(3)], axis=1
        )
        return dot(lhs, win[...])

    sample = jnp.mean(rows(16, 1)[:, :128] + bias, axis=0, keepdims=True)
    shift[...] = sample

    def step(it, _):
        acc = rows(4 * it, 4)
        base = shift[...]
        one = jnp.zeros((8, CHAN), F32)
        two = jnp.zeros((8, CHAN), F32)
        for r in range(4):
            x = (acc[:, r * 128 : r * 128 + 128] + bias).astype(BF)
            for b in range(4):
                fa[8 * it + 2 * b + r // 2, r % 2] = x[b * 128 : b * 128 + 128]
            d = (x.astype(F32) - base).reshape(64, 8, CHAN)
            one = one + jnp.sum(d, axis=0)
            two = two + jnp.sum(d * d, axis=0)
        sums[0] += one
        sums[1] += two
        return 0

    lax.fori_loop(0, 8, step, 0, unroll=UF)


def group_mean(x):
    lane = lax.broadcasted_iota(jnp.int32, x.shape, 1)
    total = x
    for k in (1, 2):
        low = (lane // k) % 2 == 0
        total = total + jnp.where(low, pltpu.roll(total, CHAN - k, 1), pltpu.roll(total, k, 1))
    return total * 0.25


def scale_shift(sums, shift, gamma, beta):
    n = float(PS * PS)
    one = jnp.broadcast_to(jnp.sum(sums[0], axis=0, keepdims=True), (8, CHAN)) / n
    two = jnp.broadcast_to(jnp.sum(sums[1], axis=0, keepdims=True), (8, CHAN)) / n
    own_var = jnp.maximum(two - one * one, 0.0)
    mean = one + shift[...]
    g_mean = group_mean(mean)
    off = mean - g_mean
    g_var = group_mean(own_var + off * off)
    scale = gamma[...] / jnp.sqrt(g_var + 1e-05)
    return scale[0:1], (beta[...] - g_mean * scale)[0:1]


def norm_stage(scale, offset, fa, nb):
    half_scale = 0.5 * scale
    half_offset = 0.5 * offset

    def step(p, _):
        x = fa[p].astype(F32).reshape(2, NT, NS, CHAN)
        h = x * half_scale + half_offset
        y = h + h * jnp.tanh(h)
        before, after = row_halo(y)
        for r in range(2):
            at, k = (p, 1) if r == 0 else (p + 1, 0)
            nb[at, k, 1 : NT + 1] = y[r].astype(BF)
            nb[at, k, 0] = before[r].astype(BF)
            nb[at, k, NT + 1] = after[r].astype(BF)
        return 0

    lax.fori_loop(0, 64, step, 0, unroll=UN)


def mid_step(it, wmid, nb, fa, sb):
    p0 = 8 * it
    lhs = []
    for k in range(4):
        for dx in range(3):
            lhs.append(nb[pl.ds(p0 + k // 2, 8), k % 2, dx : dx + 8].reshape(1024, CHAN))
    acc = dot(jnp.concatenate(lhs, axis=1), wmid[...])
    for r in range(2):
        x = acc[:, r * 128 : r * 128 + 128] + fa[pl.ds(p0, 8), r].astype(F32).reshape(1024, CHAN)
        x = x.reshape(8, NT, NS, CHAN)
        before, after = row_halo(x)
        for b in range(8):
            at = 2 * b + r + 1
            q, k = 4 * it + at // 4, at % 4
            sb[q, k, 1 : NT + 1] = x[b].astype(BF)
            sb[q, k, 0] = before[b].astype(BF)
            sb[q, k, NT + 1] = after[b].astype(BF)


def out_step(it, wout, sb, xh, xl):
    g0 = 4 * it
    lhs = [sb[pl.ds(g0 + k // 4, 4), k % 4].reshape(4 * XR, CHAN) for k in range(6)]
    lhs.append(xh[pl.ds(g0, 4)].reshape(4 * XR, CHAN))
    lhs.append(xl[pl.ds(g0, 4)].reshape(4 * XR, CHAN))
    acc = dot(jnp.concatenate(lhs, axis=1), wout[...])
    y0 = acc[:, :128].reshape(4, NT + 2, NS, 128)
    y1 = acc[:, 128:].reshape(4, NT + 2, NS, 128)
    centre = pltpu.roll(y0[:, 1 : NT + 1].reshape(512, 128), 64, 1).reshape(4, NT, NS, 128)
    res = y0[:, 0:NT] + centre + y1[:, 2 : NT + 2]
    res = res.reshape(4, 128, 128)
    lane = lax.broadcasted_iota(jnp.int32, (128, 128), 1)
    parts = []
    for h in range(2):
        both = jnp.where(lane < 48, res[2 * h], pltpu.roll(res[2 * h + 1], 48, 1))
        parts.append(jnp.transpose(both)[:96])
    return jnp.concatenate(parts, axis=0).astype(BF)


class CoarseRows:
    def __init__(self, shard, rows, send_sem, recv_sem):
        self.shard, self.rows = shard, rows
        self.send_sem, self.recv_sem = send_sem, recv_sem
        self.r, self.p = lax.axis_index("region"), lax.axis_index("patch")
        self.n_r, self.n_p = lax.axis_size("region"), lax.axis_size("patch")
        self.has_up, self.has_down = self.r > 0, self.r < self.n_r - 1
        self.feeds_down = (self.p == self.n_p - 1) & self.has_down
        self.feeds_up = (self.p < 5) & self.has_up

    def prepare(self, coarse_state):
        r, n_r, rows = self.r, self.n_r, self.rows
        @pl.when(r == 0)
        def _():
            rows[0] = jnp.zeros((24, 256), F32)

        @pl.when(r == n_r - 1)
        def _():
            rows[9:14] = jnp.zeros((5, 24, 256), F32)

        self.shard[...] = jnp.concatenate([coarse_state[:, c, :] for c in range(2)], axis=0)
        rows[1 + self.p] = self.shard[...]

    def spread(self, hi, lo):
        pad = jnp.zeros((16 - VARS, 256), F32)
        for n in range(14):
            x = self.rows[n]
            x = jnp.concatenate([x[:VARS], pad, x[VARS:], pad], axis=0)
            hi[n * 32 : n * 32 + 32], lo[n * 32 : n * 32 + 32] = split(x)
        hi[KC - 64 :] = jnp.zeros((64, 256), BF)
        lo[KC - 64 :] = jnp.zeros((64, 256), BF)

    def greet(self):
        r, p, n_p = self.r, self.p, self.n_p
        barrier = pltpu.get_barrier_semaphore()

        def hello(to):
            pl.semaphore_signal(barrier, inc=1, device_id=to, device_id_type=MESH)

        for d in range(1, n_p):
            hello((r, (p + d) % n_p))

        @pl.when(self.has_up)
        def _():
            hello((r - 1, n_p - 1))

        @pl.when(self.has_down)
        def _():
            for k in range(5):
                hello((r + 1, k))

        count = n_p - 1 + jnp.where(self.feeds_down, n_p, 0) + jnp.where(self.feeds_up, n_p, 0)
        pl.semaphore_wait(barrier, count)

    def copy(self, row, k, to):
        return pltpu.make_async_remote_copy(
            src_ref=self.shard,
            dst_ref=self.rows.at[row],
            send_sem=self.send_sem.at[k],
            recv_sem=self.recv_sem.at[row],
            device_id=to,
            device_id_type=MESH,
        )

    def each(self, act):
        r, p, n_p = self.r, self.p, self.n_p

        @pl.when(self.feeds_down)
        def _():
            for k in range(n_p):
                act(self.copy(0, 7 + k, (r + 1, k)))

        @pl.when(self.feeds_up)
        def _():
            for k in range(n_p):
                act(self.copy(9 + p, 15 + k, (r - 1, k)))

        for d in range(1, n_p):
            act(self.copy(1 + p, d - 1, (r, (p + d) % n_p)))

    def start(self):
        self.each(lambda c: c.start())

    def finish(self):
        r, p, n_p = self.r, self.p, self.n_p
        for d in range(1, n_p):
            q = (p + d) % n_p
            self.copy(1 + q, 0, (r, q)).wait_recv()

        @pl.when(self.has_up)
        def _():
            self.copy(0, 0, (r - 1, n_p - 1)).wait_recv()

        @pl.when(self.has_down)
        def _():
            for k in range(5):
                self.copy(9 + k, 0, (r + 1, k)).wait_recv()

        self.each(lambda c: c.wait_send())


CHUNK = 16 * VARS


class Sharer:
    def __init__(self, out, g, send_sem, recv_sem, tail_sem, own_sem):
        self.out, self.g = out, g
        self.send_sem, self.recv_sem = send_sem, recv_sem
        self.tail_sem, self.own_sem = tail_sem, own_sem
        p = lax.axis_index("patch")
        z, y = p // 2, p % 2
        self.me = p
        self.fore = ((z + 1) % 4) * 2 + y
        self.back = ((z + 3) % 4) * 2 + y
        self.pair = z * 2 + 1 - y
        self.far = ((z + 2) % 4) * 2 + y

    def at(self, owner, q):
        start = pl.multiple_of((owner * 16 + q) * CHUNK, CHUNK)
        return self.g.at[pl.ds(start, CHUNK)]

    def remote(self, src, dst, stream, sem, to):
        return pltpu.make_async_remote_copy(
            src_ref=src,
            dst_ref=dst,
            send_sem=self.send_sem.at[stream],
            recv_sem=sem,
            device_id={"patch": to},
            device_id_type=MESH,
        )

    def arrived(self, owner, q, stream):
        there = self.at(owner, q)
        self.remote(there, there, stream, self.recv_sem.at[stream, q], self.fore).wait_recv()

    def own(self, slot, n):
        q = slot * 8 + n
        src = self.out.at[pl.ds(pl.multiple_of(q * CHUNK, CHUNK), CHUNK)]
        dst = self.at(self.me, q)
        even = n % 2 == 0
        fore, back = jnp.where(even, q, 16), jnp.where(even, 16, q)
        self.remote(src, dst, 2, self.recv_sem.at[2, q], self.pair).start()
        self.remote(src, dst, 0, self.recv_sem.at[0, fore], self.fore).start()
        self.remote(src, dst, 1, self.recv_sem.at[1, back], self.back).start()

    def keep(self, slot):
        src = self.out.at[pl.ds(pl.multiple_of(slot * GROUP, GROUP), GROUP)]
        dst = self.g.at[pl.ds(pl.multiple_of((self.me * 2 + slot) * GROUP, GROUP), GROUP)]
        pltpu.make_async_copy(src, dst, self.own_sem).start()

    def far_on(self, slot, n):
        q = slot * 8 + n
        odd = n % 2
        source = jnp.where(odd == 1, self.fore, self.back)
        to = jnp.where(odd == 1, self.back, self.fore)
        self.arrived(source, q, odd)
        there = self.at(source, q)
        self.remote(there, there, 5 + odd, self.recv_sem.at[3, q], to).start()

        @pl.when((n == 2) | (n == 5))
        def _():
            self.remote(there, there, 9, self.tail_sem.at[3], self.pair).start()

    def pair_on(self, slot, n):
        q = slot * 8 + n
        self.arrived(self.pair, q, 2)
        mine = self.at(self.pair, q)

        @pl.when(n != 2)
        def _():
            self.remote(mine, mine, 3, self.tail_sem.at[0], self.fore).start()

        @pl.when(n != 5)
        def _():
            self.remote(mine, mine, 4, self.tail_sem.at[1], self.back).start()

    def second(self, slot, n):
        q = slot * 8 + n
        self.arrived(self.far, q, 3)
        there = self.at(self.far, q)
        self.remote(there, there, 7, self.tail_sem.at[2], self.pair).start()

    def finish(self):
        def chunks(n):
            return self.g.at[pl.ds(0, n * CHUNK)]

        def both(stream, sem, n):
            return self.remote(chunks(n), chunks(n), stream, sem, self.fore)

        both(3, self.tail_sem.at[0], 14).wait()
        both(4, self.tail_sem.at[1], 14).wait()
        both(7, self.tail_sem.at[2], 16).wait()
        both(9, self.tail_sem.at[3], 4).wait()
        both(0, self.recv_sem.at[0, 16], 8).wait_recv()
        both(1, self.recv_sem.at[1, 16], 8).wait_recv()
        for k in range(3):
            both(k, self.tail_sem.at[0], 16).wait_send()
        both(5, self.tail_sem.at[0], 8).wait_send()
        both(6, self.tail_sem.at[0], 8).wait_send()
        pltpu.make_async_copy(chunks(16), chunks(16), self.own_sem).wait()


def pack_weights(w_in, w_mid, w_out, win, wmid, wout):
    zero = jnp.zeros((CHAN, CHAN), BF)
    for dx in range(3):
        for r in range(4):
            cols = slice(r * CHAN, r * CHAN + CHAN)
            parts = [w_in[k - r, dx] if 0 <= k - r < 3 else zero[:16] for k in range(8)]
            win[dx * 128 : dx * 128 + 128, cols] = jnp.concatenate(parts, axis=0)
        for r in range(2):
            cols = slice(r * CHAN, r * CHAN + CHAN)
            for k in range(4):
                at = (k * 3 + dx) * CHAN
                wmid[at : at + CHAN, cols] = w_mid[k - r, dx] if 0 <= k - r < 3 else zero
    for k in range(6):
        halves = []
        for h in range(2):
            parts = []
            for dx in (2 * h, 2 * h + 1):
                for r in range(4):
                    used = dx < 3 and 0 <= k - r < 3
                    parts.append(w_out[k - r, dx].astype(F32) if used else jnp.zeros((VARS, CHAN), F32))
                parts.append(jnp.zeros((16, CHAN), F32))
            halves.append(jnp.transpose(jnp.concatenate(parts, axis=0)))
        wout[k * CHAN : k * CHAN + CHAN] = jnp.concatenate(halves, axis=1).astype(BF)
    row = lax.broadcasted_iota(jnp.int32, (CHAN, 256), 0)
    col = lax.broadcasted_iota(jnp.int32, (CHAN, 256), 1) - 64
    r, v = row // 16 - 1, row % 16
    keep = (r >= 0) & (r < 4) & (v < VARS) & (col == r * VARS + v)
    ident = jnp.where(keep, 1.0, 0.0).astype(BF)
    wout[6 * CHAN : 7 * CHAN] = ident
    wout[7 * CHAN :] = ident


def patch_kernel(
    grid_size, anchors, coarse_state, w_in, b_in, gamma, beta, w_mid, w_out, g,
    shard, rows, chi, clo, loc, pos, win, wmid, wout, out, xh, xl, fa, nb, sb, shift, sums,
    csend_sem, crecv_sem, send_sem, recv_sem, tail_sem, own_sem,
):
    height, breadth, limit_y, limit_x = grid_size
    coarse = CoarseRows(shard, rows, csend_sem, crecv_sem)
    share = Sharer(out, g, send_sem, recv_sem, tail_sem, own_sem)
    coarse.prepare(coarse_state)
    coarse.greet()
    coarse.start()
    pack_weights(w_in, w_mid, w_out, win, wmid, wout)
    zero = jnp.zeros((NT + 2, NS, CHAN), BF)
    nb[0, 0] = zero
    nb[64, 1] = zero
    sb[0, 0] = zero
    sb[32, 1] = zero
    c0 = coarse.r * 16 - 2
    coarse.finish()
    coarse.spread(chi, clo)

    def hand_on(act, slot, low, high):
        def one(n, _):
            getattr(share, act)(slot, n)
            return 0

        if low < high:
            lax.fori_loop(low, high, one, 0)

    def one_slot(slot, _):
        def later(name):
            if name in LATER:

                @pl.when(slot == 1)
                def _():
                    for act, low, high in LATER[name]:
                        hand_on(act, 0, low, high)

        here = share.me * 2 + slot
        row_tables(anchors[0, here], c0, height, limit_y, loc, pos)
        hx, xpos = column_tables(anchors[1, here], breadth, limit_x)
        later("tables")
        interp_stage(hx, xpos, chi, clo, loc, pos, xh, xl)
        later("interp")
        first_stage(win, b_in, xh, fa, shift, sums)
        later("first")
        scale, offset = scale_shift(sums, shift, gamma, beta)
        norm_stage(scale, offset, fa, nb)
        later("norm")

        def out_chunk(it):
            at = pl.multiple_of((slot * 8 + it) * CHUNK, CHUNK)
            out[pl.ds(at, CHUNK)] = out_step(it, wout, sb, xh, xl)

        mid_step(0, wmid, nb, fa, sb)
        mid_step(1, wmid, nb, fa, sb)

        def step(it, _):
            out_chunk(it - 2)
            mid_step(it, wmid, nb, fa, sb)
            share.own(slot, it - 2)

            @pl.when(it >= 2 + LAG)
            def _():
                share.far_on(slot, it - 2 - LAG)

            @pl.when((slot == 1) & (it >= START) & (it < START + COUNT))
            def _():
                share.second(0, it - START + 8 - COUNT)

            @pl.when((slot == 1) & (it >= 2 + LAG2))
            def _():
                share.second(1, it - 2 - LAG2)

            return 0

        lax.fori_loop(2, 8, step, 0)
        out_chunk(6)
        out_chunk(7)
        share.own(slot, 6)
        share.own(slot, 7)
        hand_on("far_on", slot, 6 - LAG, 6)
        share.keep(slot)
        return 0

    lax.fori_loop(0, 2, one_slot, 0)
    for act, low, high in DRAIN:
        hand_on(act, 1, low, high)
    share.finish()


VM = pl.BlockSpec(memory_space=pltpu.VMEM)
SM = pl.BlockSpec(memory_space=pltpu.SMEM)


def run_patches(grid_size, anchors, coarse_state, weights):
    return pl.pallas_call(
        partial(patch_kernel, grid_size),
        out_shape=jax.ShapeDtypeStruct((16 * GROUP, 128), BF),
        in_specs=[SM] + [VM] * 7,
        out_specs=pl.BlockSpec(memory_space=pltpu.HBM),
        scratch_shapes=[
            pltpu.VMEM((24, 256), F32),
            pltpu.VMEM((14, 24, 256), F32),
            pltpu.VMEM((KC, 256), BF),
            pltpu.VMEM((KC, 256), BF),
            pltpu.VMEM((16, 256), F32),
            pltpu.VMEM((2, 16, 256), F32),
            pltpu.VMEM((3 * 128, 4 * CHAN), BF),
            pltpu.VMEM((12 * CHAN, 2 * CHAN), BF),
            pltpu.VMEM((8 * CHAN, 256), BF),
            pltpu.VMEM((2 * GROUP, 128), BF),
            pltpu.VMEM((32, NT + 2, NS, 128), BF),
            pltpu.VMEM((32, NT + 2, NS, 128), BF),
            pltpu.VMEM((64, 2, 128, CHAN), BF),
            pltpu.VMEM((65, 2, NT + 2, NS, CHAN), BF),
            pltpu.VMEM((33, 4, NT + 2, NS, CHAN), BF),
            pltpu.VMEM((1, CHAN), F32),
            pltpu.VMEM((2, 8, CHAN), F32),
            pltpu.SemaphoreType.DMA((23,)),
            pltpu.SemaphoreType.DMA((14,)),
            pltpu.SemaphoreType.DMA((10,)),
            pltpu.SemaphoreType.DMA((4, 17)),
            pltpu.SemaphoreType.DMA((4,)),
            pltpu.SemaphoreType.DMA,
        ],
        compiler_params=pltpu.CompilerParams(
            vmem_limit_bytes=56 * 2**20, collective_id=0, has_side_effects=True
        ),
        name="patch_net",
    )(anchors, coarse_state, *weights)


class Placer:
    def __init__(self, anchors, count, blend, gathered, first, acc, cov, buf, sem):
        self.anchors, self.count, self.blend = anchors, count, blend
        self.gathered, self.first, self.acc, self.cov = gathered, first, acc, cov
        self.buf, self.sem = buf, sem
        self.top = lax.axis_index("region") * TH
        self.left = lax.axis_index("patch") * TW
        self.size = (PS - first) * VARS

    def where(self, s):
        return self.anchors[0, s] - self.top, self.anchors[1, s] - self.left

    def meets(self, s):
        dy, dx = self.where(s)
        met = (s < self.count[0]) & (dx > -PS) & (dx < TW)
        return met & (dy > 0) if self.first else met

    def fetch(self, s):
        at = pl.multiple_of(s * GROUP + self.first * VARS, 96)
        return pltpu.make_async_copy(
            self.gathered.at[pl.ds(at, self.size)], self.buf.at[s], self.sem.at[s]
        )

    def run(self):
        def start(s, _):
            @pl.when(self.meets(s))
            def _():
                self.fetch(s).start()

            return 0

        lax.fori_loop(0, 16, start, 0)
        acc, cov = self.acc, self.cov
        acc[...] = jnp.zeros_like(acc)
        cov[...] = jnp.zeros_like(cov)
        lane = lax.broadcasted_iota(jnp.int32, (128, TW), 0)
        x_at = lax.broadcasted_iota(jnp.int32, (128, TW), 1)
        shift = x_at - (lane % NS) * NT - lane // NS
        cov_y = lax.broadcasted_iota(jnp.int32, cov.shape, 0) + self.first
        cov_x = lax.broadcasted_iota(jnp.int32, cov.shape, 1)
        step = min(self.size, 768)

        def add(s, _):
            @pl.when(self.meets(s))
            def _():
                dy, dx = self.where(s)
                weight = self.blend[s].astype(F32)
                onehot = jnp.where(shift == dx, weight, 0.0).astype(BF)
                par = dy % 2
                base = ((dy - par) // 2) * 24
                inside = (cov_y >= dy) & (cov_y < dy + PS) & (cov_x >= dx) & (cov_x < dx + PS)
                cov[...] += jnp.where(inside, weight, 0.0)
                self.fetch(s).wait()
                for n in range(self.size // step):
                    y = dot(self.buf[s, n * step : n * step + step], onehot)
                    at = pl.multiple_of(base + n * step, 8)
                    for h in range(2):
                        acc[par, h, pl.ds(at, step)] += y[:, h * 128 : h * 128 + 128]

            return 0

        lax.fori_loop(0, 16, add, 0)

    def rows(self, v, h, start, n):
        even = self.acc[0, h, pl.ds(start * VARS + v, n, VARS)]
        odd = self.acc[1, h, pl.ds((start - 1) * VARS + v, n, VARS)]
        return even + odd


def place_own_kernel(anchors, count, blend, gathered, num, cover, acc, cov, buf, sem):
    placer = Placer(anchors, count, blend, gathered, 0, acc, cov, buf, sem)
    placer.run()
    half = TH // 2
    cover[...] = cov[:half]
    inverse = 1.0 / jnp.maximum(cov[half:], 1.0)
    for v in range(VARS):
        for h in range(2):
            cols = slice(h * 128, h * 128 + 128)
            num[v, half:, cols] = placer.rows(v, h, half, half) * inverse[:, cols]
            num[v, 8:half, cols] = placer.rows(v, h, 8, half - 8)
            num[v, :8, cols] = acc[0, h, pl.ds(v, 8, VARS)]
            num[v, 1:8, cols] += acc[1, h, pl.ds(v, 7, VARS)]


def finish_kernel(num, cover, low, cover_low, out):
    inverse = 1.0 / jnp.maximum(cover[...] + cover_low[0].astype(F32), 1.0)
    out[...] = (num[...] + low[...].astype(F32)) * inverse


def run_finish(num, cover, low):
    half = TH // 2
    return pl.pallas_call(
        finish_kernel,
        grid=(2,),
        out_shape=jax.ShapeDtypeStruct(num.shape, F32),
        in_specs=[
            pl.BlockSpec((VARS // 2, half, TW), lambda i: (i, 0, 0)),
            pl.BlockSpec((half, TW), lambda i: (0, 0)),
            pl.BlockSpec((VARS // 2, half, TW), lambda i: (i, 0, 0)),
            pl.BlockSpec((1, half, TW), lambda i: (VARS, 0, 0)),
        ],
        out_specs=pl.BlockSpec((VARS // 2, half, TW), lambda i: (i, 0, 0)),
        input_output_aliases={0: 0},
        name="finish",
    )(num, cover, low, low)


def place_over_kernel(anchors, count, blend, gathered, over, acc, cov, buf, sem):
    half = PS // 2
    placer = Placer(anchors, count, blend, gathered, half, acc, cov, buf, sem)
    placer.run()
    over[VARS] = cov[half:].astype(BF)
    for v in range(VARS):
        for h in range(2):
            over[v, :, h * 128 : h * 128 + 128] = placer.rows(v, h, half, half).astype(BF)


def place_call(kernel, first, cov_rows, outs, args, name):
    lines = (PS - first + TH // 2) * VARS
    size = (PS - first) * VARS
    return pl.pallas_call(
        kernel,
        out_shape=outs,
        in_specs=[SM, SM, SM, pl.BlockSpec(memory_space=pltpu.HBM)],
        out_specs=jax.tree.map(lambda _: VM, outs),
        scratch_shapes=[
            pltpu.VMEM((2, 2, lines, 128), F32),
            pltpu.VMEM((cov_rows, TW), F32),
            pltpu.VMEM((16, size, 128), BF),
            pltpu.SemaphoreType.DMA((16,)),
        ],
        compiler_params=pltpu.CompilerParams(vmem_limit_bytes=60 * 2**20),
        cost_estimate=pl.CostEstimate(flops=2 * 8 * size * 128 * 256, bytes_accessed=16 * size * 256, transcendentals=0),
        name=name,
    )(*args)


def run_place(anchors, count, blend, gathered):
    args = (anchors, count, blend, gathered)
    over_shape = jax.ShapeDtypeStruct((VARS + 1, TH // 2, TW), BF)
    own_shape = (
        jax.ShapeDtypeStruct((VARS, TH, TW), F32),
        jax.ShapeDtypeStruct((TH // 2, TW), F32),
    )
    over = place_call(place_over_kernel, PS // 2, TH, over_shape, args, "place_over")
    n = lax.axis_size("region")
    low = lax.ppermute(over, "region", [(i, i + 1) for i in range(n - 1)])
    num, cover = place_call(place_own_kernel, 0, TH, own_shape, args, "place_own")
    return num, cover, low


def per_device(coarse_state, anchors, region_count, blend, w_in, b_in, gamma, beta, w_mid, w_out):
    n_region = lax.axis_size("region")
    n_patch = lax.axis_size("patch")
    limit_y = coarse_state.shape[1] * n_region * n_patch
    limit_x = coarse_state.shape[2]
    grid_size = (TH * n_region, TW * n_patch, limit_y, limit_x)
    weights = (
        w_in,
        b_in.reshape(1, CHAN),
        gamma.reshape(1, CHAN),
        beta.reshape(1, CHAN),
        w_mid,
        w_out.transpose(0, 1, 3, 2),
    )
    places = anchors.T
    gathered = run_patches(grid_size, places, coarse_state, weights)
    num, cover, low = run_place(places, region_count, blend, gathered)
    return run_finish(num, cover, low)


def solution(mesh):
    return jax.shard_map(
        per_device,
        mesh=mesh,
        in_specs=(
            P(None, ("region", "patch"), None),
            P("region", None),
            P("region"),
            P("region"),
            P(),
            P(),
            P(),
            P(),
            P(),
            P(),
        ),
        out_specs=P(None, "region", "patch"),
        check_vma=False,
    )
```

```python
import math
from functools import partial

import jax
import jax.numpy as jnp
from jax import lax
from jax.experimental import pallas as pl
from jax.experimental.pallas import tpu as pltpu
from jax.sharding import PartitionSpec as P

VARS = 12
CHAN = 128
PS = 128
F = 8
TH = 128
TW = 256
BF = jnp.bfloat16
F32 = jnp.float32
NT, NS = 8, 16
XR = (NT + 2) * NS
KC = 512
GROUP = PS * VARS
UI, UF, UN = 8, 8, 16
FINISH = 2
LAG, LAG2 = 4, 6
LATER = {
    "tables": (("pair_on", 0, 4),),
    "interp": (("far_on", 6, 8), ("pair_on", 4, 8)),
    "first": (("second", 0, 4),),
    "norm": (("second", 4, 6),),
}
START, COUNT = 2, 2
DRAIN = (("far_on", 6, 8), ("pair_on", 0, 4), ("second", 0, 4), ("pair_on", 4, 8), ("second", 4, 8))
MESH = pl.DeviceIdType.MESH


def dot(a, b):
    return jnp.dot(a, b, preferred_element_type=F32)


def dot_nt(a, b):
    return lax.dot_general(a, b, (((1,), (1,)), ((), ())), preferred_element_type=F32)


def split(x):
    hi = x.astype(BF)
    return hi, (x - hi.astype(F32)).astype(BF)


def row_halo(x):
    rows = x.shape[0]
    s = lax.broadcasted_iota(jnp.int32, (rows, NS, CHAN), 1)
    before = jnp.where(s == 0, 0.0, pltpu.roll(x[:, NT - 1], 1, 1))
    after = jnp.where(s == NS - 1, 0.0, pltpu.roll(x[:, 0], NS - 1, 1))
    return before, after


def column_tables(anchor_x, breadth, limit):
    row = lax.broadcasted_iota(jnp.int32, (XR, 256), 0)
    d = lax.broadcasted_iota(jnp.int32, (XR, 256), 1)
    j = (row % NS) * NT + row // NS - 1
    good = (j >= 0) & (j < PS)
    x = (anchor_x + j).astype(F32)
    at = jnp.clip((x + 0.5) * (1.0 / F) - 0.5, 0.0, limit - 1.0)
    hat = jnp.maximum(0.0, 1.0 - jnp.abs(at - d.astype(F32)))
    hat = jnp.where(good, hat, 0.0).astype(BF)
    lane = d[:, :128]
    angle = x[:, :128] * (2.0 * math.pi / breadth)
    pos = jnp.where(lane == 13, jnp.sin(angle), jnp.where(lane == 14, jnp.cos(angle), 0.0))
    pos = jnp.where(lane == 12, 1.0, pos)
    pos = jnp.where(good[:, :128], pos, 0.0)
    return hat, pos


def row_tables(anchor_y, c0, height, limit, loc_ref, pos_ref):
    g = lax.broadcasted_iota(jnp.int32, (16, 256), 0)
    lane = lax.broadcasted_iota(jnp.int32, (16, 256), 1)
    k, ch = (lane % 128) // 16, lane % 16
    i = 8 * g + 4 * (lane // 128) - 1 + k
    good = (i >= 0) & (i < PS) & (k < 6)
    y = (anchor_y + i).astype(F32)
    loc = jnp.clip((y + 0.5) * (1.0 / F) - 0.5, 0.0, limit - 1.0) - c0.astype(F32)
    loc_ref[...] = jnp.where(good, loc - 14.0, -1000.0)
    angle = y * (2.0 * math.pi / height)
    pos = jnp.where(ch == 12, jnp.sin(angle), jnp.where(ch == 13, jnp.cos(angle), 0.0))
    pos_ref[0] = jnp.where(good, pos, 0.0)
    pos_ref[1] = jnp.where(good, 1.0, 0.0)


def interp_stage(hx, xpos, chi, clo, loc_ref, pos_ref, xh, xl):
    t1 = dot_nt(hx, chi[...]) + dot_nt(hx, clo[...])
    t1 = jnp.concatenate([t1[:, :128] + xpos, t1[:, 128:]], axis=1)
    hi, lo = split(t1)
    lhs = jnp.concatenate([hi, lo], axis=0)
    v_at = lax.broadcasted_iota(jnp.int32, (16, 256), 0)
    ch_at = lax.broadcasted_iota(jnp.int32, (16, 256), 1) % 16
    diag = jnp.where((v_at == ch_at) & (v_at < VARS), 1.0, 0.0).astype(BF)
    pick_y = jnp.where(v_at == 12, 1.0, 0.0)
    pick_x = jnp.where((v_at == 13) & (ch_at == 14) | (v_at == 14) & (ch_at == 15), 1.0, 0.0)
    one = jnp.ones((16, 256), BF)
    none = jnp.zeros((16, 256), BF)

    def step(g, _):
        loc = jnp.broadcast_to(loc_ref[pl.ds(g, 1)], (16, 256)).astype(BF)
        extra = pick_y * pos_ref[0, pl.ds(g, 1)] + pick_x * pos_ref[1, pl.ds(g, 1)]
        blocks = []
        for c in range(28):
            hat = jnp.maximum(none, one - jnp.abs(loc - BF(c - 14))) * diag
            if c == 0:
                hat = hat + extra.astype(BF)
            blocks.append(hat)
        blocks.append(jnp.zeros((64, 256), BF))
        res = dot(lhs, jnp.concatenate(blocks, axis=0))
        x = res[:XR] + res[XR:]
        for h in range(2):
            xa, xb = split(x[:, h * 128 : h * 128 + 128])
            xh[2 * g + h] = xa.reshape(NT + 2, NS, 128)
            xl[2 * g + h] = xb.reshape(NT + 2, NS, 128)
        return 0

    lax.fori_loop(0, 16, step, 0, unroll=UI)


def first_stage(win, b_in, xh, fa, shift, sums):
    bias = b_in[...]
    sums[...] = jnp.zeros_like(sums)

    def rows(at, n):
        lhs = jnp.concatenate(
            [xh[pl.ds(at, n), dx : dx + 8].reshape(n * 128, 128) for dx in range(3)], axis=1
        )
        return dot(lhs, win[...])

    sample = jnp.mean(rows(16, 1)[:, :128] + bias, axis=0, keepdims=True)
    shift[...] = sample

    def step(it, _):
        acc = rows(4 * it, 4)
        base = shift[...]
        one = jnp.zeros((8, CHAN), F32)
        two = jnp.zeros((8, CHAN), F32)
        for r in range(4):
            x = (acc[:, r * 128 : r * 128 + 128] + bias).astype(BF)
            for b in range(4):
                fa[8 * it + 2 * b + r // 2, r % 2] = x[b * 128 : b * 128 + 128]
            d = (x.astype(F32) - base).reshape(64, 8, CHAN)
            one = one + jnp.sum(d, axis=0)
            two = two + jnp.sum(d * d, axis=0)
        sums[0] += one
        sums[1] += two
        return 0

    lax.fori_loop(0, 8, step, 0, unroll=UF)


def group_mean(x):
    lane = lax.broadcasted_iota(jnp.int32, x.shape, 1)
    total = x
    for k in (1, 2):
        low = (lane // k) % 2 == 0
        total = total + jnp.where(low, pltpu.roll(total, CHAN - k, 1), pltpu.roll(total, k, 1))
    return total * 0.25


def scale_shift(sums, shift, gamma, beta):
    n = float(PS * PS)
    one = jnp.broadcast_to(jnp.sum(sums[0], axis=0, keepdims=True), (8, CHAN)) / n
    two = jnp.broadcast_to(jnp.sum(sums[1], axis=0, keepdims=True), (8, CHAN)) / n
    own_var = jnp.maximum(two - one * one, 0.0)
    mean = one + shift[...]
    g_mean = group_mean(mean)
    off = mean - g_mean
    g_var = group_mean(own_var + off * off)
    scale = gamma[...] / jnp.sqrt(g_var + 1e-05)
    return scale[0:1], (beta[...] - g_mean * scale)[0:1]


def norm_stage(scale, offset, fa, nb):
    half_scale = 0.5 * scale
    half_offset = 0.5 * offset

    def step(p, _):
        x = fa[p].astype(F32).reshape(2, NT, NS, CHAN)
        h = x * half_scale + half_offset
        y = h + h * jnp.tanh(h)
        before, after = row_halo(y)
        for r in range(2):
            at, k = (p, 1) if r == 0 else (p + 1, 0)
            nb[at, k, 1 : NT + 1] = y[r].astype(BF)
            nb[at, k, 0] = before[r].astype(BF)
            nb[at, k, NT + 1] = after[r].astype(BF)
        return 0

    lax.fori_loop(0, 64, step, 0, unroll=UN)


def mid_step(it, wmid, nb, fa, sb):
    p0 = 8 * it
    lhs = []
    for k in range(4):
        for dx in range(3):
            lhs.append(nb[pl.ds(p0 + k // 2, 8), k % 2, dx : dx + 8].reshape(1024, CHAN))
    acc = dot(jnp.concatenate(lhs, axis=1), wmid[...])
    for r in range(2):
        x = acc[:, r * 128 : r * 128 + 128] + fa[pl.ds(p0, 8), r].astype(F32).reshape(1024, CHAN)
        x = x.reshape(8, NT, NS, CHAN)
        before, after = row_halo(x)
        for b in range(8):
            at = 2 * b + r + 1
            q, k = 4 * it + at // 4, at % 4
            sb[q, k, 1 : NT + 1] = x[b].astype(BF)
            sb[q, k, 0] = before[b].astype(BF)
            sb[q, k, NT + 1] = after[b].astype(BF)


def out_step(it, wout, sb, xh, xl):
    g0 = 4 * it
    lhs = [sb[pl.ds(g0 + k // 4, 4), k % 4].reshape(4 * XR, CHAN) for k in range(6)]
    lhs.append(xh[pl.ds(g0, 4)].reshape(4 * XR, CHAN))
    lhs.append(xl[pl.ds(g0, 4)].reshape(4 * XR, CHAN))
    acc = dot(jnp.concatenate(lhs, axis=1), wout[...])
    y0 = acc[:, :128].reshape(4, NT + 2, NS, 128)
    y1 = acc[:, 128:].reshape(4, NT + 2, NS, 128)
    centre = pltpu.roll(y0[:, 1 : NT + 1].reshape(512, 128), 64, 1).reshape(4, NT, NS, 128)
    res = y0[:, 0:NT] + centre + y1[:, 2 : NT + 2]
    res = res.reshape(4, 128, 128)
    lane = lax.broadcasted_iota(jnp.int32, (128, 128), 1)
    parts = []
    for h in range(2):
        both = jnp.where(lane < 48, res[2 * h], pltpu.roll(res[2 * h + 1], 48, 1))
        parts.append(jnp.transpose(both)[:96])
    return jnp.concatenate(parts, axis=0).astype(BF)


class CoarseRows:
    def __init__(self, shard, rows, send_sem, recv_sem):
        self.shard, self.rows = shard, rows
        self.send_sem, self.recv_sem = send_sem, recv_sem
        self.r, self.p = lax.axis_index("region"), lax.axis_index("patch")
        self.n_r, self.n_p = lax.axis_size("region"), lax.axis_size("patch")
        self.has_up, self.has_down = self.r > 0, self.r < self.n_r - 1
        self.feeds_down = (self.p == self.n_p - 1) & self.has_down
        self.feeds_up = (self.p < 5) & self.has_up

    def prepare(self, coarse_state):
        r, n_r, rows = self.r, self.n_r, self.rows
        @pl.when(r == 0)
        def _():
            rows[0] = jnp.zeros((24, 256), F32)

        @pl.when(r == n_r - 1)
        def _():
            rows[9:14] = jnp.zeros((5, 24, 256), F32)

        self.shard[...] = jnp.concatenate([coarse_state[:, c, :] for c in range(2)], axis=0)
        rows[1 + self.p] = self.shard[...]

    def spread(self, hi, lo):
        pad = jnp.zeros((16 - VARS, 256), F32)
        for n in range(14):
            x = self.rows[n]
            x = jnp.concatenate([x[:VARS], pad, x[VARS:], pad], axis=0)
            hi[n * 32 : n * 32 + 32], lo[n * 32 : n * 32 + 32] = split(x)
        hi[KC - 64 :] = jnp.zeros((64, 256), BF)
        lo[KC - 64 :] = jnp.zeros((64, 256), BF)

    def greet(self):
        r, p, n_p = self.r, self.p, self.n_p
        barrier = pltpu.get_barrier_semaphore()

        def hello(to):
            pl.semaphore_signal(barrier, inc=1, device_id=to, device_id_type=MESH)

        for d in range(1, n_p):
            hello((r, (p + d) % n_p))

        @pl.when(self.has_up)
        def _():
            hello((r - 1, n_p - 1))

        @pl.when(self.has_down)
        def _():
            for k in range(5):
                hello((r + 1, k))

        count = n_p - 1 + jnp.where(self.feeds_down, n_p, 0) + jnp.where(self.feeds_up, n_p, 0)
        pl.semaphore_wait(barrier, count)

    def copy(self, row, k, to):
        return pltpu.make_async_remote_copy(
            src_ref=self.shard,
            dst_ref=self.rows.at[row],
            send_sem=self.send_sem.at[k],
            recv_sem=self.recv_sem.at[row],
            device_id=to,
            device_id_type=MESH,
        )

    def each(self, act):
        r, p, n_p = self.r, self.p, self.n_p

        @pl.when(self.feeds_down)
        def _():
            for k in range(n_p):
                act(self.copy(0, 7 + k, (r + 1, k)))

        @pl.when(self.feeds_up)
        def _():
            for k in range(n_p):
                act(self.copy(9 + p, 15 + k, (r - 1, k)))

        for d in range(1, n_p):
            act(self.copy(1 + p, d - 1, (r, (p + d) % n_p)))

    def start(self):
        self.each(lambda c: c.start())

    def finish(self):
        r, p, n_p = self.r, self.p, self.n_p
        for d in range(1, n_p):
            q = (p + d) % n_p
            self.copy(1 + q, 0, (r, q)).wait_recv()

        @pl.when(self.has_up)
        def _():
            self.copy(0, 0, (r - 1, n_p - 1)).wait_recv()

        @pl.when(self.has_down)
        def _():
            for k in range(5):
                self.copy(9 + k, 0, (r + 1, k)).wait_recv()

        self.each(lambda c: c.wait_send())


CHUNK = 16 * VARS


class Sharer:
    def __init__(self, out, g, send_sem, recv_sem, tail_sem, own_sem):
        self.out, self.g = out, g
        self.send_sem, self.recv_sem = send_sem, recv_sem
        self.tail_sem, self.own_sem = tail_sem, own_sem
        p = lax.axis_index("patch")
        z, y = p // 2, p % 2
        self.me = p
        self.fore = ((z + 1) % 4) * 2 + y
        self.back = ((z + 3) % 4) * 2 + y
        self.pair = z * 2 + 1 - y
        self.far = ((z + 2) % 4) * 2 + y

    def at(self, owner, q):
        start = pl.multiple_of((owner * 16 + q) * CHUNK, CHUNK)
        return self.g.at[pl.ds(start, CHUNK)]

    def remote(self, src, dst, stream, sem, to):
        return pltpu.make_async_remote_copy(
            src_ref=src,
            dst_ref=dst,
            send_sem=self.send_sem.at[stream],
            recv_sem=sem,
            device_id={"patch": to},
            device_id_type=MESH,
        )

    def arrived(self, owner, q, stream):
        there = self.at(owner, q)
        self.remote(there, there, stream, self.recv_sem.at[stream, q], self.fore).wait_recv()

    def own(self, slot, n):
        q = slot * 8 + n
        src = self.out.at[pl.ds(pl.multiple_of(q * CHUNK, CHUNK), CHUNK)]
        dst = self.at(self.me, q)
        even = n % 2 == 0
        fore, back = jnp.where(even, q, 16), jnp.where(even, 16, q)
        self.remote(src, dst, 2, self.recv_sem.at[2, q], self.pair).start()
        self.remote(src, dst, 0, self.recv_sem.at[0, fore], self.fore).start()
        self.remote(src, dst, 1, self.recv_sem.at[1, back], self.back).start()

    def keep(self, slot):
        src = self.out.at[pl.ds(pl.multiple_of(slot * GROUP, GROUP), GROUP)]
        dst = self.g.at[pl.ds(pl.multiple_of((self.me * 2 + slot) * GROUP, GROUP), GROUP)]
        pltpu.make_async_copy(src, dst, self.own_sem).start()

    def far_on(self, slot, n):
        q = slot * 8 + n
        odd = n % 2
        source = jnp.where(odd == 1, self.fore, self.back)
        to = jnp.where(odd == 1, self.back, self.fore)
        self.arrived(source, q, odd)
        there = self.at(source, q)
        self.remote(there, there, 5 + odd, self.recv_sem.at[3, q], to).start()

        @pl.when((n == 2) | (n == 5))
        def _():
            self.remote(there, there, 9, self.tail_sem.at[3], self.pair).start()

    def pair_on(self, slot, n):
        q = slot * 8 + n
        self.arrived(self.pair, q, 2)
        mine = self.at(self.pair, q)

        @pl.when(n != 2)
        def _():
            self.remote(mine, mine, 3, self.tail_sem.at[0], self.fore).start()

        @pl.when(n != 5)
        def _():
            self.remote(mine, mine, 4, self.tail_sem.at[1], self.back).start()

    def second(self, slot, n):
        q = slot * 8 + n
        self.arrived(self.far, q, 3)
        there = self.at(self.far, q)
        self.remote(there, there, 7, self.tail_sem.at[2], self.pair).start()

    def finish(self):
        def chunks(n):
            return self.g.at[pl.ds(0, n * CHUNK)]

        def both(stream, sem, n):
            return self.remote(chunks(n), chunks(n), stream, sem, self.fore)

        both(3, self.tail_sem.at[0], 14).wait()
        both(4, self.tail_sem.at[1], 14).wait()
        both(7, self.tail_sem.at[2], 16).wait()
        both(9, self.tail_sem.at[3], 4).wait()
        both(0, self.recv_sem.at[0, 16], 8).wait_recv()
        both(1, self.recv_sem.at[1, 16], 8).wait_recv()
        for k in range(3):
            both(k, self.tail_sem.at[0], 16).wait_send()
        both(5, self.tail_sem.at[0], 8).wait_send()
        both(6, self.tail_sem.at[0], 8).wait_send()
        pltpu.make_async_copy(chunks(16), chunks(16), self.own_sem).wait()


def pack_weights(w_in, w_mid, w_out, win, wmid, wout):
    zero = jnp.zeros((CHAN, CHAN), BF)
    for dx in range(3):
        for r in range(4):
            cols = slice(r * CHAN, r * CHAN + CHAN)
            parts = [w_in[k - r, dx] if 0 <= k - r < 3 else zero[:16] for k in range(8)]
            win[dx * 128 : dx * 128 + 128, cols] = jnp.concatenate(parts, axis=0)
        for r in range(2):
            cols = slice(r * CHAN, r * CHAN + CHAN)
            for k in range(4):
                at = (k * 3 + dx) * CHAN
                wmid[at : at + CHAN, cols] = w_mid[k - r, dx] if 0 <= k - r < 3 else zero
    for k in range(6):
        halves = []
        for h in range(2):
            parts = []
            for dx in (2 * h, 2 * h + 1):
                for r in range(4):
                    used = dx < 3 and 0 <= k - r < 3
                    parts.append(w_out[k - r, dx].astype(F32) if used else jnp.zeros((VARS, CHAN), F32))
                parts.append(jnp.zeros((16, CHAN), F32))
            halves.append(jnp.transpose(jnp.concatenate(parts, axis=0)))
        wout[k * CHAN : k * CHAN + CHAN] = jnp.concatenate(halves, axis=1).astype(BF)
    row = lax.broadcasted_iota(jnp.int32, (CHAN, 256), 0)
    col = lax.broadcasted_iota(jnp.int32, (CHAN, 256), 1) - 64
    r, v = row // 16 - 1, row % 16
    keep = (r >= 0) & (r < 4) & (v < VARS) & (col == r * VARS + v)
    ident = jnp.where(keep, 1.0, 0.0).astype(BF)
    wout[6 * CHAN : 7 * CHAN] = ident
    wout[7 * CHAN :] = ident


def patch_kernel(
    grid_size, anchors, coarse_state, w_in, b_in, gamma, beta, w_mid, w_out, g,
    shard, rows, chi, clo, hx, xpos, loc, pos, win, wmid, wout, out, xh, xl, fa, nb, sb, shift, sums,
    csend_sem, crecv_sem, send_sem, recv_sem, tail_sem, own_sem,
):
    height, breadth, limit_y, limit_x = grid_size
    coarse = CoarseRows(shard, rows, csend_sem, crecv_sem)
    share = Sharer(out, g, send_sem, recv_sem, tail_sem, own_sem)
    coarse.prepare(coarse_state)
    coarse.greet()
    coarse.start()
    pack_weights(w_in, w_mid, w_out, win, wmid, wout)
    zero = jnp.zeros((NT + 2, NS, CHAN), BF)
    nb[0, 0] = zero
    nb[64, 1] = zero
    sb[0, 0] = zero
    sb[32, 1] = zero
    c0 = coarse.r * 16 - 2

    def tables(slot, _):
        here = share.me * 2 + slot
        row_tables(anchors[0, here], c0, height, limit_y, loc.at[slot], pos.at[slot])
        hx[slot], xpos[slot] = column_tables(anchors[1, here], breadth, limit_x)
        return 0

    lax.fori_loop(0, 2, tables, 0)
    coarse.finish()
    coarse.spread(chi, clo)

    def hand_on(act, slot, low, high):
        def one(n, _):
            getattr(share, act)(slot, n)
            return 0

        if low < high:
            lax.fori_loop(low, high, one, 0)

    def one_slot(slot, _):
        def later(name):
            if name in LATER:

                @pl.when(slot == 1)
                def _():
                    for act, low, high in LATER[name]:
                        hand_on(act, 0, low, high)

        later("tables")
        interp_stage(hx[slot], xpos[slot], chi, clo, loc.at[slot], pos.at[slot], xh, xl)
        later("interp")
        first_stage(win, b_in, xh, fa, shift, sums)
        later("first")
        scale, offset = scale_shift(sums, shift, gamma, beta)
        norm_stage(scale, offset, fa, nb)
        later("norm")

        def out_chunk(it):
            at = pl.multiple_of((slot * 8 + it) * CHUNK, CHUNK)
            out[pl.ds(at, CHUNK)] = out_step(it, wout, sb, xh, xl)

        mid_step(0, wmid, nb, fa, sb)
        mid_step(1, wmid, nb, fa, sb)

        def step(it, _):
            out_chunk(it - 2)
            mid_step(it, wmid, nb, fa, sb)
            share.own(slot, it - 2)

            @pl.when(it >= 2 + LAG)
            def _():
                share.far_on(slot, it - 2 - LAG)

            @pl.when((slot == 1) & (it >= START) & (it < START + COUNT))
            def _():
                share.second(0, it - START + 8 - COUNT)

            @pl.when((slot == 1) & (it >= 2 + LAG2))
            def _():
                share.second(1, it - 2 - LAG2)

            return 0

        lax.fori_loop(2, 8, step, 0)
        out_chunk(6)
        out_chunk(7)
        share.own(slot, 6)
        share.own(slot, 7)
        hand_on("far_on", slot, 6 - LAG, 6)
        share.keep(slot)
        return 0

    lax.fori_loop(0, 2, one_slot, 0)
    for act, low, high in DRAIN:
        hand_on(act, 1, low, high)
    share.finish()


VM = pl.BlockSpec(memory_space=pltpu.VMEM)
SM = pl.BlockSpec(memory_space=pltpu.SMEM)


def run_patches(grid_size, anchors, coarse_state, weights):
    return pl.pallas_call(
        partial(patch_kernel, grid_size),
        out_shape=jax.ShapeDtypeStruct((16 * GROUP, 128), BF),
        in_specs=[SM] + [VM] * 7,
        out_specs=pl.BlockSpec(memory_space=pltpu.HBM),
        scratch_shapes=[
            pltpu.VMEM((24, 256), F32),
            pltpu.VMEM((14, 24, 256), F32),
            pltpu.VMEM((KC, 256), BF),
            pltpu.VMEM((KC, 256), BF),
            pltpu.VMEM((2, XR, 256), BF),
            pltpu.VMEM((2, XR, 128), F32),
            pltpu.VMEM((2, 16, 256), F32),
            pltpu.VMEM((2, 2, 16, 256), F32),
            pltpu.VMEM((3 * 128, 4 * CHAN), BF),
            pltpu.VMEM((12 * CHAN, 2 * CHAN), BF),
            pltpu.VMEM((8 * CHAN, 256), BF),
            pltpu.VMEM((2 * GROUP, 128), BF),
            pltpu.VMEM((32, NT + 2, NS, 128), BF),
            pltpu.VMEM((32, NT + 2, NS, 128), BF),
            pltpu.VMEM((64, 2, 128, CHAN), BF),
            pltpu.VMEM((65, 2, NT + 2, NS, CHAN), BF),
            pltpu.VMEM((33, 4, NT + 2, NS, CHAN), BF),
            pltpu.VMEM((1, CHAN), F32),
            pltpu.VMEM((2, 8, CHAN), F32),
            pltpu.SemaphoreType.DMA((23,)),
            pltpu.SemaphoreType.DMA((14,)),
            pltpu.SemaphoreType.DMA((10,)),
            pltpu.SemaphoreType.DMA((4, 17)),
            pltpu.SemaphoreType.DMA((4,)),
            pltpu.SemaphoreType.DMA,
        ],
        compiler_params=pltpu.CompilerParams(
            vmem_limit_bytes=56 * 2**20, collective_id=0, has_side_effects=True
        ),
        name="patch_net",
    )(anchors, coarse_state, *weights)


class Placer:
    def __init__(self, anchors, count, blend, gathered, first, acc, cov, buf, sem):
        self.anchors, self.count, self.blend = anchors, count, blend
        self.gathered, self.first, self.acc, self.cov = gathered, first, acc, cov
        self.buf, self.sem = buf, sem
        self.top = lax.axis_index("region") * TH
        self.left = lax.axis_index("patch") * TW
        self.size = (PS - first) * VARS

    def where(self, s):
        return self.anchors[0, s] - self.top, self.anchors[1, s] - self.left

    def meets(self, s):
        dy, dx = self.where(s)
        met = (s < self.count[0]) & (dx > -PS) & (dx < TW)
        return met & (dy > 0) if self.first else met

    def fetch(self, s):
        at = pl.multiple_of(s * GROUP + self.first * VARS, 96)
        return pltpu.make_async_copy(
            self.gathered.at[pl.ds(at, self.size)], self.buf.at[s], self.sem.at[s]
        )

    def run(self):
        def start(s, _):
            @pl.when(self.meets(s))
            def _():
                self.fetch(s).start()

            return 0

        lax.fori_loop(0, 16, start, 0)
        acc, cov = self.acc, self.cov
        acc[...] = jnp.zeros_like(acc)
        cov[...] = jnp.zeros_like(cov)
        lane = lax.broadcasted_iota(jnp.int32, (128, TW), 0)
        x_at = lax.broadcasted_iota(jnp.int32, (128, TW), 1)
        shift = x_at - (lane % NS) * NT - lane // NS
        cov_y = lax.broadcasted_iota(jnp.int32, cov.shape, 0) + self.first
        cov_x = lax.broadcasted_iota(jnp.int32, cov.shape, 1)
        step = min(self.size, 768)

        def add(s, _):
            @pl.when(self.meets(s))
            def _():
                dy, dx = self.where(s)
                weight = self.blend[s].astype(F32)
                onehot = jnp.where(shift == dx, weight, 0.0).astype(BF)
                par = dy % 2
                base = ((dy - par) // 2) * 24
                inside = (cov_y >= dy) & (cov_y < dy + PS) & (cov_x >= dx) & (cov_x < dx + PS)
                cov[...] += jnp.where(inside, weight, 0.0)
                self.fetch(s).wait()
                for n in range(self.size // step):
                    y = dot(self.buf[s, n * step : n * step + step], onehot)
                    at = pl.multiple_of(base + n * step, 8)
                    for h in range(2):
                        acc[par, h, pl.ds(at, step)] += y[:, h * 128 : h * 128 + 128]

            return 0

        lax.fori_loop(0, 16, add, 0)

    def rows(self, v, h, start, n):
        even = self.acc[0, h, pl.ds(start * VARS + v, n, VARS)]
        odd = self.acc[1, h, pl.ds((start - 1) * VARS + v, n, VARS)]
        return even + odd


def place_own_kernel(anchors, count, blend, gathered, num, acc, cov, buf, sem):
    placer = Placer(anchors, count, blend, gathered, 0, acc, cov, buf, sem)
    placer.run()
    half = TH // 2
    inverse = 1.0 / jnp.maximum(cov[half:], 1.0)
    for v in range(VARS):
        for h in range(2):
            cols = slice(h * 128, h * 128 + 128)
            num[v, half:, cols] = placer.rows(v, h, half, half) * inverse[:, cols]
            num[v, 8:half, cols] = placer.rows(v, h, 8, half - 8)
            num[v, :8, cols] = acc[0, h, pl.ds(v, 8, VARS)]
            num[v, 1:8, cols] += acc[1, h, pl.ds(v, 7, VARS)]


def finish_kernel(anchors, count, blend, num, low, cover_low, out, inverse):
    @pl.when(pl.program_id(0) == 0)
    def _():
        top = lax.axis_index("region") * TH
        left = lax.axis_index("patch") * TW
        y = lax.broadcasted_iota(jnp.int32, inverse.shape, 0) + top
        x = lax.broadcasted_iota(jnp.int32, inverse.shape, 1) + left
        inverse[...] = cover_low[0].astype(F32)

        def add(s, _):
            dy, dx = y - anchors[0, s], x - anchors[1, s]
            weight = jnp.where(s < count[0], blend[s], 0).astype(F32)
            inverse[...] += jnp.where((dy >= 0) & (dy < PS) & (dx >= 0) & (dx < PS), weight, 0.0)
            return 0

        lax.fori_loop(0, 16, add, 0)
        inverse[...] = 1.0 / jnp.maximum(inverse[...], 1.0)

    out[...] = (num[...] + low[...].astype(F32)) * inverse[...]


def run_finish(places, count, blend, num, low):
    half, n = TH // 2, VARS // FINISH
    own = pl.BlockSpec((n, half, TW), lambda i: (i, 0, 0))
    return pl.pallas_call(
        finish_kernel,
        grid=(FINISH,),
        out_shape=jax.ShapeDtypeStruct(num.shape, F32),
        in_specs=[SM, SM, SM, own, own, pl.BlockSpec((1, half, TW), lambda i: (VARS, 0, 0))],
        out_specs=own,
        scratch_shapes=[pltpu.VMEM((half, TW), F32)],
        input_output_aliases={3: 0},
        name="finish",
    )(places, count, blend, num, low, low)


def place_over_kernel(anchors, count, blend, gathered, over, acc, cov, buf, sem):
    half = PS // 2
    placer = Placer(anchors, count, blend, gathered, half, acc, cov, buf, sem)
    placer.run()
    over[VARS] = cov[half:].astype(BF)
    for v in range(VARS):
        for h in range(2):
            over[v, :, h * 128 : h * 128 + 128] = placer.rows(v, h, half, half).astype(BF)


def place_call(kernel, first, cov_rows, outs, args, name):
    lines = (PS - first + TH // 2) * VARS
    size = (PS - first) * VARS
    return pl.pallas_call(
        kernel,
        out_shape=outs,
        in_specs=[SM, SM, SM, pl.BlockSpec(memory_space=pltpu.HBM)],
        out_specs=jax.tree.map(lambda _: VM, outs),
        scratch_shapes=[
            pltpu.VMEM((2, 2, lines, 128), F32),
            pltpu.VMEM((cov_rows, TW), F32),
            pltpu.VMEM((16, size, 128), BF),
            pltpu.SemaphoreType.DMA((16,)),
        ],
        compiler_params=pltpu.CompilerParams(vmem_limit_bytes=60 * 2**20),
        cost_estimate=pl.CostEstimate(flops=2 * 8 * size * 128 * 256, bytes_accessed=16 * size * 256, transcendentals=0),
        name=name,
    )(*args)


def run_place(anchors, count, blend, gathered):
    args = (anchors, count, blend, gathered)
    over_shape = jax.ShapeDtypeStruct((VARS + 1, TH // 2, TW), BF)
    own_shape = jax.ShapeDtypeStruct((VARS, TH, TW), F32)
    over = place_call(place_over_kernel, PS // 2, TH, over_shape, args, "place_over")
    n = lax.axis_size("region")
    low = lax.ppermute(over, "region", [(i, i + 1) for i in range(n - 1)])
    num = place_call(place_own_kernel, 0, TH, own_shape, args, "place_own")
    return num, low


def per_device(coarse_state, anchors, region_count, blend, w_in, b_in, gamma, beta, w_mid, w_out):
    n_region = lax.axis_size("region")
    n_patch = lax.axis_size("patch")
    limit_y = coarse_state.shape[1] * n_region * n_patch
    limit_x = coarse_state.shape[2]
    grid_size = (TH * n_region, TW * n_patch, limit_y, limit_x)
    weights = (
        w_in,
        b_in.reshape(1, CHAN),
        gamma.reshape(1, CHAN),
        beta.reshape(1, CHAN),
        w_mid,
        w_out.transpose(0, 1, 3, 2),
    )
    places = anchors.T
    gathered = run_patches(grid_size, places, coarse_state, weights)
    num, low = run_place(places, region_count, blend, gathered)
    return run_finish(places, region_count, blend, num, low)


def solution(mesh):
    return jax.shard_map(
        per_device,
        mesh=mesh,
        in_specs=(
            P(None, ("region", "patch"), None),
            P("region", None),
            P("region"),
            P("region"),
            P(),
            P(),
            P(),
            P(),
            P(),
            P(),
        ),
        out_specs=P(None, "region", "patch"),
        check_vma=False,
    )
```

```python
import math
from functools import partial

import jax
import jax.numpy as jnp
from jax import lax
from jax.experimental import pallas as pl
from jax.experimental.pallas import tpu as pltpu
from jax.sharding import PartitionSpec as P

VARS = 12
CHAN = 128
PS = 128
F = 8
TH = 128
TW = 256
BF = jnp.bfloat16
F32 = jnp.float32
NT, NS = 8, 16
XR = (NT + 2) * NS
KC = 512
GROUP = PS * VARS
UI, UF, UN = 8, 8, 16
FINISH = 2
LAG, LAG2 = 4, 6
LATER = {
    "tables": (("pair_on", 0, 4),),
    "interp": (("far_on", 6, 8), ("pair_on", 4, 8)),
    "first": (("second", 0, 4),),
    "norm": (("second", 4, 6),),
}
START, COUNT = 2, 2
DRAIN = (("far_on", 6, 8), ("second", 0, 2), ("pair_on", 0, 4), ("second", 2, 4), ("pair_on", 4, 8), ("second", 4, 8))
MESH = pl.DeviceIdType.MESH


def dot(a, b):
    return jnp.dot(a, b, preferred_element_type=F32)


def dot_nt(a, b):
    return lax.dot_general(a, b, (((1,), (1,)), ((), ())), preferred_element_type=F32)


def split(x):
    hi = x.astype(BF)
    return hi, (x - hi.astype(F32)).astype(BF)


def row_halo(x):
    rows = x.shape[0]
    s = lax.broadcasted_iota(jnp.int32, (rows, NS, CHAN), 1)
    before = jnp.where(s == 0, 0.0, pltpu.roll(x[:, NT - 1], 1, 1))
    after = jnp.where(s == NS - 1, 0.0, pltpu.roll(x[:, 0], NS - 1, 1))
    return before, after


def column_tables(anchor_x, breadth, limit):
    row = lax.broadcasted_iota(jnp.int32, (XR, 256), 0)
    d = lax.broadcasted_iota(jnp.int32, (XR, 256), 1)
    j = (row % NS) * NT + row // NS - 1
    good = (j >= 0) & (j < PS)
    x = (anchor_x + j).astype(F32)
    at = jnp.clip((x + 0.5) * (1.0 / F) - 0.5, 0.0, limit - 1.0)
    hat = jnp.maximum(0.0, 1.0 - jnp.abs(at - d.astype(F32)))
    hat = jnp.where(good, hat, 0.0).astype(BF)
    lane = d[:, :128]
    angle = x[:, :128] * (2.0 * math.pi / breadth)
    pos = jnp.where(lane == 13, jnp.sin(angle), jnp.where(lane == 14, jnp.cos(angle), 0.0))
    pos = jnp.where(lane == 12, 1.0, pos)
    pos = jnp.where(good[:, :128], pos, 0.0)
    return hat, pos


def row_tables(anchor_y, c0, height, limit, loc_ref, pos_ref):
    g = lax.broadcasted_iota(jnp.int32, (16, 256), 0)
    lane = lax.broadcasted_iota(jnp.int32, (16, 256), 1)
    k, ch = (lane % 128) // 16, lane % 16
    i = 8 * g + 4 * (lane // 128) - 1 + k
    good = (i >= 0) & (i < PS) & (k < 6)
    y = (anchor_y + i).astype(F32)
    loc = jnp.clip((y + 0.5) * (1.0 / F) - 0.5, 0.0, limit - 1.0) - c0.astype(F32)
    loc_ref[...] = jnp.where(good, loc - 14.0, -1000.0)
    angle = y * (2.0 * math.pi / height)
    pos = jnp.where(ch == 12, jnp.sin(angle), jnp.where(ch == 13, jnp.cos(angle), 0.0))
    pos_ref[0] = jnp.where(good, pos, 0.0)
    pos_ref[1] = jnp.where(good, 1.0, 0.0)


def interp_stage(hx, xpos, chi, clo, loc_ref, pos_ref, xh, xl):
    t1 = dot_nt(hx, chi[...]) + dot_nt(hx, clo[...])
    t1 = jnp.concatenate([t1[:, :128] + xpos, t1[:, 128:]], axis=1)
    hi, lo = split(t1)
    lhs = jnp.concatenate([hi, lo], axis=0)
    v_at = lax.broadcasted_iota(jnp.int32, (16, 256), 0)
    ch_at = lax.broadcasted_iota(jnp.int32, (16, 256), 1) % 16
    diag = jnp.where((v_at == ch_at) & (v_at < VARS), 1.0, 0.0).astype(BF)
    pick_y = jnp.where(v_at == 12, 1.0, 0.0)
    pick_x = jnp.where((v_at == 13) & (ch_at == 14) | (v_at == 14) & (ch_at == 15), 1.0, 0.0)
    one = jnp.ones((16, 256), BF)
    none = jnp.zeros((16, 256), BF)

    def step(g, _):
        loc = jnp.broadcast_to(loc_ref[pl.ds(g, 1)], (16, 256)).astype(BF)
        extra = pick_y * pos_ref[0, pl.ds(g, 1)] + pick_x * pos_ref[1, pl.ds(g, 1)]
        blocks = []
        for c in range(28):
            hat = jnp.maximum(none, one - jnp.abs(loc - BF(c - 14))) * diag
            if c == 0:
                hat = hat + extra.astype(BF)
            blocks.append(hat)
        blocks.append(jnp.zeros((64, 256), BF))
        res = dot(lhs, jnp.concatenate(blocks, axis=0))
        x = res[:XR] + res[XR:]
        for h in range(2):
            xa, xb = split(x[:, h * 128 : h * 128 + 128])
            xh[2 * g + h] = xa.reshape(NT + 2, NS, 128)
            xl[2 * g + h] = xb.reshape(NT + 2, NS, 128)
        return 0

    lax.fori_loop(0, 16, step, 0, unroll=UI)


def first_stage(win, b_in, xh, fa, shift, sums):
    bias = b_in[...]
    sums[...] = jnp.zeros_like(sums)

    def rows(at, n):
        lhs = jnp.concatenate(
            [xh[pl.ds(at, n), dx : dx + 8].reshape(n * 128, 128) for dx in range(3)], axis=1
        )
        return dot(lhs, win[...])

    sample = jnp.mean(rows(16, 1)[:, :128] + bias, axis=0, keepdims=True)
    shift[...] = sample

    def step(it, _):
        acc = rows(4 * it, 4)
        base = shift[...]
        one = jnp.zeros((8, CHAN), F32)
        two = jnp.zeros((8, CHAN), F32)
        for r in range(4):
            x = (acc[:, r * 128 : r * 128 + 128] + bias).astype(BF)
            for b in range(4):
                fa[8 * it + 2 * b + r // 2, r % 2] = x[b * 128 : b * 128 + 128]
            d = (x.astype(F32) - base).reshape(64, 8, CHAN)
            one = one + jnp.sum(d, axis=0)
            two = two + jnp.sum(d * d, axis=0)
        sums[0] += one
        sums[1] += two
        return 0

    lax.fori_loop(0, 8, step, 0, unroll=UF)


def group_mean(x):
    lane = lax.broadcasted_iota(jnp.int32, x.shape, 1)
    total = x
    for k in (1, 2):
        low = (lane // k) % 2 == 0
        total = total + jnp.where(low, pltpu.roll(total, CHAN - k, 1), pltpu.roll(total, k, 1))
    return total * 0.25


def scale_shift(sums, shift, gamma, beta):
    n = float(PS * PS)
    one = jnp.broadcast_to(jnp.sum(sums[0], axis=0, keepdims=True), (8, CHAN)) / n
    two = jnp.broadcast_to(jnp.sum(sums[1], axis=0, keepdims=True), (8, CHAN)) / n
    own_var = jnp.maximum(two - one * one, 0.0)
    mean = one + shift[...]
    g_mean = group_mean(mean)
    off = mean - g_mean
    g_var = group_mean(own_var + off * off)
    scale = gamma[...] / jnp.sqrt(g_var + 1e-05)
    return scale[0:1], (beta[...] - g_mean * scale)[0:1]


def norm_stage(scale, offset, fa, nb):
    half_scale = 0.5 * scale
    half_offset = 0.5 * offset

    def step(p, _):
        x = fa[p].astype(F32).reshape(2, NT, NS, CHAN)
        h = x * half_scale + half_offset
        y = h + h * jnp.tanh(h)
        before, after = row_halo(y)
        for r in range(2):
            at, k = (p, 1) if r == 0 else (p + 1, 0)
            nb[at, k, 1 : NT + 1] = y[r].astype(BF)
            nb[at, k, 0] = before[r].astype(BF)
            nb[at, k, NT + 1] = after[r].astype(BF)
        return 0

    lax.fori_loop(0, 64, step, 0, unroll=UN)


def mid_step(it, wmid, nb, fa, sb):
    p0 = 8 * it
    lhs = []
    for k in range(4):
        for dx in range(3):
            lhs.append(nb[pl.ds(p0 + k // 2, 8), k % 2, dx : dx + 8].reshape(1024, CHAN))
    acc = dot(jnp.concatenate(lhs, axis=1), wmid[...])
    for r in range(2):
        x = acc[:, r * 128 : r * 128 + 128] + fa[pl.ds(p0, 8), r].astype(F32).reshape(1024, CHAN)
        x = x.reshape(8, NT, NS, CHAN)
        before, after = row_halo(x)
        for b in range(8):
            at = 2 * b + r + 1
            q, k = 4 * it + at // 4, at % 4
            sb[q, k, 1 : NT + 1] = x[b].astype(BF)
            sb[q, k, 0] = before[b].astype(BF)
            sb[q, k, NT + 1] = after[b].astype(BF)


def out_step(it, wout, sb, xh, xl):
    g0 = 4 * it
    lhs = [sb[pl.ds(g0 + k // 4, 4), k % 4].reshape(4 * XR, CHAN) for k in range(6)]
    lhs.append(xh[pl.ds(g0, 4)].reshape(4 * XR, CHAN))
    lhs.append(xl[pl.ds(g0, 4)].reshape(4 * XR, CHAN))
    acc = dot(jnp.concatenate(lhs, axis=1), wout[...])
    y0 = acc[:, :128].reshape(4, NT + 2, NS, 128)
    y1 = acc[:, 128:].reshape(4, NT + 2, NS, 128)
    centre = pltpu.roll(y0[:, 1 : NT + 1].reshape(512, 128), 64, 1).reshape(4, NT, NS, 128)
    res = y0[:, 0:NT] + centre + y1[:, 2 : NT + 2]
    res = res.reshape(4, 128, 128)
    lane = lax.broadcasted_iota(jnp.int32, (128, 128), 1)
    parts = []
    for h in range(2):
        both = jnp.where(lane < 48, res[2 * h], pltpu.roll(res[2 * h + 1], 48, 1))
        parts.append(jnp.transpose(both)[:96])
    return jnp.concatenate(parts, axis=0).astype(BF)


class CoarseRows:
    def __init__(self, shard, rows, send_sem, recv_sem):
        self.shard, self.rows = shard, rows
        self.send_sem, self.recv_sem = send_sem, recv_sem
        self.r, self.p = lax.axis_index("region"), lax.axis_index("patch")
        self.n_r, self.n_p = lax.axis_size("region"), lax.axis_size("patch")
        self.has_up, self.has_down = self.r > 0, self.r < self.n_r - 1
        self.feeds_down = (self.p == self.n_p - 1) & self.has_down
        self.feeds_up = (self.p < 5) & self.has_up

    def prepare(self, coarse_state):
        r, n_r, rows = self.r, self.n_r, self.rows
        @pl.when(r == 0)
        def _():
            rows[0] = jnp.zeros((24, 256), F32)

        @pl.when(r == n_r - 1)
        def _():
            rows[9:14] = jnp.zeros((5, 24, 256), F32)

        self.shard[...] = jnp.concatenate([coarse_state[:, c, :] for c in range(2)], axis=0)
        rows[1 + self.p] = self.shard[...]

    def spread(self, hi, lo):
        pad = jnp.zeros((16 - VARS, 256), F32)
        for n in range(14):
            x = self.rows[n]
            x = jnp.concatenate([x[:VARS], pad, x[VARS:], pad], axis=0)
            hi[n * 32 : n * 32 + 32], lo[n * 32 : n * 32 + 32] = split(x)
        hi[KC - 64 :] = jnp.zeros((64, 256), BF)
        lo[KC - 64 :] = jnp.zeros((64, 256), BF)

    def greet(self):
        r, p, n_p = self.r, self.p, self.n_p
        barrier = pltpu.get_barrier_semaphore()

        def hello(to):
            pl.semaphore_signal(barrier, inc=1, device_id=to, device_id_type=MESH)

        for d in range(1, n_p):
            hello((r, (p + d) % n_p))

        @pl.when(self.has_up)
        def _():
            hello((r - 1, n_p - 1))

        @pl.when(self.has_down)
        def _():
            for k in range(5):
                hello((r + 1, k))

        count = n_p - 1 + jnp.where(self.feeds_down, n_p, 0) + jnp.where(self.feeds_up, n_p, 0)
        pl.semaphore_wait(barrier, count)

    def copy(self, row, k, to):
        return pltpu.make_async_remote_copy(
            src_ref=self.shard,
            dst_ref=self.rows.at[row],
            send_sem=self.send_sem.at[k],
            recv_sem=self.recv_sem.at[row],
            device_id=to,
            device_id_type=MESH,
        )

    def each(self, act):
        r, p, n_p = self.r, self.p, self.n_p

        @pl.when(self.feeds_down)
        def _():
            for k in range(n_p):
                act(self.copy(0, 7 + k, (r + 1, k)))

        @pl.when(self.feeds_up)
        def _():
            for k in range(n_p):
                act(self.copy(9 + p, 15 + k, (r - 1, k)))

        for d in range(1, n_p):
            act(self.copy(1 + p, d - 1, (r, (p + d) % n_p)))

    def start(self):
        self.each(lambda c: c.start())

    def finish(self):
        r, p, n_p = self.r, self.p, self.n_p
        for d in range(1, n_p):
            q = (p + d) % n_p
            self.copy(1 + q, 0, (r, q)).wait_recv()

        @pl.when(self.has_up)
        def _():
            self.copy(0, 0, (r - 1, n_p - 1)).wait_recv()

        @pl.when(self.has_down)
        def _():
            for k in range(5):
                self.copy(9 + k, 0, (r + 1, k)).wait_recv()

    def sent(self):
        self.each(lambda c: c.wait_send())


CHUNK = 16 * VARS


class Sharer:
    def __init__(self, out, g, send_sem, recv_sem, tail_sem, own_sem):
        self.out, self.g = out, g
        self.send_sem, self.recv_sem = send_sem, recv_sem
        self.tail_sem, self.own_sem = tail_sem, own_sem
        p = lax.axis_index("patch")
        z, y = p // 2, p % 2
        self.me = p
        self.fore = ((z + 1) % 4) * 2 + y
        self.back = ((z + 3) % 4) * 2 + y
        self.pair = z * 2 + 1 - y
        self.far = ((z + 2) % 4) * 2 + y

    def at(self, owner, q):
        start = pl.multiple_of((owner * 16 + q) * CHUNK, CHUNK)
        return self.g.at[pl.ds(start, CHUNK)]

    def remote(self, src, dst, stream, sem, to):
        return pltpu.make_async_remote_copy(
            src_ref=src,
            dst_ref=dst,
            send_sem=self.send_sem.at[stream],
            recv_sem=sem,
            device_id={"patch": to},
            device_id_type=MESH,
        )

    def arrived(self, owner, q, stream):
        there = self.at(owner, q)
        self.remote(there, there, stream, self.recv_sem.at[stream, q], self.fore).wait_recv()

    def own(self, slot, n):
        q = slot * 8 + n
        src = self.out.at[pl.ds(pl.multiple_of(q * CHUNK, CHUNK), CHUNK)]
        dst = self.at(self.me, q)
        even = n % 2 == 0
        fore, back = jnp.where(even, q, 16), jnp.where(even, 16, q)
        self.remote(src, dst, 2, self.recv_sem.at[2, q], self.pair).start()
        self.remote(src, dst, 0, self.recv_sem.at[0, fore], self.fore).start()
        self.remote(src, dst, 1, self.recv_sem.at[1, back], self.back).start()

    def keep(self, slot):
        src = self.out.at[pl.ds(pl.multiple_of(slot * GROUP, GROUP), GROUP)]
        dst = self.g.at[pl.ds(pl.multiple_of((self.me * 2 + slot) * GROUP, GROUP), GROUP)]
        pltpu.make_async_copy(src, dst, self.own_sem).start()

    def far_on(self, slot, n):
        q = slot * 8 + n
        odd = n % 2
        source = jnp.where(odd == 1, self.fore, self.back)
        to = jnp.where(odd == 1, self.back, self.fore)
        self.arrived(source, q, odd)
        there = self.at(source, q)
        self.remote(there, there, 5 + odd, self.recv_sem.at[3, q], to).start()

        @pl.when((n == 2) | (n == 5))
        def _():
            self.remote(there, there, 9, self.tail_sem.at[3], self.pair).start()

    def pair_on(self, slot, n):
        q = slot * 8 + n
        self.arrived(self.pair, q, 2)
        mine = self.at(self.pair, q)

        @pl.when(n != 2)
        def _():
            self.remote(mine, mine, 3, self.tail_sem.at[0], self.fore).start()

        @pl.when(n != 5)
        def _():
            self.remote(mine, mine, 4, self.tail_sem.at[1], self.back).start()

    def second(self, slot, n):
        q = slot * 8 + n
        self.arrived(self.far, q, 3)
        there = self.at(self.far, q)
        self.remote(there, there, 7, self.tail_sem.at[2], self.pair).start()

    def finish(self):
        def chunks(n):
            return self.g.at[pl.ds(0, n * CHUNK)]

        def both(stream, sem, n):
            return self.remote(chunks(n), chunks(n), stream, sem, self.fore)

        both(3, self.tail_sem.at[0], 14).wait()
        both(4, self.tail_sem.at[1], 14).wait()
        both(7, self.tail_sem.at[2], 16).wait()
        both(9, self.tail_sem.at[3], 4).wait()
        both(0, self.recv_sem.at[0, 16], 8).wait_recv()
        both(1, self.recv_sem.at[1, 16], 8).wait_recv()
        for k in range(3):
            both(k, self.tail_sem.at[0], 16).wait_send()
        both(5, self.tail_sem.at[0], 8).wait_send()
        both(6, self.tail_sem.at[0], 8).wait_send()
        pltpu.make_async_copy(chunks(16), chunks(16), self.own_sem).wait()


def pack_weights(w_in, w_mid, w_out, win, wmid, wout):
    zero = jnp.zeros((CHAN, CHAN), BF)
    for dx in range(3):
        for r in range(4):
            cols = slice(r * CHAN, r * CHAN + CHAN)
            parts = [w_in[k - r, dx] if 0 <= k - r < 3 else zero[:16] for k in range(8)]
            win[dx * 128 : dx * 128 + 128, cols] = jnp.concatenate(parts, axis=0)
        for r in range(2):
            cols = slice(r * CHAN, r * CHAN + CHAN)
            for k in range(4):
                at = (k * 3 + dx) * CHAN
                wmid[at : at + CHAN, cols] = w_mid[k - r, dx] if 0 <= k - r < 3 else zero
    for k in range(6):
        halves = []
        for h in range(2):
            parts = []
            for dx in (2 * h, 2 * h + 1):
                for r in range(4):
                    used = dx < 3 and 0 <= k - r < 3
                    parts.append(w_out[k - r, dx].astype(F32) if used else jnp.zeros((VARS, CHAN), F32))
                parts.append(jnp.zeros((16, CHAN), F32))
            halves.append(jnp.transpose(jnp.concatenate(parts, axis=0)))
        wout[k * CHAN : k * CHAN + CHAN] = jnp.concatenate(halves, axis=1).astype(BF)
    row = lax.broadcasted_iota(jnp.int32, (CHAN, 256), 0)
    col = lax.broadcasted_iota(jnp.int32, (CHAN, 256), 1) - 64
    r, v = row // 16 - 1, row % 16
    keep = (r >= 0) & (r < 4) & (v < VARS) & (col == r * VARS + v)
    ident = jnp.where(keep, 1.0, 0.0).astype(BF)
    wout[6 * CHAN : 7 * CHAN] = ident
    wout[7 * CHAN :] = ident


def patch_kernel(
    grid_size, anchors, coarse_state, w_in, b_in, gamma, beta, w_mid, w_out, g,
    shard, rows, chi, clo, hx, xpos, loc, pos, win, wmid, wout, out, xh, xl, fa, nb, sb, shift, sums,
    csend_sem, crecv_sem, send_sem, recv_sem, tail_sem, own_sem,
):
    height, breadth, limit_y, limit_x = grid_size
    coarse = CoarseRows(shard, rows, csend_sem, crecv_sem)
    share = Sharer(out, g, send_sem, recv_sem, tail_sem, own_sem)
    coarse.prepare(coarse_state)
    coarse.greet()
    coarse.start()
    pack_weights(w_in, w_mid, w_out, win, wmid, wout)
    zero = jnp.zeros((NT + 2, NS, CHAN), BF)
    nb[0, 0] = zero
    nb[64, 1] = zero
    sb[0, 0] = zero
    sb[32, 1] = zero
    c0 = coarse.r * 16 - 2

    def tables(slot, _):
        here = share.me * 2 + slot
        row_tables(anchors[0, here], c0, height, limit_y, loc.at[slot], pos.at[slot])
        hx[slot], xpos[slot] = column_tables(anchors[1, here], breadth, limit_x)
        return 0

    lax.fori_loop(0, 2, tables, 0)
    coarse.finish()
    coarse.spread(chi, clo)

    def hand_on(act, slot, low, high):
        def one(n, _):
            getattr(share, act)(slot, n)
            return 0

        if low < high:
            lax.fori_loop(low, high, one, 0)

    def one_slot(slot, _):
        def later(name):
            if name in LATER:

                @pl.when(slot == 1)
                def _():
                    for act, low, high in LATER[name]:
                        hand_on(act, 0, low, high)

        later("tables")
        interp_stage(hx[slot], xpos[slot], chi, clo, loc.at[slot], pos.at[slot], xh, xl)
        later("interp")
        first_stage(win, b_in, xh, fa, shift, sums)
        later("first")
        scale, offset = scale_shift(sums, shift, gamma, beta)
        norm_stage(scale, offset, fa, nb)
        later("norm")

        def out_chunk(it):
            at = pl.multiple_of((slot * 8 + it) * CHUNK, CHUNK)
            out[pl.ds(at, CHUNK)] = out_step(it, wout, sb, xh, xl)

        mid_step(0, wmid, nb, fa, sb)
        mid_step(1, wmid, nb, fa, sb)

        def step(it, _):
            out_chunk(it - 2)
            mid_step(it, wmid, nb, fa, sb)
            share.own(slot, it - 2)

            @pl.when(it >= 2 + LAG)
            def _():
                share.far_on(slot, it - 2 - LAG)

            @pl.when((slot == 1) & (it >= START) & (it < START + COUNT))
            def _():
                share.second(0, it - START + 8 - COUNT)

            @pl.when((slot == 1) & (it >= 2 + LAG2))
            def _():
                share.second(1, it - 2 - LAG2)

            return 0

        lax.fori_loop(2, 8, step, 0)
        out_chunk(6)
        out_chunk(7)
        share.own(slot, 6)
        share.own(slot, 7)
        hand_on("far_on", slot, 6 - LAG, 6)
        return 0

    lax.fori_loop(0, 2, one_slot, 0)
    share.keep(0)
    share.keep(1)
    for act, low, high in DRAIN:
        hand_on(act, 1, low, high)
    share.finish()
    coarse.sent()


VM = pl.BlockSpec(memory_space=pltpu.VMEM)
SM = pl.BlockSpec(memory_space=pltpu.SMEM)


def run_patches(grid_size, anchors, coarse_state, weights):
    return pl.pallas_call(
        partial(patch_kernel, grid_size),
        out_shape=jax.ShapeDtypeStruct((16 * GROUP, 128), BF),
        in_specs=[SM] + [VM] * 7,
        out_specs=pl.BlockSpec(memory_space=pltpu.HBM),
        scratch_shapes=[
            pltpu.VMEM((24, 256), F32),
            pltpu.VMEM((14, 24, 256), F32),
            pltpu.VMEM((KC, 256), BF),
            pltpu.VMEM((KC, 256), BF),
            pltpu.VMEM((2, XR, 256), BF),
            pltpu.VMEM((2, XR, 128), F32),
            pltpu.VMEM((2, 16, 256), F32),
            pltpu.VMEM((2, 2, 16, 256), F32),
            pltpu.VMEM((3 * 128, 4 * CHAN), BF),
            pltpu.VMEM((12 * CHAN, 2 * CHAN), BF),
            pltpu.VMEM((8 * CHAN, 256), BF),
            pltpu.VMEM((2 * GROUP, 128), BF),
            pltpu.VMEM((32, NT + 2, NS, 128), BF),
            pltpu.VMEM((32, NT + 2, NS, 128), BF),
            pltpu.VMEM((64, 2, 128, CHAN), BF),
            pltpu.VMEM((65, 2, NT + 2, NS, CHAN), BF),
            pltpu.VMEM((33, 4, NT + 2, NS, CHAN), BF),
            pltpu.VMEM((1, CHAN), F32),
            pltpu.VMEM((2, 8, CHAN), F32),
            pltpu.SemaphoreType.DMA((23,)),
            pltpu.SemaphoreType.DMA((14,)),
            pltpu.SemaphoreType.DMA((10,)),
            pltpu.SemaphoreType.DMA((4, 17)),
            pltpu.SemaphoreType.DMA((4,)),
            pltpu.SemaphoreType.DMA,
        ],
        compiler_params=pltpu.CompilerParams(
            vmem_limit_bytes=56 * 2**20, collective_id=0, has_side_effects=True
        ),
        name="patch_net",
    )(anchors, coarse_state, *weights)


class Placer:
    def __init__(self, anchors, count, blend, gathered, first, acc, cov, buf, sem):
        self.anchors, self.count, self.blend = anchors, count, blend
        self.gathered, self.first, self.acc, self.cov = gathered, first, acc, cov
        self.buf, self.sem = buf, sem
        self.top = lax.axis_index("region") * TH
        self.left = lax.axis_index("patch") * TW
        self.size = (PS - first) * VARS

    def where(self, s):
        return self.anchors[0, s] - self.top, self.anchors[1, s] - self.left

    def meets(self, s):
        dy, dx = self.where(s)
        met = (s < self.count[0]) & (dx > -PS) & (dx < TW)
        return met & (dy > 0) if self.first else met

    def fetch(self, s):
        at = pl.multiple_of(s * GROUP + self.first * VARS, 96)
        return pltpu.make_async_copy(
            self.gathered.at[pl.ds(at, self.size)], self.buf.at[s], self.sem.at[s]
        )

    def run(self):
        def start(s, _):
            @pl.when(self.meets(s))
            def _():
                self.fetch(s).start()

            return 0

        lax.fori_loop(0, 16, start, 0)
        acc, cov = self.acc, self.cov
        acc[...] = jnp.zeros_like(acc)
        cov[...] = jnp.zeros_like(cov)
        lane = lax.broadcasted_iota(jnp.int32, (128, TW), 0)
        x_at = lax.broadcasted_iota(jnp.int32, (128, TW), 1)
        shift = x_at - (lane % NS) * NT - lane // NS
        cov_y = lax.broadcasted_iota(jnp.int32, cov.shape, 0) + (TH if self.first else TH // 2)
        cov_x = lax.broadcasted_iota(jnp.int32, cov.shape, 1)
        step = self.size // 2

        def add(s, _):
            @pl.when(self.meets(s))
            def _():
                dy, dx = self.where(s)
                weight = self.blend[s].astype(F32)
                onehot = jnp.where(shift == dx, weight, 0.0).astype(BF)
                par = dy % 2
                base = ((dy - par) // 2) * 24
                inside = (cov_y >= dy) & (cov_y < dy + PS) & (cov_x >= dx) & (cov_x < dx + PS)
                cov[...] += jnp.where(inside, weight, 0.0)
                self.fetch(s).wait()

                def part(n):
                    y = dot(self.buf[s, n * step : n * step + step], onehot)
                    at = pl.multiple_of(base + n * step, 8)
                    for h in range(2):
                        acc[par, h, pl.ds(at, step)] += y[:, h * 128 : h * 128 + 128]

                if self.first:
                    pl.when(dy > PS // 4)(lambda: part(0))
                else:
                    part(0)
                part(1)

            return 0

        lax.fori_loop(0, 16, add, 0)

    def rows(self, v, h, start, n):
        even = self.acc[0, h, pl.ds(start * VARS + v, n, VARS)]
        odd = self.acc[1, h, pl.ds((start - 1) * VARS + v, n, VARS)]
        return even + odd


def place_own_kernel(anchors, count, blend, gathered, num, acc, cov, buf, sem):
    placer = Placer(anchors, count, blend, gathered, 0, acc, cov, buf, sem)
    placer.run()
    half = TH // 2
    inverse = 1.0 / jnp.maximum(cov[...], 1.0)
    for v in range(VARS):
        for h in range(2):
            cols = slice(h * 128, h * 128 + 128)
            num[v, half:, cols] = placer.rows(v, h, half, half) * inverse[:, cols]
            num[v, 8:half, cols] = placer.rows(v, h, 8, half - 8)
            num[v, :8, cols] = acc[0, h, pl.ds(v, 8, VARS)]
            num[v, 1:8, cols] += acc[1, h, pl.ds(v, 7, VARS)]


def finish_kernel(anchors, count, blend, num, low, cover_low, out, inverse):
    @pl.when(pl.program_id(0) == 0)
    def _():
        top = lax.axis_index("region") * TH
        left = lax.axis_index("patch") * TW
        y = lax.broadcasted_iota(jnp.int32, inverse.shape, 0) + top
        x = lax.broadcasted_iota(jnp.int32, inverse.shape, 1) + left
        inverse[...] = cover_low[0].astype(F32)

        def add(s, _):
            dy, dx = y - anchors[0, s], x - anchors[1, s]
            weight = jnp.where(s < count[0], blend[s], 0).astype(F32)
            inverse[...] += jnp.where((dy >= 0) & (dy < PS) & (dx >= 0) & (dx < PS), weight, 0.0)
            return 0

        lax.fori_loop(0, 16, add, 0)
        inverse[...] = 1.0 / jnp.maximum(inverse[...], 1.0)

    out[...] = (num[...] + low[...].astype(F32)) * inverse[...]


def run_finish(places, count, blend, num, low):
    half, n = TH // 2, VARS // FINISH
    own = pl.BlockSpec((n, half, TW), lambda i: (i, 0, 0))
    return pl.pallas_call(
        finish_kernel,
        grid=(FINISH,),
        out_shape=jax.ShapeDtypeStruct(num.shape, F32),
        in_specs=[SM, SM, SM, own, own, pl.BlockSpec((1, half, TW), lambda i: (VARS, 0, 0))],
        out_specs=own,
        scratch_shapes=[pltpu.VMEM((half, TW), F32)],
        input_output_aliases={3: 0},
        name="finish",
    )(places, count, blend, num, low, low)


def place_over_kernel(anchors, count, blend, gathered, over, acc, cov, buf, sem):
    half = PS // 2
    placer = Placer(anchors, count, blend, gathered, half, acc, cov, buf, sem)
    placer.run()
    over[VARS] = cov[...].astype(BF)
    for v in range(VARS):
        for h in range(2):
            over[v, :, h * 128 : h * 128 + 128] = placer.rows(v, h, half, half).astype(BF)


def place_call(kernel, first, cov_rows, outs, args, name):
    lines = (PS - first + TH // 2) * VARS
    size = (PS - first) * VARS
    return pl.pallas_call(
        kernel,
        out_shape=outs,
        in_specs=[SM, SM, SM, pl.BlockSpec(memory_space=pltpu.HBM)],
        out_specs=jax.tree.map(lambda _: VM, outs),
        scratch_shapes=[
            pltpu.VMEM((2, 2, lines, 128), F32),
            pltpu.VMEM((cov_rows, TW), F32),
            pltpu.VMEM((16, size, 128), BF),
            pltpu.SemaphoreType.DMA((16,)),
        ],
        compiler_params=pltpu.CompilerParams(vmem_limit_bytes=60 * 2**20),
        cost_estimate=pl.CostEstimate(flops=2 * 8 * size * 128 * 256, bytes_accessed=16 * size * 256, transcendentals=0),
        name=name,
    )(*args)


def run_place(anchors, count, blend, gathered):
    args = (anchors, count, blend, gathered)
    over_shape = jax.ShapeDtypeStruct((VARS + 1, TH // 2, TW), BF)
    own_shape = jax.ShapeDtypeStruct((VARS, TH, TW), F32)
    over = place_call(place_over_kernel, PS // 2, TH // 2, over_shape, args, "place_over")
    n = lax.axis_size("region")
    low = lax.ppermute(over, "region", [(i, i + 1) for i in range(n - 1)])
    num = place_call(place_own_kernel, 0, TH // 2, own_shape, args, "place_own")
    return num, low


def per_device(coarse_state, anchors, region_count, blend, w_in, b_in, gamma, beta, w_mid, w_out):
    n_region = lax.axis_size("region")
    n_patch = lax.axis_size("patch")
    limit_y = coarse_state.shape[1] * n_region * n_patch
    limit_x = coarse_state.shape[2]
    grid_size = (TH * n_region, TW * n_patch, limit_y, limit_x)
    weights = (
        w_in,
        b_in.reshape(1, CHAN),
        gamma.reshape(1, CHAN),
        beta.reshape(1, CHAN),
        w_mid,
        w_out.transpose(0, 1, 3, 2),
    )
    places = anchors.T
    gathered = run_patches(grid_size, places, coarse_state, weights)
    num, low = run_place(places, region_count, blend, gathered)
    return run_finish(places, region_count, blend, num, low)


def solution(mesh):
    return jax.shard_map(
        per_device,
        mesh=mesh,
        in_specs=(
            P(None, ("region", "patch"), None),
            P("region", None),
            P("region"),
            P("region"),
            P(),
            P(),
            P(),
            P(),
            P(),
            P(),
        ),
        out_specs=P(None, "region", "patch"),
        check_vma=False,
    )
```
